32 devices in a mesh: seq: 4 (over y, x), exp: 8 (over z, core).
Axes of the slice: x: 2, y: 2, z: 4, core: 2. Of those that a mesh axis runs over, the one named last changes fastest.
Arguments:
- hidden_in: bfloat16 [2048, 2048], P(('seq', 'exp')), may hold values from -6 to 6
- query_proj: bfloat16 [2048, 2048], P('seq', 'exp'), may hold values from -40 to 40
- key_proj: bfloat16 [2048, 2048], P('seq', 'exp'), may hold values from -40 to 40
- value_proj: bfloat16 [2048, 4096], P('seq', 'exp'), may hold values from -6 to 6
- gate_proj: bfloat16 [2048, 4096], P('seq', 'exp'), may hold values from -6 to 6
- log_decay: float32 [32, 2048], P('exp', 'seq'), may hold values from -0.6 to 0
- write_rate: float32 [32, 2048], P('exp', 'seq'), may hold values from 0 to 1
- head_gain: float32 [128], replicated, may hold values from 0.1 to 1.9
- out_weight: bfloat16 [4096, 2048], P('exp'), may hold values from -0.09375 to 0.09375
- post_gain: float32 [2048], replicated, may hold values from 0.1 to 1.9
- expert_ids: int32 [2048, 4], P(('seq', 'exp')), may hold values from 0 to 7, all different within a row; in each aligned block of 64 rows (0 to 63, 64 to 127, ...) at most 64 rows name the same one
- route_weight: bfloat16 [2048, 4], P(('seq', 'exp')), may hold values from 0.19921875 to 1
- gate_weight: bfloat16 [8, 2048, 512], P('exp'), may hold values from -0.125 to 0.125
- up_weight: bfloat16 [8, 2048, 512], P('exp'), may hold values from -0.125 to 0.125
- down_weight: bfloat16 [8, 512, 2048], P('exp'), may hold values from -0.25 to 0.25
Outputs:
- layer_out: bfloat16 [2048, 2048], P(('seq', 'exp'))
The draws below stay inside these ranges and needn't reach their ends.
Inputs may be any that keep to these rules, and one draw needn't show every extreme that they name: `expert_ids`: each token names 4 different experts. Within the tokens of one device (aligned blocks of 64 tokens in sequence order) no expert is named by more than 64 tokens, and in every draw some block names some expert exactly 64 times.
All inputs are finite; a program needn't handle non-finite values.
Results may differ from the reference program's by a relative error of at most 0.02.
Values may be sent and summed in bfloat16 or wider, within the bound.
No kernel may reach another device: no remote copies, remote signals or barrier semaphores. Data moves between devices by JAX's collectives and lax.ppermute only.
A program may use at most 128 MiB of HBM per device.

```python
import math
import jax
import jax.numpy as jnp
import numpy as np
from jax import lax

D = 2048
FF = 512
DK = 128
DV = 128
KHEADS = 16
VALUE_HEAD_COUNT = 32
TOPK = 4
TOKEN_COUNT = 2048
TOK_DEV = 64
EXPERTS = 8
CAP = 64
N_SEQ = 4
N_EXP = 8


def rough_matrix(key, row_total, col_total, offset):
    piece_list = jax.random.split(key, 5)
    row_scale = jnp.exp(jax.random.uniform(piece_list[0], (row_total, 1), jnp.float32, 0.0, math.log(10.0)))
    col_scale = jnp.exp(jax.random.uniform(piece_list[1], (1, col_total), jnp.float32, -0.35, 0.35))
    shared_part = jax.random.uniform(piece_list[4], (1, col_total), jnp.float32, -1.0, 1.0) * offset
    base_draw = jax.random.normal(piece_list[2], (row_total, col_total), jnp.float32) + shared_part
    return jnp.clip(base_draw * row_scale * col_scale, -40.0, 40.0)


def head_plan(key):
    piece_list = jax.random.split(jax.random.fold_in(key, 11), 7)
    fast_share = 0.25
    middle_share = 0.35
    class_draw = jax.random.uniform(piece_list[0], (VALUE_HEAD_COUNT, 1), jnp.float32)
    fast_flag = class_draw < fast_share
    middle_flag = jnp.logical_and(jnp.logical_not(fast_flag), class_draw < fast_share + middle_share)
    fast_rate = -1.0 / jax.random.uniform(piece_list[1], (VALUE_HEAD_COUNT, 1), jnp.float32, 30.0, 50.0)
    middle_rate = -1.0 / jax.random.uniform(piece_list[6], (VALUE_HEAD_COUNT, 1), jnp.float32, 100.0, 240.0)
    slow_rate = -jax.random.uniform(piece_list[2], (VALUE_HEAD_COUNT, 1), jnp.float32, 0.03, 0.2) * math.log(10.0) / TOKEN_COUNT
    head_speed = jnp.where(fast_flag, fast_rate, jnp.where(middle_flag, middle_rate, slow_rate))
    random_perturbation = jax.random.uniform(piece_list[3], (VALUE_HEAD_COUNT, TOKEN_COUNT), jnp.float32, 0.5, 1.5)
    spike_location = jax.random.randint(piece_list[4], (VALUE_HEAD_COUNT, 2), 0, TOKEN_COUNT)
    spike_retention = jax.random.uniform(piece_list[5], (VALUE_HEAD_COUNT, 2), jnp.float32, 0.6, 0.8)
    token_position = jnp.arange(TOKEN_COUNT, dtype=jnp.int32)[None, :, None]
    spike_logarithm = jnp.sum(jnp.where(token_position == spike_location[:, None, :], jnp.log(spike_retention)[:, None, :], 0.0), axis=2)
    return (fast_flag, middle_flag, head_speed * random_perturbation + spike_logarithm)


def draw_query_proj(key, part):
    return rough_matrix(jax.random.fold_in(key, 3), TOKEN_COUNT, KHEADS * DK, 0.0).astype(jnp.bfloat16)


def draw_key_proj(key, part):
    return rough_matrix(jax.random.fold_in(key, 5), TOKEN_COUNT, KHEADS * DK, 2.5).astype(jnp.bfloat16)


def draw_log_decay(key, part):
    fast_flag, middle_flag, decay_log = head_plan(key)
    return decay_log


def draw_write_rate(key, part):
    fast_flag, middle_flag, decay_log = head_plan(key)
    piece_list = jax.random.split(jax.random.fold_in(key, 23), 3)
    fast_rate = jax.random.uniform(piece_list[0], (VALUE_HEAD_COUNT, TOKEN_COUNT), jnp.float32, 0.3, 0.9)
    middle_rate = jax.random.uniform(piece_list[2], (VALUE_HEAD_COUNT, TOKEN_COUNT), jnp.float32, 0.1, 0.3)
    slow_rate = DK / TOKEN_COUNT * jax.random.uniform(piece_list[1], (VALUE_HEAD_COUNT, TOKEN_COUNT), jnp.float32, 1.5, 3.0)
    return jnp.where(fast_flag, fast_rate, jnp.where(middle_flag, middle_rate, slow_rate))


def steps_of(stream_key, shape, cuts, low, largest):
    factor_of, own = 1.0, jax.random.fold_in(stream_key, 6)
    for axis_at, shards_of in cuts:
        draws = jnp.exp(jax.random.uniform(jax.random.fold_in(own, axis_at), (shards_of,), jnp.float32, low / len(cuts), largest / len(cuts)))
        factor_of = factor_of * jnp.repeat(draws, shape[axis_at] // shards_of).reshape([-1 if axis == axis_at else 1 for axis in range(len(shape))])
    return factor_of


def assign_block(own_key, own, number, rows, count, top, limit, lean):
    ranking = jax.random.permutation(own_key, count)
    heavy_load, ordinary = shares(count, rows * top, limit, lean, True), shares(count, rows * top, limit, lean, False)
    places = jnp.arange(count)

    def named(tallies, turn):
        used = int((tallies > 0).sum())
        fixed = max(1, used // 4)
        passed = fixed + (places - fixed + turn * (used - fixed)) % max(1, count - fixed)
        return jnp.zeros((count,), jnp.int32).at[ranking[jnp.where(places < fixed, places, passed)]].set(jnp.asarray(tallies, jnp.int32))

    tallies = jnp.where(number % 4 == 0, named(heavy_load, number // 4), named(ordinary, number - number // 4 - 1))
    mixed = jax.random.permutation(jax.random.fold_in(own, 3), count)
    giver, taker = mixed[0:count // 2 * 2:2], mixed[1:count // 2 * 2:2]
    margin = jnp.minimum(tallies[giver] - 1, limit - tallies[taker]) // 2
    margin = jnp.where((giver == ranking[0]) | (taker == ranking[0]) | (tallies[taker] == 0), 0, jnp.maximum(margin, 0))
    passed = jax.random.randint(jax.random.fold_in(own, 4), (count // 2,), 0, 1 << 20) % (margin + 1)
    tallies = tallies.at[giver].add(-passed).at[taker].add(passed)
    labels = jnp.searchsorted(jnp.cumsum(tallies), jnp.arange(rows * top), side="right").astype(jnp.int32)
    listing = labels.reshape(top, rows).T
    listing = listing[jax.random.permutation(jax.random.fold_in(own, 1), rows)]
    turn = jax.random.randint(jax.random.fold_in(own, 2), (rows, 1), 0, top)
    return jnp.take_along_axis(listing, (jnp.arange(top)[None, :] + turn) % top, axis=1)


def shares(number_of, total, bound, slope, full):
    weights = [(1 << 20) // math.isqrt(grade ** slope) + 1 for grade in range(1, number_of + 1)]
    largest = bound if full else min(bound, max(-(-total // number_of), total * weights[0] // sum(weights)))
    least = 1 if total - largest >= number_of - 1 else 0
    given, surplus = [largest] + [least] * (number_of - 1), total - largest - least * (number_of - 1)
    while surplus > 0:
        movable = [i for i in range(1, number_of) if given[i] < largest] or [i for i in range(1, number_of) if given[i] < bound]
        whole, remaining = sum([weights[i] for i in movable]), surplus
        for i in movable:
            addition = min(bound - given[i], max(1, remaining * weights[i] // whole), surplus)
            given[i] = given[i] + addition
            surplus = surplus - addition
    return np.array(given)


def centred(stream_key, dims, width, most, shards=(), held_as=jnp.bfloat16):
    entries = jax.random.normal(stream_key, dims, jnp.float32) * width
    if len(shards) > 0:
        entries = steps_of(stream_key, dims, shards, -0.22, 0.18) * entries
    return jnp.clip(entries, min=-most, max=most).astype(held_as)


def setup_inputs(seed: int = 0) -> dict:
    seeds = jax.random.split(jax.random.key(seed), 16)
    hidden_in = centred(seeds[0], (TOKEN_COUNT, D), 1.0, 6.0, ((0, 32),))
    query_proj = draw_query_proj(jax.random.fold_in(seeds[15], 71), 0)
    key_proj = draw_key_proj(jax.random.fold_in(seeds[15], 71), 0)
    value_proj = centred(seeds[3], (TOKEN_COUNT, VALUE_HEAD_COUNT * DV), 1.0, 6.0, ((0, 4), (1, 8)))
    gate_proj = centred(seeds[4], (TOKEN_COUNT, VALUE_HEAD_COUNT * DV), 1.0, 6.0, ((0, 4), (1, 8)))
    log_decay = draw_log_decay(jax.random.fold_in(seeds[15], 71), 0)
    write_rate = draw_write_rate(jax.random.fold_in(seeds[15], 71), 0)
    head_gain = jnp.clip(1.0 + 0.18 * jax.random.normal(seeds[7], (DV,), jnp.float32), 0.1, 1.9)
    out_weight = centred(seeds[8], (VALUE_HEAD_COUNT * DV, D), (VALUE_HEAD_COUNT * DV) ** -0.5, 0.09375, ((0, 8),))
    post_gain = jnp.clip(1.0 + 0.18 * jax.random.normal(seeds[9], (D,), jnp.float32), 0.1, 1.9)
    expert_ids_keys = jax.random.split(jax.random.fold_in(seeds[10], 1), TOKEN_COUNT // TOK_DEV)
    expert_ids_turns = jax.random.permutation(jax.random.fold_in(seeds[10], 3), TOKEN_COUNT // TOK_DEV)
    expert_ids = jax.vmap(lambda own, number: assign_block(jax.random.fold_in(seeds[10], 2), own, number, TOK_DEV, EXPERTS, TOPK, CAP, 2))(expert_ids_keys, expert_ids_turns).reshape((TOKEN_COUNT, TOPK))
    route_weight = jnp.clip(0.19921875 + 0.80078125 * jax.random.uniform(seeds[11], (TOKEN_COUNT, TOPK), jnp.float32) ** steps_of(seeds[11], (TOKEN_COUNT, TOPK), ((0, 32),), -0.2, 0.2), 0.19921875, 1.0).astype(jnp.bfloat16)
    gate_weight = centred(seeds[12], (EXPERTS, D, FF), D ** -0.5, 0.125, ((0, 8),))
    up_weight = centred(seeds[13], (EXPERTS, D, FF), D ** -0.5, 0.125, ((0, 8),))
    down_weight = centred(seeds[14], (EXPERTS, FF, D), FF ** -0.5, 0.25, ((0, 8),))
    return dict(hidden_in=hidden_in, query_proj=query_proj, key_proj=key_proj, value_proj=value_proj, gate_proj=gate_proj, log_decay=log_decay, write_rate=write_rate, head_gain=head_gain, out_weight=out_weight, post_gain=post_gain, expert_ids=expert_ids, route_weight=route_weight, gate_weight=gate_weight, up_weight=up_weight, down_weight=down_weight)


EPS = 1e-06
HIGHEST_ACCURACY = lax.Precision.HIGHEST

def unit_rows(matrix):
    return matrix * lax.rsqrt(lax.optimization_barrier(jnp.sum(matrix * matrix, axis=-1, keepdims=True)) + EPS)

def reference(hidden_in, query_proj, key_proj, value_proj, gate_proj, log_decay, write_rate, head_gain, out_weight, post_gain, expert_ids, route_weight, gate_weight, up_weight, down_weight):
    group_size = VALUE_HEAD_COUNT // KHEADS

    def advance(carried, inputs):
        query_row, key_row, value_row, gate_row, decay_row, rate_row = inputs
        query_unit = unit_rows(query_row.astype(jnp.float32).reshape(KHEADS, DK)) * DK ** (-0.5)
        key_unit = unit_rows(key_row.astype(jnp.float32).reshape(KHEADS, DK))
        query_unit = jnp.repeat(query_unit, group_size, axis=0)
        key_unit = jnp.repeat(key_unit, group_size, axis=0)
        value_heads = value_row.astype(jnp.float32).reshape(VALUE_HEAD_COUNT, DV)
        retain = jnp.exp(decay_row)
        recalled = jnp.einsum('hvk,hk->hv', carried, key_unit, precision=HIGHEST_ACCURACY)
        carried = retain[:, None, None] * (carried - rate_row[:, None, None] * recalled[:, :, None] * key_unit[:, None, :]) + rate_row[:, None, None] * value_heads[:, :, None] * key_unit[:, None, :]
        readout = jnp.einsum('hvk,hk->hv', carried, query_unit, precision=HIGHEST_ACCURACY)
        gate_heads = gate_row.astype(jnp.float32).reshape(VALUE_HEAD_COUNT, DV)
        scaled = readout * lax.rsqrt(lax.optimization_barrier(jnp.mean(readout * readout, axis=-1, keepdims=True)) + EPS)
        mixed_row = scaled * head_gain * jax.nn.silu(gate_heads)
        return (carried, mixed_row.reshape(VALUE_HEAD_COUNT * DV).astype(jnp.bfloat16))
    initial = jnp.zeros((VALUE_HEAD_COUNT, DV, DK), jnp.float32)
    unused_state, mixed = lax.scan(advance, initial, (query_proj, key_proj, value_proj, gate_proj, log_decay.T, write_rate.T))
    residual = hidden_in.astype(jnp.float32) + jnp.dot(mixed, out_weight, preferred_element_type=jnp.float32)
    normed = (residual * lax.rsqrt(lax.optimization_barrier(jnp.mean(residual * residual, axis=-1, keepdims=True)) + EPS) * post_gain).astype(jnp.bfloat16)
    row_total = TOKEN_COUNT * TOPK
    room_rows = N_SEQ * N_EXP * CAP
    flat_ids = expert_ids.reshape(-1)
    flat_weight = route_weight.reshape(-1).astype(jnp.float32)
    owner_tok = jnp.arange(row_total, dtype=jnp.int32) // TOPK

    def add_expert(running_sum, expert):
        is_hit = flat_ids == expert
        token_position = jnp.cumsum(is_hit.astype(jnp.int32)) - 1
        target = jnp.where(is_hit, token_position, room_rows).astype(jnp.int32)
        sources = jnp.zeros((room_rows,), jnp.int32).at[target].set(owner_tok, mode='drop')
        slot_weight = jnp.zeros((room_rows,), jnp.float32).at[target].set(flat_weight, mode='drop')
        picked = normed[sources]
        gate_act = jnp.dot(picked, gate_weight[expert], preferred_element_type=jnp.float32)
        up_act = jnp.dot(picked, up_weight[expert], preferred_element_type=jnp.float32)
        hidden = (jax.nn.silu(gate_act) * up_act).astype(jnp.bfloat16)
        produced = jnp.dot(hidden, down_weight[expert], preferred_element_type=jnp.float32).astype(jnp.bfloat16)
        running_sum = running_sum.at[sources].add(produced.astype(jnp.float32) * slot_weight[:, None])
        return (running_sum, None)
    combined, unused_out = lax.scan(add_expert, residual, jnp.arange(EXPERTS, dtype=jnp.int32))
    return combined.astype(jnp.bfloat16)
```

```python
import functools

import jax
import jax.numpy as jnp
from jax import lax
from jax.experimental import pallas as pl
from jax.experimental.pallas import tpu as pltpu
from jax.sharding import PartitionSpec as P

DK = 128
DV = 128
EPS = 1e-06
BLOCK = 128
LANES = 128
F32 = jnp.float32
BF16 = jnp.bfloat16
EXACT = lax.Precision.HIGHEST
VMEM_BYTES = 48 * 1024 * 1024


def whole(memory_space=pltpu.VMEM):
    return pl.BlockSpec(memory_space=memory_space)


def mm(a, b):
    return jnp.dot(a.astype(BF16), b.astype(BF16), preferred_element_type=F32)


def mm_nt(a, b, precision=None):
    return lax.dot_general(
        a, b, (((1,), (1,)), ((), ())), preferred_element_type=F32, precision=precision
    )


def split(a):
    high = a.astype(BF16)
    return high, (a - high.astype(F32)).astype(BF16)


def mm_left2(a, b):
    high, low = split(a)
    return jnp.dot(
        jnp.concatenate([high, low], axis=1),
        jnp.concatenate([b, b], axis=0),
        preferred_element_type=F32,
    )


def mm_right2(a, b):
    high, low = split(b)
    return jnp.dot(
        jnp.concatenate([a, a], axis=1),
        jnp.concatenate([high, low], axis=0),
        preferred_element_type=F32,
    )


def mm_both2(a, b):
    a_high, a_low = split(a)
    b_high, b_low = split(b)
    return jnp.dot(
        jnp.concatenate([a_high, a_low, a_high], axis=1),
        jnp.concatenate([b_high, b_high, b_low], axis=0),
        preferred_element_type=F32,
    )


def grids():
    row = lax.broadcasted_iota(jnp.int32, (BLOCK, BLOCK), 0)
    col = lax.broadcasted_iota(jnp.int32, (BLOCK, BLOCK), 1)
    return row, col


def stacked(ref, blocks):
    return jnp.concatenate([ref[:, c * BLOCK : (c + 1) * BLOCK] for c in range(blocks)], axis=0)


def decays(decay_ref, blocks, row, col):
    by_row = stacked(decay_ref, blocks)
    upto = jnp.where(row >= col, 1.0, 0.0).astype(F32)
    cum_rows = mm_nt(by_row, upto, EXACT)
    cum_cols = mm_nt(upto, by_row, EXACT)
    return cum_rows, cum_cols


def state_kernel(key_ref, value_ref, decay_ref, rate_ref, wu_ref, prefix_ref, total_ref):
    heads = decay_ref.shape[0]
    key_heads = key_ref.shape[1] // DK
    group = heads // key_heads
    blocks = key_ref.shape[0] // BLOCK
    row, col = grids()
    gap_bits = jnp.bitwise_xor(row, col)
    strict = row > col
    diagonal = row == col
    eye = jnp.where(diagonal, 1.0, 0.0).astype(F32)
    cum_rows, cum_cols = decays(decay_ref, blocks, row, col)
    rate_rows = stacked(rate_ref, blocks)
    rate_cols = mm_nt(eye, rate_rows, EXACT)
    carried = [None] * heads
    for c in range(blocks):
        tokens = slice(c * BLOCK, (c + 1) * BLOCK)
        keys, keys_t, grams, unit_rows, unit_cols = [], [], [], [], []
        for g in range(key_heads):
            key = key_ref[tokens, g * DK : (g + 1) * DK]
            gram = mm_nt(key, key)
            on_diagonal = jnp.where(diagonal, gram, 0.0)
            unit_rows.append(lax.rsqrt(jnp.sum(on_diagonal, axis=0, keepdims=True) + EPS))
            unit_cols.append(lax.rsqrt(jnp.sum(on_diagonal, axis=1, keepdims=True) + EPS))
            keys.append(key)
            keys_t.append(key.astype(F32).T.astype(BF16))
            grams.append(gram * unit_rows[g] * unit_cols[g])
        lower, solve = [], []
        for h in range(heads):
            at = c * heads + h
            cum_row, cum_col = cum_rows[at : at + 1, :], cum_cols[:, at : at + 1]
            fade = jnp.exp(jnp.where(strict, cum_col - cum_row, 0.0))
            part = jnp.where(strict, grams[h // group] * fade * rate_cols[:, at : at + 1], 0.0)
            lower.append(part)
            solve.append(eye - jnp.where(gap_bits == 1, part, 0.0))
        size = 2
        while size < BLOCK:
            shift = size.bit_length() - 1
            inside = lax.shift_right_logical(gap_bits, shift) == 1
            right = [
                mm(jnp.where(inside, lower[h], 0.0), solve[h]) for h in range(heads)
            ]
            solve = [solve[h] - mm(solve[h], right[h]) for h in range(heads)]
            size *= 2
        first = [s.astype(BF16) for s in solve]
        rest = [eye - first[h].astype(F32) - mm_left2(lower[h], first[h]) for h in range(heads)]
        solve = [first[h].astype(F32) + mm(first[h], rest[h]) for h in range(heads)]
        for h in range(heads):
            at = c * heads + h
            g = h // group
            cum_row, cum_col = cum_rows[at : at + 1, :], cum_cols[:, at : at + 1]
            rate_row = rate_rows[at : at + 1, :]
            end = cum_row[:, BLOCK - 1 :]
            w = mm_left2(solve[h] * (rate_row * jnp.exp(cum_row) * unit_rows[g]), keys[g])
            u = mm_left2(solve[h] * rate_row, value_ref[tokens, h * DV : (h + 1) * DV])
            wu = jnp.concatenate([w, u], axis=1)
            wu_ref[h, c] = wu.astype(BF16)
            tail = mm_right2(keys_t[g], wu * (jnp.exp(end - cum_col) * unit_cols[g]))
            kept = jnp.exp(end)
            bias = jnp.concatenate([jnp.zeros((DK, DK), F32), tail[:, DK:]], axis=1)
            if c == 0:
                start = jnp.concatenate([eye, jnp.zeros((DK, DV), F32)], axis=1)
                prefix_ref[h, c] = start.astype(BF16)
                carried[h] = jnp.concatenate([kept * eye - tail[:, :DK], tail[:, DK:]], axis=1)
            else:
                prefix_ref[h, c] = carried[h].astype(BF16)
                carried[h] = kept * carried[h] + bias - mm_both2(tail[:, :DK], carried[h])
    for h in range(heads):
        total_ref[h] = carried[h].astype(BF16)


def readout_kernel(query_ref, key_ref, gate_ref, gain_ref, decay_ref, wu_ref, prefix_ref,
                   lin_ref, own_ref, gated_ref):
    heads = decay_ref.shape[0]
    key_heads = key_ref.shape[1] // DK
    group = heads // key_heads
    blocks = key_ref.shape[0] // BLOCK
    row, col = grids()
    causal = row >= col
    diagonal = row == col
    cum_rows, cum_cols = decays(decay_ref, blocks, row, col)
    for c in range(blocks):
        tokens = slice(c * BLOCK, (c + 1) * BLOCK)
        for g in range(key_heads):
            key = key_ref[tokens, g * DK : (g + 1) * DK]
            query = query_ref[tokens, g * DK : (g + 1) * DK]
            key_f, query_f = key.astype(F32), query.astype(F32)
            gram = jnp.where(diagonal, mm_nt(key, key), 0.0)
            unit_row = lax.rsqrt(jnp.sum(gram, axis=0, keepdims=True) + EPS)
            query_unit = query_f * (
                lax.rsqrt(jnp.sum(query_f * query_f, axis=1, keepdims=True) + EPS) * DK ** (-0.5)
            )
            query_scale = lax.rsqrt(
                jnp.sum(query_f * query_f, axis=1, keepdims=True) + EPS
            ) * DK ** (-0.5)
            plain = mm_nt(query, key) * unit_row * query_scale
            for h in range(g * group, (g + 1) * group):
                at = c * heads + h
                cum_row, cum_col = cum_rows[at : at + 1, :], cum_cols[:, at : at + 1]
                fade = jnp.exp(jnp.where(causal, cum_col - cum_row, 0.0))
                scores = jnp.where(causal, plain * fade, 0.0)
                mixed_wu = mm(scores, wu_ref[h, c])
                reach = query_unit * jnp.exp(cum_col) - mixed_wu[:, :DK]
                lanes = slice(h * DV, (h + 1) * DV)
                if c == 0:
                    lin_ref[tokens, lanes] = reach.astype(BF16)
                    own_ref[tokens, lanes] = mixed_wu[:, DK:]
                else:
                    spread = mm(reach, prefix_ref[h, c])
                    lin_ref[tokens, lanes] = spread[:, :DK].astype(BF16)
                    own_ref[tokens, lanes] = mixed_wu[:, DK:] + spread[:, DK:]
        for h in range(heads):
            lanes = slice(h * DV, (h + 1) * DV)
            gate = gate_ref[tokens, lanes].astype(F32)
            gated_ref[tokens, lanes] = gain_ref[...] * gate / (1.0 + jnp.exp(-gate))


def compose_kernel(own_ref, got_ref, out_ref):
    for h in range(own_ref.shape[0]):
        out = mm(own_ref[h, :, :DK], got_ref[h])
        bias = own_ref[h, :, DK:].astype(F32)
        out_ref[h] = (
            out + jnp.concatenate([jnp.zeros((DK, DK), F32), bias], axis=1)
        ).astype(BF16)


def compose(own, got):
    return pl.pallas_call(
        compose_kernel,
        out_shape=jax.ShapeDtypeStruct(own.shape, BF16),
        in_specs=[whole(), whole()],
        out_specs=whole(),
    )(own, got)


def bias_kernel(own_ref, got_ref, out_ref):
    for h in range(own_ref.shape[0]):
        out = mm(own_ref[h, :, :DK], got_ref[h])
        out_ref[h] = (out + own_ref[h, :, DK:].astype(F32)).astype(BF16)


def compose_bias(own, got):
    return pl.pallas_call(
        bias_kernel,
        out_shape=jax.ShapeDtypeStruct(got.shape, BF16),
        in_specs=[whole(), whole()],
        out_specs=whole(),
    )(own, got)


def mix_kernel(core_ref, state_ref, lin_ref, own_ref, gated_ref, keep_ref, send_ref):
    core = core_ref[0]
    heads = state_ref.shape[0]
    rows = keep_ref.shape[1]
    for z in range(keep_ref.shape[0]):
        for out_ref, side in ((send_ref, 1 - core), (keep_ref, core)):
            tokens = pl.ds(pl.multiple_of((2 * z + side) * rows, rows), rows)
            for h in range(heads):
                lanes = slice(h * DV, (h + 1) * DV)
                readout = own_ref[tokens, lanes] + mm(lin_ref[tokens, lanes], state_ref[h])
                scale = lax.rsqrt(jnp.mean(readout * readout, axis=1, keepdims=True) + EPS)
                out_ref[z, :, lanes] = (readout * scale * gated_ref[tokens, lanes]).astype(BF16)


def norm_kernel(hidden_ref, mine_ref, right_ref, left_ref, gain_ref, ids_ref, weight_ref,
                residual_ref, out_ref):
    residual = (
        hidden_ref[...].astype(F32)
        + mine_ref[...].astype(F32)
        + right_ref[...].astype(F32)
        + left_ref[...].astype(F32)
    )
    residual_ref[...] = residual
    scale = lax.rsqrt(jnp.mean(residual * residual, axis=1, keepdims=True) + EPS)
    width = residual.shape[1]
    out_ref[:, :width] = (residual * scale * gain_ref[...]).astype(BF16)
    lane = lax.broadcasted_iota(jnp.int32, (residual.shape[0], LANES), 1)
    routes = jnp.zeros((residual.shape[0], LANES), F32)
    for k in range(ids_ref.shape[1]):
        routes += jnp.where(
            ids_ref[:, k : k + 1] == lane, weight_ref[:, k : k + 1].astype(F32), 0.0
        )
    out_ref[:, width:] = routes.astype(BF16)


def expert_kernel(places, halves, place_ref, *refs):
    slots = refs[: 2 * places - 1]
    gate_own, up_own, down_own, gate_sib, up_sib, down_sib, out_ref, x_ref, sum_ref = refs[
        2 * places - 1 :
    ]
    step = pl.program_id(0)
    place, core = place_ref[0], place_ref[1]
    rows = slots[0].shape[0]
    width = out_ref.shape[-1]

    @pl.when(step == 0)
    def _():
        for number, slot in enumerate(slots):
            spot = place + number - (places - 1)

            @pl.when(jnp.logical_and(spot >= 0, spot < places))
            def _(slot=slot, spot=spot):
                x_ref[pl.ds(pl.multiple_of(spot * rows, rows), rows), :] = slot[...]

    def add(gate, up, down, expert, fresh):
        x = x_ref[:, :width]
        gate_act = jnp.dot(x, gate[0], preferred_element_type=F32)
        up_act = jnp.dot(x, up[0], preferred_element_type=F32)
        inner = (gate_act / (1.0 + jnp.exp(-gate_act)) * up_act).astype(BF16)
        routes = x_ref[:, width:].astype(F32)
        lane = lax.broadcasted_iota(jnp.int32, routes.shape, 1)
        weight = jnp.sum(jnp.where(lane == expert, routes, 0.0), axis=1, keepdims=True)
        more = jnp.dot(inner, down[0], preferred_element_type=F32) * weight

        @pl.when(fresh)
        def _():
            sum_ref[...] = more

        @pl.when(jnp.logical_not(fresh))
        def _():
            sum_ref[...] += more

    @pl.when(step < halves)
    def _():
        add(gate_own, up_own, down_own, 2 * place + core, step == 0)

    @pl.when(step >= halves)
    def _():
        add(gate_sib, up_sib, down_sib, 2 * place + 1 - core, step < 0)

    @pl.when(step == 2 * halves - 1)
    def _():
        out_ref[...] = sum_ref[...].astype(BF16).reshape(out_ref.shape)


def experts(place, core, slots, own, sib, places):
    rows = slots[0].shape[0]
    width = own[0].shape[1]
    inner = own[0].shape[2]
    tile = 256
    halves = inner // tile

    def specs(at):
        return [
            pl.BlockSpec((1, width, tile), lambda i: (0, 0, at(i))),
            pl.BlockSpec((1, width, tile), lambda i: (0, 0, at(i))),
            pl.BlockSpec((1, tile, width), lambda i: (0, at(i), 0)),
        ]

    return pl.pallas_call(
        functools.partial(expert_kernel, places, halves),
        grid=(2 * halves,),
        out_shape=jax.ShapeDtypeStruct((places, rows, width), BF16),
        in_specs=[whole(pltpu.SMEM)]
        + [whole()] * len(slots)
        + specs(lambda i: jnp.minimum(i, halves - 1))
        + specs(lambda i: jnp.maximum(i - halves, 0)),
        out_specs=whole(),
        scratch_shapes=[
            pltpu.VMEM((places * rows, slots[0].shape[1]), BF16),
            pltpu.VMEM((places * rows, width), F32),
        ],
        compiler_params=pltpu.CompilerParams(vmem_limit_bytes=VMEM_BYTES),
    )(jnp.stack([place, core]).astype(jnp.int32), *slots, *own, *sib)


def rightward(places, count):
    return [(2 * i + c, 2 * i + 2 + c) for i in range(min(count, places - 1)) for c in range(2)]


def leftward(places, count):
    return [
        (2 * i + c, 2 * i - 2 + c)
        for i in range(places - 1, max(places - 1 - count, 0), -1)
        for c in range(2)
    ]


def line_scatter(parts, place, places):
    def part(at):
        return lax.dynamic_index_in_dim(parts, jnp.clip(at, 0, places - 1), 0, False)

    right = left = None
    for t in range(1, places):
        to_right, to_left = part(places - t + place), part(t + place - places)
        if t > 1:
            to_right = (to_right.astype(F32) + right.astype(F32)).astype(BF16)
            to_left = (to_left.astype(F32) + left.astype(F32)).astype(BF16)
        right = lax.ppermute(to_right, "exp", rightward(places, t))
        left = lax.ppermute(to_left, "exp", leftward(places, t))
    return part(place), right, left


def line_gather(own, places):
    slots = {0: own}
    right = left = own
    for t in range(1, places):
        right = lax.ppermute(
            right, "exp", [(a, b) for a, b in rightward(places, places) if a // 2 >= t - 1]
        )
        left = lax.ppermute(
            left, "exp", [(a, b) for a, b in leftward(places, places) if a // 2 <= places - t]
        )
        slots[-t], slots[t] = right, left
    return [slots[t] for t in range(1 - places, places)]


def per_device(
    hidden_in,
    query_proj,
    key_proj,
    value_proj,
    gate_proj,
    log_decay,
    write_rate,
    head_gain,
    out_weight,
    post_gain,
    expert_ids,
    route_weight,
    gate_weight,
    up_weight,
    down_weight,
):
    length = value_proj.shape[0]
    heads = value_proj.shape[1] // DV
    blocks = length // BLOCK
    tok, width = hidden_in.shape
    seqs, exps = lax.axis_size("seq"), lax.axis_size("exp")
    places = exps // 2
    me = lax.axis_index("exp")
    place, core = me // 2, me % 2
    swap = [(i, i ^ 1) for i in range(exps)]

    out_sib = lax.ppermute(out_weight, "exp", swap)
    own = (gate_weight, up_weight, down_weight)
    sib = tuple(lax.ppermute(w, "exp", swap) for w in own)

    wide = jax.ShapeDtypeStruct((heads, blocks, DK, DK + DV), BF16)
    wu, prefixes, total = pl.pallas_call(
        state_kernel,
        out_shape=(wide, wide, jax.ShapeDtypeStruct((heads, DK, DK + DV), BF16)),
        in_specs=[whole()] * 4,
        out_specs=(whole(),) * 3,
        compiler_params=pltpu.CompilerParams(vmem_limit_bytes=VMEM_BYTES),
        cost_estimate=pl.CostEstimate(flops=10**10, bytes_accessed=4 * 10**6, transcendentals=0),
    )(key_proj, value_proj, log_decay, write_rate)

    lin, own_read, gated = pl.pallas_call(
        readout_kernel,
        out_shape=(
            jax.ShapeDtypeStruct((length, heads * DV), BF16),
            jax.ShapeDtypeStruct((length, heads * DV), F32),
            jax.ShapeDtypeStruct((length, heads * DV), F32),
        ),
        in_specs=[whole()] * 7,
        out_specs=(whole(),) * 3,
        compiler_params=pltpu.CompilerParams(vmem_limit_bytes=VMEM_BYTES),
        cost_estimate=pl.CostEstimate(flops=6 * 10**9, bytes_accessed=4 * 10**6, transcendentals=0),
    )(query_proj, key_proj, gate_proj, head_gain.reshape(1, DV), log_decay, wu, prefixes)

    upto, before, step = total, None, 1
    while step < seqs:
        pairs = [(i, i + step) for i in range(seqs - step)]
        last = 2 * step >= seqs
        sent = upto[:, :, DK:] if last and before is not None else upto
        got = lax.ppermute(sent, "seq", pairs)
        if last:
            state = got[:, :, DK:] if before is None else compose_bias(before, got)
        else:
            upto = compose(upto, got)
            before = got if before is None else compose(before, got)
        step *= 2

    half = jax.ShapeDtypeStruct((places, tok, heads * DV), BF16)
    keep, send = pl.pallas_call(
        mix_kernel,
        out_shape=(half, half),
        in_specs=[whole(pltpu.SMEM)] + [whole()] * 4,
        out_specs=(whole(),) * 2,
        compiler_params=pltpu.CompilerParams(vmem_limit_bytes=VMEM_BYTES),
    )(core.reshape(1).astype(jnp.int32), state, lin, own_read, gated)
    got = lax.ppermute(send, "exp", swap)
    parts = (
        jnp.dot(keep.reshape(-1, heads * DV), out_weight, preferred_element_type=F32)
        + jnp.dot(got.reshape(-1, heads * DV), out_sib, preferred_element_type=F32)
    ).astype(BF16).reshape(places, tok, width)

    mine, right, left = line_scatter(parts, place, places)
    residual, normed = pl.pallas_call(
        norm_kernel,
        out_shape=(
            jax.ShapeDtypeStruct((tok, width), F32),
            jax.ShapeDtypeStruct((tok, width + LANES), BF16),
        ),
        in_specs=[whole()] * 7,
        out_specs=(whole(),) * 2,
    )(hidden_in, mine, right, left, post_gain.reshape(1, width), expert_ids, route_weight)
    slots = line_gather(normed, places)
    sums = experts(place, core, slots, own, sib, places)
    mine, right, left = line_scatter(sums, place, places)
    return (
        residual + mine.astype(F32) + right.astype(F32) + left.astype(F32)
    ).astype(BF16)


def solution(mesh):
    in_specs = (
        P(("seq", "exp"), None),
        P("seq", "exp"),
        P("seq", "exp"),
        P("seq", "exp"),
        P("seq", "exp"),
        P("exp", "seq"),
        P("exp", "seq"),
        P(),
        P("exp", None),
        P(),
        P(("seq", "exp"), None),
        P(("seq", "exp"), None),
        P("exp", None, None),
        P("exp", None, None),
        P("exp", None, None),
    )
    out_specs = P(("seq", "exp"), None)
    return jax.shard_map(
        per_device, mesh=mesh, in_specs=in_specs, out_specs=out_specs, check_vma=False
    )
```

```python
import functools

import jax
import jax.numpy as jnp
from jax import lax
from jax.experimental import pallas as pl
from jax.experimental.pallas import tpu as pltpu
from jax.sharding import PartitionSpec as P

DK = 128
DV = 128
EPS = 1e-06
BLOCK = 128
LANES = 128
F32 = jnp.float32
BF16 = jnp.bfloat16
EXACT = lax.Precision.HIGHEST
SMALL_VMEM = 20 * 1024 * 1024
EXPERT_VMEM = 32 * 1024 * 1024


def whole(memory_space=pltpu.VMEM):
    return pl.BlockSpec(memory_space=memory_space)


def blocks_of(*arrays):
    return [pl.BlockSpec(a.shape, lambda i, n=a.ndim: (0,) * n) for a in arrays]


def mm(a, b):
    return jnp.dot(a.astype(BF16), b.astype(BF16), preferred_element_type=F32)


def mm_nt(a, b, precision=None):
    return lax.dot_general(
        a, b, (((1,), (1,)), ((), ())), preferred_element_type=F32, precision=precision
    )


def split(a):
    high = a.astype(BF16)
    return high, (a - high.astype(F32)).astype(BF16)


def mm_left2(a, b):
    high, low = split(a)
    return jnp.dot(
        jnp.concatenate([high, low], axis=1),
        jnp.concatenate([b, b], axis=0),
        preferred_element_type=F32,
    )


def mm_right2(a, b):
    high, low = split(b)
    return jnp.dot(
        jnp.concatenate([a, a], axis=1),
        jnp.concatenate([high, low], axis=0),
        preferred_element_type=F32,
    )


def mm_both2(a, b):
    a_high, a_low = split(a)
    b_high, b_low = split(b)
    return jnp.dot(
        jnp.concatenate([a_high, a_low, a_high], axis=1),
        jnp.concatenate([b_high, b_high, b_low], axis=0),
        preferred_element_type=F32,
    )


def grids():
    row = lax.broadcasted_iota(jnp.int32, (BLOCK, BLOCK), 0)
    col = lax.broadcasted_iota(jnp.int32, (BLOCK, BLOCK), 1)
    return row, col


def stacked(ref, blocks):
    return jnp.concatenate([ref[:, c * BLOCK : (c + 1) * BLOCK] for c in range(blocks)], axis=0)


def decays(decay_ref, blocks, row, col):
    by_row = stacked(decay_ref, blocks)
    upto = jnp.where(row >= col, 1.0, 0.0).astype(F32)
    cum_rows = mm_nt(by_row, upto, EXACT)
    cum_cols = mm_nt(upto, by_row, EXACT)
    return cum_rows, cum_cols


def state_kernel(key_ref, value_ref, decay_ref, rate_ref, wu_ref, prefix_ref, total_ref):
    heads = decay_ref.shape[0]
    key_heads = key_ref.shape[1] // DK
    group = heads // key_heads
    blocks = key_ref.shape[0] // BLOCK
    row, col = grids()
    gap_bits = jnp.bitwise_xor(row, col)
    strict = row > col
    diagonal = row == col
    eye = jnp.where(diagonal, 1.0, 0.0).astype(F32)
    cum_rows, cum_cols = decays(decay_ref, blocks, row, col)
    rate_rows = stacked(rate_ref, blocks)
    rate_cols = mm_nt(eye, rate_rows, EXACT)
    carried = [None] * heads
    for c in range(blocks):
        tokens = slice(c * BLOCK, (c + 1) * BLOCK)
        keys, keys_t, grams, unit_rows, unit_cols = [], [], [], [], []
        for g in range(key_heads):
            key = key_ref[tokens, g * DK : (g + 1) * DK]
            gram = mm_nt(key, key)
            on_diagonal = jnp.where(diagonal, gram, 0.0)
            unit_rows.append(lax.rsqrt(jnp.sum(on_diagonal, axis=0, keepdims=True) + EPS))
            unit_cols.append(lax.rsqrt(jnp.sum(on_diagonal, axis=1, keepdims=True) + EPS))
            keys.append(key)
            keys_t.append(key.astype(F32).T.astype(BF16))
            grams.append(gram * unit_rows[g] * unit_cols[g])
        lower, solve = [], []
        for h in range(heads):
            at = c * heads + h
            cum_row, cum_col = cum_rows[at : at + 1, :], cum_cols[:, at : at + 1]
            fade = jnp.exp(jnp.where(strict, cum_col - cum_row, 0.0))
            part = jnp.where(strict, grams[h // group] * fade * rate_cols[:, at : at + 1], 0.0)
            lower.append(part)
            solve.append(eye - jnp.where(gap_bits == 1, part, 0.0))
        size = 2
        while size < BLOCK:
            shift = size.bit_length() - 1
            inside = lax.shift_right_logical(gap_bits, shift) == 1
            right = [
                mm(jnp.where(inside, lower[h], 0.0), solve[h]) for h in range(heads)
            ]
            solve = [solve[h] - mm(solve[h], right[h]) for h in range(heads)]
            size *= 2
        first = [s.astype(BF16) for s in solve]
        rest = [eye - first[h].astype(F32) - mm_left2(lower[h], first[h]) for h in range(heads)]
        solve = [first[h].astype(F32) + mm(first[h], rest[h]) for h in range(heads)]
        for h in range(heads):
            at = c * heads + h
            g = h // group
            cum_row, cum_col = cum_rows[at : at + 1, :], cum_cols[:, at : at + 1]
            rate_row = rate_rows[at : at + 1, :]
            end = cum_row[:, BLOCK - 1 :]
            w = mm_left2(solve[h] * (rate_row * jnp.exp(cum_row) * unit_rows[g]), keys[g])
            u = mm_left2(solve[h] * rate_row, value_ref[tokens, h * DV : (h + 1) * DV])
            wu = jnp.concatenate([w, u], axis=1)
            wu_ref[h, c] = wu.astype(BF16)
            tail = mm_right2(keys_t[g], wu * (jnp.exp(end - cum_col) * unit_cols[g]))
            kept = jnp.exp(end)
            bias = jnp.concatenate([jnp.zeros((DK, DK), F32), tail[:, DK:]], axis=1)
            if c == 0:
                start = jnp.concatenate([eye, jnp.zeros((DK, DV), F32)], axis=1)
                prefix_ref[h, c] = start.astype(BF16)
                carried[h] = jnp.concatenate([kept * eye - tail[:, :DK], tail[:, DK:]], axis=1)
            else:
                prefix_ref[h, c] = carried[h].astype(BF16)
                carried[h] = kept * carried[h] + bias - mm_both2(tail[:, :DK], carried[h])
    for h in range(heads):
        total_ref[h] = carried[h].astype(BF16)


def readout_kernel(query_ref, key_ref, gate_ref, gain_ref, decay_ref, ids_ref, weight_ref, wu_ref, prefix_ref,
                   lin_ref, own_ref, gated_ref, routes_ref):
    expert = lax.broadcasted_iota(jnp.int32, (LANES, ids_ref.shape[1]), 0)
    routes = jnp.zeros(expert.shape, F32)
    for k in range(ids_ref.shape[0]):
        routes += jnp.where(
            ids_ref[k : k + 1, :] == expert, weight_ref[k : k + 1, :].astype(F32), 0.0
        )
    routes_ref[...] = routes.T.astype(BF16)
    heads = decay_ref.shape[0]
    key_heads = key_ref.shape[1] // DK
    group = heads // key_heads
    blocks = key_ref.shape[0] // BLOCK
    row, col = grids()
    causal = row >= col
    diagonal = row == col
    cum_rows, cum_cols = decays(decay_ref, blocks, row, col)
    for c in range(blocks):
        tokens = slice(c * BLOCK, (c + 1) * BLOCK)
        for g in range(key_heads):
            key = key_ref[tokens, g * DK : (g + 1) * DK]
            query = query_ref[tokens, g * DK : (g + 1) * DK]
            key_f, query_f = key.astype(F32), query.astype(F32)
            gram = jnp.where(diagonal, mm_nt(key, key), 0.0)
            unit_row = lax.rsqrt(jnp.sum(gram, axis=0, keepdims=True) + EPS)
            query_unit = query_f * (
                lax.rsqrt(jnp.sum(query_f * query_f, axis=1, keepdims=True) + EPS) * DK ** (-0.5)
            )
            query_scale = lax.rsqrt(
                jnp.sum(query_f * query_f, axis=1, keepdims=True) + EPS
            ) * DK ** (-0.5)
            plain = mm_nt(query, key) * unit_row * query_scale
            for h in range(g * group, (g + 1) * group):
                at = c * heads + h
                cum_row, cum_col = cum_rows[at : at + 1, :], cum_cols[:, at : at + 1]
                fade = jnp.exp(jnp.where(causal, cum_col - cum_row, 0.0))
                scores = jnp.where(causal, plain * fade, 0.0)
                mixed_wu = mm(scores, wu_ref[h, c])
                reach = query_unit * jnp.exp(cum_col) - mixed_wu[:, :DK]
                lanes = slice(h * DV, (h + 1) * DV)
                if c == 0:
                    lin_ref[tokens, lanes] = reach.astype(BF16)
                    own_ref[tokens, lanes] = mixed_wu[:, DK:]
                else:
                    spread = mm(reach, prefix_ref[h, c])
                    lin_ref[tokens, lanes] = spread[:, :DK].astype(BF16)
                    own_ref[tokens, lanes] = mixed_wu[:, DK:] + spread[:, DK:]
        for h in range(heads):
            lanes = slice(h * DV, (h + 1) * DV)
            gate = gate_ref[tokens, lanes].astype(F32)
            gated_ref[tokens, lanes] = gain_ref[...] * gate / (1.0 + jnp.exp(-gate))


def scan_kernel(last, later_ref, own_ref, got_ref, before_ref, total_ref, prefix_ref):
    later = later_ref[0] == 1
    for h in range(own_ref.shape[0]):
        own, got = own_ref[h], got_ref[h]
        first = jnp.where(later, got, own)
        second = jnp.where(later, own, got)
        bias = second[:, DK:].astype(F32)
        if last:
            total_ref[h] = (mm(second[:, :DK], first[:, DK:]) + bias).astype(BF16)
        else:
            total_ref[h] = (
                mm(second[:, :DK], first)
                + jnp.concatenate([jnp.zeros((DK, DK), F32), bias], axis=1)
            ).astype(BF16)
        before = before_ref[h]
        joined = mm(before[:, :DK], got) + jnp.concatenate(
            [jnp.zeros((DK, DK), F32), before[:, DK:].astype(F32)], axis=1
        )
        prefix_ref[h] = jnp.where(later, joined.astype(BF16), before)


def scan_step(later, own, got, before, last):
    heads = own.shape[0]
    total = jax.ShapeDtypeStruct((heads, DK, DV if last else DK + DV), BF16)
    return pl.pallas_call(
        functools.partial(scan_kernel, last),
        out_shape=(total, jax.ShapeDtypeStruct(own.shape, BF16)),
        in_specs=[whole(pltpu.SMEM)] + [whole()] * 3,
        out_specs=(whole(),) * 2,
        compiler_params=pltpu.CompilerParams(vmem_limit_bytes=SMALL_VMEM),
    )(later, own, got, before)


def mix_kernel(core_ref, prefix_ref, got_ref, lin_ref, own_ref, gated_ref, keep_ref, send_ref):
    core, place, later = core_ref[0], core_ref[1], core_ref[2] == 1
    heads = prefix_ref.shape[0]
    places = keep_ref.shape[0]
    rows = keep_ref.shape[1]
    states = []
    for h in range(heads):
        prefix = prefix_ref[h]
        bias = prefix[:, DK:].astype(F32)
        joined = mm(prefix[:, :DK], got_ref[h]) + bias
        states.append(jnp.where(later, joined, bias).astype(BF16))
    for d in range(places):
        at = jnp.bitwise_xor(place, d)
        for out_ref, side in ((send_ref, 1 - core), (keep_ref, core)):
            tokens = pl.ds(pl.multiple_of((2 * at + side) * rows, rows), rows)
            for h in range(heads):
                lanes = slice(h * DV, (h + 1) * DV)
                readout = own_ref[tokens, lanes] + mm(lin_ref[tokens, lanes], states[h])
                scale = lax.rsqrt(jnp.mean(readout * readout, axis=1, keepdims=True) + EPS)
                out_ref[d, :, lanes] = (readout * scale * gated_ref[tokens, lanes]).astype(BF16)


def project_kernel(keep_ref, got_ref, own_ref, sib_ref, *out_refs):
    rows = keep_ref.shape[1]
    depth = keep_ref.shape[2]
    product = jnp.dot(
        keep_ref[...].reshape(-1, depth), own_ref[...], preferred_element_type=F32
    ) + jnp.dot(got_ref[...].reshape(-1, depth), sib_ref[...], preferred_element_type=F32)
    for d, out_ref in enumerate(out_refs):
        out_ref[...] = product[d * rows : (d + 1) * rows].astype(BF16)


def project(keep, got, own, sib):
    places, rows, depth = keep.shape
    width = own.shape[1]
    tile = 512
    return pl.pallas_call(
        project_kernel,
        grid=(width // tile,),
        out_shape=(jax.ShapeDtypeStruct((rows, width), BF16),) * places,
        in_specs=[pl.BlockSpec((places, rows, depth), lambda i: (0, 0, 0))] * 2
        + [pl.BlockSpec((depth, tile), lambda i: (0, i))] * 2,
        out_specs=(pl.BlockSpec((rows, tile), lambda i: (0, i)),) * places,
        compiler_params=pltpu.CompilerParams(vmem_limit_bytes=SMALL_VMEM),
    )(keep, got, own, sib)


def norm_kernel(hidden_ref, gain_ref, routes_ref, *refs):
    *part_refs, residual_ref, out_ref = refs
    residual = hidden_ref[...].astype(F32)
    for part_ref in part_refs:
        residual += part_ref[...].astype(F32)
    residual_ref[...] = residual
    scale = lax.rsqrt(jnp.mean(residual * residual, axis=1, keepdims=True) + EPS)
    width = residual.shape[1]
    out_ref[:, :width] = (residual * scale * gain_ref[...]).astype(BF16)
    out_ref[:, width:] = routes_ref[...]


def expert_kernel(places, halves, place_ref, *refs):
    slots = refs[:places]
    gate_own, up_own, down_own, gate_sib, up_sib, down_sib = refs[places : places + 6]
    out_refs = refs[places + 6 : -2]
    x_ref, sum_ref = refs[-2:]
    step = pl.program_id(0)
    place, core = place_ref[0], place_ref[1]
    rows, width = out_refs[0].shape

    @pl.when(step == 0)
    def _():
        for d, slot in enumerate(slots):
            x_ref[d * rows : (d + 1) * rows, :] = slot[...]

    def add(gate, up, down, expert, fresh):
        x = x_ref[:, :width]
        gate_act = jnp.dot(x, gate[0], preferred_element_type=F32)
        up_act = jnp.dot(x, up[0], preferred_element_type=F32)
        inner = (gate_act / (1.0 + jnp.exp(-gate_act)) * up_act).astype(BF16)
        routes = x_ref[:, width:].astype(F32)
        lane = lax.broadcasted_iota(jnp.int32, routes.shape, 1)
        weight = jnp.sum(jnp.where(lane == expert, routes, 0.0), axis=1, keepdims=True)
        more = jnp.dot(inner, down[0], preferred_element_type=F32) * weight

        @pl.when(fresh)
        def _():
            sum_ref[...] = more

        @pl.when(jnp.logical_not(fresh))
        def _():
            sum_ref[...] += more

    @pl.when(step < halves)
    def _():
        add(gate_own, up_own, down_own, 2 * place + core, step == 0)

    @pl.when(step >= halves)
    def _():
        add(gate_sib, up_sib, down_sib, 2 * place + 1 - core, step < 0)

    @pl.when(step == 2 * halves - 1)
    def _():
        for d, out_ref in enumerate(out_refs):
            out_ref[...] = sum_ref[d * rows : (d + 1) * rows].astype(BF16)


def experts(place_core, slots, own, sib):
    places = len(slots)
    rows = slots[0].shape[0]
    width = own[0].shape[1]
    inner = own[0].shape[2]
    tile = 256
    halves = inner // tile

    def specs(at):
        return [
            pl.BlockSpec((1, width, tile), lambda i: (0, 0, at(i))),
            pl.BlockSpec((1, width, tile), lambda i: (0, 0, at(i))),
            pl.BlockSpec((1, tile, width), lambda i: (0, at(i), 0)),
        ]

    return pl.pallas_call(
        functools.partial(expert_kernel, places, halves),
        grid=(2 * halves,),
        out_shape=(jax.ShapeDtypeStruct((rows, width), BF16),) * places,
        in_specs=[whole(pltpu.SMEM)]
        + [whole()] * places
        + specs(lambda i: jnp.minimum(i, halves - 1))
        + specs(lambda i: jnp.maximum(i - halves, 0)),
        out_specs=(whole(),) * places,
        scratch_shapes=[
            pltpu.VMEM((places * rows, slots[0].shape[1]), BF16),
            pltpu.VMEM((places * rows, width), F32),
        ],
        compiler_params=pltpu.CompilerParams(vmem_limit_bytes=EXPERT_VMEM),
    )(place_core, *slots, *own, *sib)


def between_places(places, d):
    return [(2 * i + c, 2 * (i ^ d) + c) for i in range(places) for c in range(2)]


def exchange(pieces):
    places = len(pieces)
    return [pieces[0]] + [
        lax.ppermute(pieces[d], "exp", between_places(places, d)) for d in range(1, places)
    ]


def per_device(
    hidden_in,
    query_proj,
    key_proj,
    value_proj,
    gate_proj,
    log_decay,
    write_rate,
    head_gain,
    out_weight,
    post_gain,
    expert_ids,
    route_weight,
    gate_weight,
    up_weight,
    down_weight,
):
    length = value_proj.shape[0]
    heads = value_proj.shape[1] // DV
    blocks = length // BLOCK
    tok, width = hidden_in.shape
    seqs, exps = lax.axis_size("seq"), lax.axis_size("exp")
    places = exps // 2
    me = lax.axis_index("exp")
    place, core = lax.div(me, 2), lax.rem(me, 2)
    here = lax.axis_index("seq")
    swap = [(i, i ^ 1) for i in range(exps)]

    out_sib = lax.ppermute(out_weight, "exp", swap)
    own = (gate_weight, up_weight, down_weight)
    sib = tuple(lax.ppermute(w, "exp", swap) for w in own)

    wide = jax.ShapeDtypeStruct((heads, blocks, DK, DK + DV), BF16)
    wu, prefixes, total = pl.pallas_call(
        state_kernel,
        out_shape=(wide, wide, jax.ShapeDtypeStruct((heads, DK, DK + DV), BF16)),
        grid=(1,),
        in_specs=blocks_of(key_proj, value_proj, log_decay, write_rate),
        out_specs=(whole(),) * 3,
        compiler_params=pltpu.CompilerParams(vmem_limit_bytes=SMALL_VMEM),
        cost_estimate=pl.CostEstimate(flops=10**10, bytes_accessed=4 * 10**6, transcendentals=0),
    )(key_proj, value_proj, log_decay, write_rate)

    lin, own_read, gated, routes = pl.pallas_call(
        readout_kernel,
        out_shape=(
            jax.ShapeDtypeStruct((length, heads * DV), BF16),
            jax.ShapeDtypeStruct((length, heads * DV), F32),
            jax.ShapeDtypeStruct((length, heads * DV), F32),
            jax.ShapeDtypeStruct((tok, LANES), BF16),
        ),
        grid=(1,),
        in_specs=blocks_of(query_proj, key_proj, gate_proj, head_gain.reshape(1, DV), log_decay, expert_ids.T,
                           route_weight.T) + [whole()] * 2,
        out_specs=(whole(),) * 4,
        compiler_params=pltpu.CompilerParams(vmem_limit_bytes=SMALL_VMEM),
        cost_estimate=pl.CostEstimate(flops=6 * 10**9, bytes_accessed=4 * 10**6, transcendentals=0),
    )(query_proj, key_proj, gate_proj, head_gain.reshape(1, DV), log_decay, expert_ids.T, route_weight.T, wu, prefixes)

    eye = jnp.concatenate([jnp.eye(DK, dtype=BF16), jnp.zeros((DK, DV), BF16)], axis=1)
    before = jnp.broadcast_to(eye, total.shape)
    summed, step = total, 1
    got = jnp.zeros((heads, DK, DV), BF16)
    later = jnp.zeros((), jnp.int32)
    while step < seqs:
        later = lax.rem(lax.div(here, step), 2)
        got = lax.ppermute(summed, "seq", [(i, i ^ step) for i in range(seqs)])
        if step == 1:
            got, out_sib, *sib = lax.optimization_barrier((got, out_sib, *sib))
        if 2 * step < seqs:
            summed, before = scan_step(later.reshape(1), summed, got, before, 4 * step >= seqs)
        step *= 2

    half = jax.ShapeDtypeStruct((places, tok, heads * DV), BF16)
    keep, send = pl.pallas_call(
        mix_kernel,
        out_shape=(half, half),
        in_specs=[whole(pltpu.SMEM)] + [whole()] * 5,
        out_specs=(whole(),) * 2,
        compiler_params=pltpu.CompilerParams(vmem_limit_bytes=SMALL_VMEM),
    )(jnp.stack([core, place, later]), before, got, lin, own_read, gated)
    got = lax.ppermute(send, "exp", swap)
    summands = exchange(project(keep, got, out_weight, out_sib))
    residual, normed = pl.pallas_call(
        norm_kernel,
        out_shape=(
            jax.ShapeDtypeStruct((tok, width), F32),
            jax.ShapeDtypeStruct((tok, width + LANES), BF16),
        ),
        in_specs=[whole()] * (3 + places),
        out_specs=(whole(),) * 2,
        compiler_params=pltpu.CompilerParams(vmem_limit_bytes=SMALL_VMEM),
    )(hidden_in, post_gain.reshape(1, width), routes, *summands)
    slots = exchange([normed] * places)
    summands = exchange(experts(jnp.stack([place, core]), slots, own, sib))
    return sum((s.astype(F32) for s in summands), residual).astype(BF16)


def solution(mesh):
    in_specs = (
        P(("seq", "exp"), None),
        P("seq", "exp"),
        P("seq", "exp"),
        P("seq", "exp"),
        P("seq", "exp"),
        P("exp", "seq"),
        P("exp", "seq"),
        P(),
        P("exp", None),
        P(),
        P(("seq", "exp"), None),
        P(("seq", "exp"), None),
        P("exp", None, None),
        P("exp", None, None),
        P("exp", None, None),
    )
    out_specs = P(("seq", "exp"), None)
    return jax.shard_map(
        per_device, mesh=mesh, in_specs=in_specs, out_specs=out_specs, check_vma=False
    )
```

```python
import functools

import jax
import jax.numpy as jnp
from jax import lax
from jax.experimental import pallas as pl
from jax.experimental.pallas import tpu as pltpu
from jax.sharding import PartitionSpec as P

DK = 128
DV = 128
EPS = 1e-06
BLOCK = 128
LANES = 128
F32 = jnp.float32
BF16 = jnp.bfloat16
EXACT = lax.Precision.HIGHEST
LARGE_VMEM = 60 * 1024 * 1024
SMALL_VMEM = 20 * 1024 * 1024
EXPERT_VMEM = 32 * 1024 * 1024
CHUNKS = 2
PAIRS_AT_ONCE = 16


def whole(memory_space=pltpu.VMEM):
    return pl.BlockSpec(memory_space=memory_space)


def blocks_of(*arrays):
    return [pl.BlockSpec(a.shape, lambda i, n=a.ndim: (0,) * n) for a in arrays]


def call(kernel, outs, *arrays, scalars=None, flops=0, vmem=LARGE_VMEM, scratch=()):
    params = pltpu.CompilerParams(vmem_limit_bytes=vmem)
    moved = sum(a.size * a.dtype.itemsize for a in (*arrays, *outs))
    return pl.pallas_call(
        kernel,
        grid=(1,),
        out_shape=tuple(outs),
        in_specs=([] if scalars is None else [whole(pltpu.SMEM)]) + blocks_of(*arrays),
        out_specs=tuple(blocks_of(*outs)),
        scratch_shapes=list(scratch),
        compiler_params=params,
        cost_estimate=pl.CostEstimate(flops=flops, bytes_accessed=moved, transcendentals=0),
    )(*(() if scalars is None else (scalars,)), *arrays)


def shape(dims, dtype):
    return jax.ShapeDtypeStruct(dims, dtype)


def mm(a, b):
    return jnp.dot(a.astype(BF16), b.astype(BF16), preferred_element_type=F32)


def mm_nt(a, b, precision=None):
    return lax.dot_general(
        a, b, (((1,), (1,)), ((), ())), preferred_element_type=F32, precision=precision
    )


def split(a):
    high = a.astype(BF16)
    return high, (a - high.astype(F32)).astype(BF16)


def mm_left2(a, b):
    high, low = split(a)
    return jnp.dot(
        jnp.concatenate([high, low], axis=1),
        jnp.concatenate([b, b], axis=0),
        preferred_element_type=F32,
    )


def mm_right2(a, b):
    high, low = split(b)
    return jnp.dot(
        jnp.concatenate([a, a], axis=1),
        jnp.concatenate([high, low], axis=0),
        preferred_element_type=F32,
    )


def mm_both2(a, b):
    a_high, a_low = split(a)
    b_high, b_low = split(b)
    return jnp.dot(
        jnp.concatenate([a_high, a_low, a_high], axis=1),
        jnp.concatenate([b_high, b_high, b_low], axis=0),
        preferred_element_type=F32,
    )


def grids():
    row = lax.broadcasted_iota(jnp.int32, (BLOCK, BLOCK), 0)
    col = lax.broadcasted_iota(jnp.int32, (BLOCK, BLOCK), 1)
    return row, col


def stacked(ref, blocks):
    return jnp.concatenate([ref[:, c * BLOCK : (c + 1) * BLOCK] for c in range(blocks)], axis=0)


def decays(decay_ref, blocks, row, col):
    by_row = stacked(decay_ref, blocks)
    upto = jnp.where(row >= col, 1.0, 0.0).astype(F32)
    cum_rows = mm_nt(by_row, upto, EXACT)
    cum_cols = mm_nt(upto, by_row, EXACT)
    return cum_rows, cum_cols


def state_kernel(key_ref, value_ref, decay_ref, rate_ref, wu_ref, prefix_ref, total_ref):
    heads = decay_ref.shape[0]
    key_heads = key_ref.shape[1] // DK
    group = heads // key_heads
    blocks = key_ref.shape[0] // BLOCK
    row, col = grids()
    gap_bits = jnp.bitwise_xor(row, col)
    strict = row > col
    diagonal = row == col
    eye = jnp.where(diagonal, 1.0, 0.0).astype(F32)
    cum_rows, cum_cols = decays(decay_ref, blocks, row, col)
    rate_rows = stacked(rate_ref, blocks)
    rate_cols = mm_nt(eye, rate_rows, EXACT)
    carried = [None] * heads
    pairs = [(c, h) for c in range(blocks) for h in range(heads)]
    unit_rows, unit_cols, keys, keys_t, grams = {}, {}, {}, {}, {}
    for c in range(blocks):
        tokens = slice(c * BLOCK, (c + 1) * BLOCK)
        for g in range(key_heads):
            key = key_ref[tokens, g * DK : (g + 1) * DK]
            gram = mm_nt(key, key)
            on_diagonal = jnp.where(diagonal, gram, 0.0)
            unit_rows[c, g] = lax.rsqrt(jnp.sum(on_diagonal, axis=0, keepdims=True) + EPS)
            unit_cols[c, g] = lax.rsqrt(jnp.sum(on_diagonal, axis=1, keepdims=True) + EPS)
            keys[c, g] = key
            keys_t[c, g] = key.astype(F32).T.astype(BF16)
            grams[c, g] = gram * unit_rows[c, g] * unit_cols[c, g]
    for lead in range(0, len(pairs), PAIRS_AT_ONCE):
        some = pairs[lead : lead + PAIRS_AT_ONCE]
        lower, solve = {}, {}
        for c, h in some:
            at = c * heads + h
            cum_row, cum_col = cum_rows[at : at + 1, :], cum_cols[:, at : at + 1]
            fade = jnp.exp(jnp.where(strict, cum_col - cum_row, 0.0))
            part = jnp.where(strict, grams[c, h // group] * fade * rate_cols[:, at : at + 1], 0.0)
            lower[c, h] = part
            solve[c, h] = eye - jnp.where(gap_bits == 1, part, 0.0)
        size = 2
        while size < BLOCK:
            shift = size.bit_length() - 1
            inside = lax.shift_right_logical(gap_bits, shift) == 1
            right = {p: mm(jnp.where(inside, lower[p], 0.0), solve[p]) for p in some}
            solve = {p: solve[p] - mm(solve[p], right[p]) for p in some}
            size *= 2
        first = {p: solve[p].astype(BF16) for p in some}
        rest = {p: eye - first[p].astype(F32) - mm_left2(lower[p], first[p]) for p in some}
        solve = {p: first[p].astype(F32) + mm(first[p], rest[p]) for p in some}
        tails = {}
        for c, h in some:
            tokens = slice(c * BLOCK, (c + 1) * BLOCK)
            at = c * heads + h
            g = h // group
            cum_row, cum_col = cum_rows[at : at + 1, :], cum_cols[:, at : at + 1]
            rate_row = rate_rows[at : at + 1, :]
            end = cum_row[:, BLOCK - 1 :]
            w = mm_left2(solve[c, h] * (rate_row * jnp.exp(cum_row) * unit_rows[c, g]), keys[c, g])
            u = mm_left2(solve[c, h] * rate_row, value_ref[tokens, h * DV : (h + 1) * DV])
            wu = jnp.concatenate([w, u], axis=1)
            wu_ref[h, c] = wu.astype(BF16)
            tails[c, h] = mm_right2(keys_t[c, g], wu * (jnp.exp(end - cum_col) * unit_cols[c, g]))
        for c, h in some:
            at = c * heads + h
            kept = jnp.exp(cum_rows[at : at + 1, BLOCK - 1 :])
            tail = tails[c, h]
            if c == 0:
                start = jnp.concatenate([eye, jnp.zeros((DK, DV), F32)], axis=1)
                prefix_ref[h, c] = start.astype(BF16)
                carried[h] = jnp.concatenate([kept * eye - tail[:, :DK], tail[:, DK:]], axis=1)
            else:
                bias = jnp.concatenate([jnp.zeros((DK, DK), F32), tail[:, DK:]], axis=1)
                prefix_ref[h, c] = carried[h].astype(BF16)
                carried[h] = kept * carried[h] + bias - mm_both2(tail[:, :DK], carried[h])
    for h in range(heads):
        total_ref[h] = carried[h].astype(BF16)


def readout_kernel(query_ref, key_ref, decay_ref, ids_ref, weight_ref, wu_ref, prefix_ref,
                   lin_ref, own_ref, routes_ref):
    expert = lax.broadcasted_iota(jnp.int32, (LANES, ids_ref.shape[1]), 0)
    routes = jnp.zeros(expert.shape, F32)
    for k in range(ids_ref.shape[0]):
        routes += jnp.where(
            ids_ref[k : k + 1, :] == expert, weight_ref[k : k + 1, :].astype(F32), 0.0
        )
    routes_ref[...] = routes.T.astype(BF16)
    heads = decay_ref.shape[0]
    key_heads = key_ref.shape[1] // DK
    group = heads // key_heads
    blocks = key_ref.shape[0] // BLOCK
    row, col = grids()
    causal = row >= col
    diagonal = row == col
    cum_rows, cum_cols = decays(decay_ref, blocks, row, col)
    for c in range(blocks):
        tokens = slice(c * BLOCK, (c + 1) * BLOCK)
        for g in range(key_heads):
            key = key_ref[tokens, g * DK : (g + 1) * DK]
            query = query_ref[tokens, g * DK : (g + 1) * DK]
            key_f, query_f = key.astype(F32), query.astype(F32)
            gram = jnp.where(diagonal, mm_nt(key, key), 0.0)
            unit_row = lax.rsqrt(jnp.sum(gram, axis=0, keepdims=True) + EPS)
            query_unit = query_f * (
                lax.rsqrt(jnp.sum(query_f * query_f, axis=1, keepdims=True) + EPS) * DK ** (-0.5)
            )
            query_scale = lax.rsqrt(
                jnp.sum(query_f * query_f, axis=1, keepdims=True) + EPS
            ) * DK ** (-0.5)
            plain = mm_nt(query, key) * unit_row * query_scale
            for h in range(g * group, (g + 1) * group):
                at = c * heads + h
                cum_row, cum_col = cum_rows[at : at + 1, :], cum_cols[:, at : at + 1]
                fade = jnp.exp(jnp.where(causal, cum_col - cum_row, 0.0))
                scores = jnp.where(causal, plain * fade, 0.0)
                mixed_wu = mm(scores, wu_ref[h, c])
                reach = query_unit * jnp.exp(cum_col) - mixed_wu[:, :DK]
                lanes = slice(h * DV, (h + 1) * DV)
                if c == 0:
                    lin_ref[tokens, lanes] = reach.astype(BF16)
                    own_ref[tokens, lanes] = mixed_wu[:, DK:]
                else:
                    spread = mm(reach, prefix_ref[h, c])
                    lin_ref[tokens, lanes] = spread[:, :DK].astype(BF16)
                    own_ref[tokens, lanes] = mixed_wu[:, DK:] + spread[:, DK:]


def mix_kernel(spot_ref, gain_ref, gate_ref, lin_ref, own_ref, *refs):
    *total_refs, keep_ref, send_ref, totals_ref = refs
    core, place, here = spot_ref[0], spot_ref[1], spot_ref[2]
    heads = total_refs[0].shape[0]
    places = keep_ref.shape[0]
    rows = keep_ref.shape[1]
    for d, total_ref in enumerate(total_refs):
        totals_ref[d] = total_ref[...]
    states = [jnp.zeros((DK, DV), F32) for _ in range(heads)]
    for source in range(len(total_refs)):
        at = jnp.maximum(jnp.bitwise_xor(here, source) - 1, 0)
        for h in range(heads):
            step = totals_ref[at, h]
            moved = mm(step[:, :DK], states[h]) + step[:, DK:].astype(F32)
            states[h] = jnp.where(source < here, moved, states[h])
    states = [state.astype(BF16) for state in states]
    for d in range(places):
        at = jnp.bitwise_xor(place, d)
        for out_ref, side in ((send_ref, 1 - core), (keep_ref, core)):
            tokens = pl.ds(pl.multiple_of((2 * at + side) * rows, rows), rows)
            for h in range(heads):
                lanes = slice(h * DV, (h + 1) * DV)
                readout = own_ref[tokens, lanes] + mm(lin_ref[tokens, lanes], states[h])
                scale = lax.rsqrt(jnp.mean(readout * readout, axis=1, keepdims=True) + EPS)
                gate = gate_ref[tokens, lanes].astype(F32)
                gated = gain_ref[...] * gate / (1.0 + jnp.exp(-gate))
                out_ref[d, :, lanes] = (readout * scale * gated).astype(BF16)


def project_kernel(tile, keep_ref, got_ref, own_ref, sib_ref, *out_refs):
    places, rows, depth = keep_ref.shape
    product = jnp.dot(
        keep_ref[...].reshape(-1, depth), own_ref[...], preferred_element_type=F32
    ) + jnp.dot(got_ref[...].reshape(-1, depth), sib_ref[...], preferred_element_type=F32)
    part = out_refs[0].shape[0]
    lanes = pl.ds(pl.multiple_of(pl.program_id(0) * tile, tile), tile)
    for number, out_ref in enumerate(out_refs):
        start = number % places * rows + number // places * part
        out_ref[:, lanes] = product[start : start + part].astype(BF16)


def project(keep, got, own, sib):
    places, rows, depth = keep.shape
    width = own.shape[1]
    tile = 512
    part = rows // CHUNKS
    outs = pl.pallas_call(
        functools.partial(project_kernel, tile),
        grid=(width // tile,),
        out_shape=(shape((part, width), BF16),) * (places * CHUNKS),
        in_specs=blocks_of(keep, got) + [pl.BlockSpec((depth, tile), lambda i: (0, i))] * 2,
        out_specs=(pl.BlockSpec((part, width), lambda i: (0, 0)),) * (places * CHUNKS),
        compiler_params=pltpu.CompilerParams(vmem_limit_bytes=LARGE_VMEM),
    )(keep, got, own, sib)
    return [outs[c * places : (c + 1) * places] for c in range(CHUNKS)]


def norm_kernel(chunk, hidden_ref, gain_ref, routes_ref, *refs):
    *part_refs, residual_ref, out_ref = refs
    rows = residual_ref.shape[0]
    tokens = slice(chunk * rows, (chunk + 1) * rows)
    residual = hidden_ref[tokens, :].astype(F32)
    for part_ref in part_refs:
        residual += part_ref[...].astype(F32)
    residual_ref[...] = residual
    scale = lax.rsqrt(jnp.mean(residual * residual, axis=1, keepdims=True) + EPS)
    width = residual.shape[1]
    out_ref[:, :width] = (residual * scale * gain_ref[...]).astype(BF16)
    out_ref[:, width:] = routes_ref[tokens, :]


def expert_kernel(places, halves, place_ref, *refs):
    slots = refs[:places]
    gate_own, up_own, down_own, gate_sib, up_sib, down_sib = refs[places : places + 6]
    out_refs = refs[places + 6 : -2]
    x_ref, sum_ref = refs[-2:]
    step = pl.program_id(0)
    place, core = place_ref[0], place_ref[1]
    rows, width = out_refs[0].shape

    @pl.when(step == 0)
    def _():
        for d, slot in enumerate(slots):
            x_ref[d * rows : (d + 1) * rows, :] = slot[...]

    def add(gate, up, down, expert, fresh):
        x = x_ref[:, :width]
        gate_act = jnp.dot(x, gate[0], preferred_element_type=F32)
        up_act = jnp.dot(x, up[0], preferred_element_type=F32)
        inner = (gate_act / (1.0 + jnp.exp(-gate_act)) * up_act).astype(BF16)
        routes = x_ref[:, width:].astype(F32)
        lane = lax.broadcasted_iota(jnp.int32, routes.shape, 1)
        weight = jnp.sum(jnp.where(lane == expert, routes, 0.0), axis=1, keepdims=True)
        more = jnp.dot(inner, down[0], preferred_element_type=F32) * weight

        @pl.when(fresh)
        def _():
            sum_ref[...] = more

        @pl.when(jnp.logical_not(fresh))
        def _():
            sum_ref[...] += more

    @pl.when(step < halves)
    def _():
        add(gate_own, up_own, down_own, 2 * place + core, step == 0)

    @pl.when(step >= halves)
    def _():
        add(gate_sib, up_sib, down_sib, 2 * place + 1 - core, step < 0)

    @pl.when(step == 2 * halves - 1)
    def _():
        for d, out_ref in enumerate(out_refs):
            out_ref[...] = sum_ref[d * rows : (d + 1) * rows].astype(BF16)


def experts(place_core, slots, own, sib):
    places = len(slots)
    rows = slots[0].shape[0]
    width = own[0].shape[1]
    inner = own[0].shape[2]
    tile = 256
    halves = inner // tile

    def specs(at):
        return [
            pl.BlockSpec((1, width, tile), lambda i: (0, 0, at(i))),
            pl.BlockSpec((1, width, tile), lambda i: (0, 0, at(i))),
            pl.BlockSpec((1, tile, width), lambda i: (0, at(i), 0)),
        ]

    return pl.pallas_call(
        functools.partial(expert_kernel, places, halves),
        grid=(2 * halves,),
        out_shape=(jax.ShapeDtypeStruct((rows, width), BF16),) * places,
        in_specs=[whole(pltpu.SMEM)]
        + blocks_of(*slots)
        + specs(lambda i: jnp.minimum(i, halves - 1))
        + specs(lambda i: jnp.maximum(i - halves, 0)),
        out_specs=(pl.BlockSpec((rows, width), lambda i: (0, 0)),) * places,
        scratch_shapes=[
            pltpu.VMEM((places * rows, slots[0].shape[1]), BF16),
            pltpu.VMEM((places * rows, width), F32),
        ],
        compiler_params=pltpu.CompilerParams(vmem_limit_bytes=EXPERT_VMEM),
    )(place_core, *slots, *own, *sib)


def between_places(places, d):
    return [(2 * i + c, 2 * (i ^ d) + c) for i in range(places) for c in range(2)]


def exchange(pieces):
    places = len(pieces)
    return [pieces[0]] + [
        lax.ppermute(pieces[d], "exp", between_places(places, d)) for d in range(1, places)
    ]


def per_device(
    hidden_in,
    query_proj,
    key_proj,
    value_proj,
    gate_proj,
    log_decay,
    write_rate,
    head_gain,
    out_weight,
    post_gain,
    expert_ids,
    route_weight,
    gate_weight,
    up_weight,
    down_weight,
):
    length = value_proj.shape[0]
    heads = value_proj.shape[1] // DV
    blocks = length // BLOCK
    tok, width = hidden_in.shape
    seqs, exps = lax.axis_size("seq"), lax.axis_size("exp")
    places = exps // 2
    me = lax.axis_index("exp")
    place, core = lax.div(me, 2), lax.rem(me, 2)
    here = lax.axis_index("seq")
    swap = [(i, i ^ 1) for i in range(exps)]

    out_sib = lax.ppermute(out_weight, "exp", swap)
    own = (gate_weight, up_weight, down_weight)
    sib = tuple(lax.ppermute(w, "exp", swap) for w in own)

    wide = shape((heads, blocks, DK, DK + DV), BF16)
    wu, prefixes, total = call(
        state_kernel,
        (wide, wide, shape((heads, DK, DK + DV), BF16)),
        key_proj,
        value_proj,
        log_decay,
        write_rate,
        flops=10**10,
    )
    total, out_sib, sib = lax.optimization_barrier((total, out_sib, sib))
    lin, own_read, routes = call(
        readout_kernel,
        (
            shape((length, heads * DV), BF16),
            shape((length, heads * DV), F32),
            shape((tok, LANES), BF16),
        ),
        query_proj,
        key_proj,
        log_decay,
        expert_ids.T,
        route_weight.T,
        wu,
        prefixes,
        flops=4 * 10**9,
    )

    totals = [
        lax.ppermute(total, "seq", [(i, i ^ d) for i in range(seqs)]) for d in range(1, seqs)
    ]

    half = shape((places, tok, heads * DV), BF16)
    keep, send = call(
        mix_kernel,
        (half, half),
        head_gain.reshape(1, DV),
        gate_proj,
        lin,
        own_read,
        *totals,
        scalars=jnp.stack([core, place, here]),
        flops=10**9,
        scratch=[pltpu.VMEM((seqs - 1, *total.shape), BF16)],
    )
    got = lax.ppermute(send, "exp", swap)
    parts = [exchange(pieces) for pieces in project(keep, got, out_weight, out_sib)]
    spot = jnp.stack([place, core])
    outs = []
    for chunk, summands in enumerate(parts):
        rows = tok // CHUNKS
        residual, normed = call(
            functools.partial(norm_kernel, chunk),
            (shape((rows, width), F32), shape((rows, width + LANES), BF16)),
            hidden_in,
            post_gain.reshape(1, width),
            routes,
            *summands,
            vmem=SMALL_VMEM,
        )
        slots = exchange([normed] * places)
        summands = exchange(experts(spot, slots, own, sib))
        outs.append(sum((s.astype(F32) for s in summands), residual).astype(BF16))
    return jnp.concatenate(outs, axis=0)


def solution(mesh):
    in_specs = (
        P(("seq", "exp"), None),
        P("seq", "exp"),
        P("seq", "exp"),
        P("seq", "exp"),
        P("seq", "exp"),
        P("exp", "seq"),
        P("exp", "seq"),
        P(),
        P("exp", None),
        P(),
        P(("seq", "exp"), None),
        P(("seq", "exp"), None),
        P("exp", None, None),
        P("exp", None, None),
        P("exp", None, None),
    )
    out_specs = P(("seq", "exp"), None)
    return jax.shard_map(
        per_device, mesh=mesh, in_specs=in_specs, out_specs=out_specs, check_vma=False
    )
```

```python
import functools

import jax
import jax.numpy as jnp
from jax import lax
from jax.experimental import pallas as pl
from jax.experimental.pallas import tpu as pltpu
from jax.sharding import PartitionSpec as P

DK = 128
DV = 128
EPS = 1e-06
BLOCK = 128
LANES = 128
F32 = jnp.float32
BF16 = jnp.bfloat16
EXACT = lax.Precision.HIGHEST
LARGE_VMEM = 60 * 1024 * 1024
SMALL_VMEM = 24 * 1024 * 1024
FETCH_VMEM = 24 * 1024 * 1024
CHUNKS = 2
SPARE = 256
PAIRS_AT_ONCE = 16


def whole(memory_space=pltpu.VMEM):
    return pl.BlockSpec(memory_space=memory_space)


def blocks_of(*arrays):
    return [pl.BlockSpec(a.shape, lambda i, n=a.ndim: (0,) * n) for a in arrays]


def fetch_kernel(*refs):
    count = len(refs) // 2
    copies = [
        pltpu.make_async_copy(refs[i], refs[count + i], refs[-1].at[i]) for i in range(count)
    ]
    for copy in copies:
        copy.start()
    for copy in copies:
        copy.wait()


def fetch(*arrays):
    return pl.pallas_call(
        fetch_kernel,
        out_shape=tuple(shape(a.shape, a.dtype) for a in arrays),
        in_specs=[whole(pl.ANY)] * len(arrays),
        out_specs=(whole(),) * len(arrays),
        scratch_shapes=[pltpu.SemaphoreType.DMA((len(arrays),))],
        compiler_params=pltpu.CompilerParams(vmem_limit_bytes=FETCH_VMEM),
        cost_estimate=pl.CostEstimate(
            flops=0, bytes_accessed=2 * sum(a.size * a.dtype.itemsize for a in arrays), transcendentals=0
        ),
    )(*arrays)


def resident(kernel, outs, *arrays, scalars=None, flops=0, scratch=()):
    moved = sum(a.size * a.dtype.itemsize for a in (*arrays, *outs))
    return pl.pallas_call(
        kernel,
        out_shape=tuple(outs),
        in_specs=([] if scalars is None else [whole(pltpu.SMEM)]) + [whole()] * len(arrays),
        out_specs=(whole(),) * len(outs),
        scratch_shapes=list(scratch),
        compiler_params=pltpu.CompilerParams(vmem_limit_bytes=SMALL_VMEM),
        cost_estimate=pl.CostEstimate(flops=flops, bytes_accessed=moved, transcendentals=0),
    )(*(() if scalars is None else (scalars,)), *arrays)


def after(value, *others):
    return lax.optimization_barrier((value, *others))[0]


def call(kernel, outs, *arrays, scalars=None, flops=0, vmem=LARGE_VMEM, scratch=(), stay=False):
    params = pltpu.CompilerParams(vmem_limit_bytes=vmem)
    moved = sum(a.size * a.dtype.itemsize for a in (*arrays, *outs))
    return pl.pallas_call(
        kernel,
        grid=(1,),
        out_shape=tuple(outs),
        in_specs=([] if scalars is None else [whole(pltpu.SMEM)]) + blocks_of(*arrays),
        out_specs=(whole(),) * len(outs) if stay else tuple(blocks_of(*outs)),
        scratch_shapes=list(scratch),
        compiler_params=params,
        cost_estimate=pl.CostEstimate(flops=flops, bytes_accessed=moved, transcendentals=0),
    )(*(() if scalars is None else (scalars,)), *arrays)


def shape(dims, dtype):
    return jax.ShapeDtypeStruct(dims, dtype)


def mm(a, b):
    return jnp.dot(a.astype(BF16), b.astype(BF16), preferred_element_type=F32)


def mm_nt(a, b, precision=None):
    return lax.dot_general(
        a, b, (((1,), (1,)), ((), ())), preferred_element_type=F32, precision=precision
    )


def split(a):
    high = a.astype(BF16)
    return high, (a - high.astype(F32)).astype(BF16)


def mm_left2(a, b):
    high, low = split(a)
    return jnp.dot(
        jnp.concatenate([high, low], axis=1),
        jnp.concatenate([b, b], axis=0),
        preferred_element_type=F32,
    )


def mm_right2(a, b):
    high, low = split(b)
    return jnp.dot(
        jnp.concatenate([a, a], axis=1),
        jnp.concatenate([high, low], axis=0),
        preferred_element_type=F32,
    )


def mm_both2(a, b):
    a_high, a_low = split(a)
    b_high, b_low = split(b)
    return jnp.dot(
        jnp.concatenate([a_high, a_low, a_high], axis=1),
        jnp.concatenate([b_high, b_high, b_low], axis=0),
        preferred_element_type=F32,
    )


def grids():
    row = lax.broadcasted_iota(jnp.int32, (BLOCK, BLOCK), 0)
    col = lax.broadcasted_iota(jnp.int32, (BLOCK, BLOCK), 1)
    return row, col


def stacked(ref, blocks):
    return jnp.concatenate([ref[:, c * BLOCK : (c + 1) * BLOCK] for c in range(blocks)], axis=0)


def decays(decay_ref, blocks, row, col):
    by_row = stacked(decay_ref, blocks)
    upto = jnp.where(row >= col, 1.0, 0.0).astype(F32)
    cum_rows = mm_nt(by_row, upto, EXACT)
    cum_cols = mm_nt(upto, by_row, EXACT)
    return cum_rows, cum_cols


def state_kernel(key_ref, value_ref, decay_ref, rate_ref, wu_ref, prefix_ref, total_ref):
    heads = decay_ref.shape[0]
    key_heads = key_ref.shape[1] // DK
    group = heads // key_heads
    blocks = key_ref.shape[0] // BLOCK
    row, col = grids()
    gap_bits = jnp.bitwise_xor(row, col)
    strict = row > col
    diagonal = row == col
    eye = jnp.where(diagonal, 1.0, 0.0).astype(F32)
    cum_rows, cum_cols = decays(decay_ref, blocks, row, col)
    rate_rows = stacked(rate_ref, blocks)
    rate_cols = mm_nt(eye, rate_rows, EXACT)
    carried = [None] * heads
    pairs = [(c, h) for c in range(blocks) for h in range(heads)]
    unit_rows, unit_cols, keys, keys_t, grams = {}, {}, {}, {}, {}
    for c in range(blocks):
        tokens = slice(c * BLOCK, (c + 1) * BLOCK)
        for g in range(key_heads):
            key = key_ref[tokens, g * DK : (g + 1) * DK]
            gram = mm_nt(key, key)
            on_diagonal = jnp.where(diagonal, gram, 0.0)
            unit_rows[c, g] = lax.rsqrt(jnp.sum(on_diagonal, axis=0, keepdims=True) + EPS)
            unit_cols[c, g] = lax.rsqrt(jnp.sum(on_diagonal, axis=1, keepdims=True) + EPS)
            keys[c, g] = key
            keys_t[c, g] = key.astype(F32).T.astype(BF16)
            grams[c, g] = gram * unit_rows[c, g] * unit_cols[c, g]
    for lead in range(0, len(pairs), PAIRS_AT_ONCE):
        some = pairs[lead : lead + PAIRS_AT_ONCE]
        lower, solve = {}, {}
        for c, h in some:
            at = c * heads + h
            cum_row, cum_col = cum_rows[at : at + 1, :], cum_cols[:, at : at + 1]
            fade = jnp.exp(jnp.where(strict, cum_col - cum_row, 0.0))
            part = jnp.where(strict, grams[c, h // group] * fade * rate_cols[:, at : at + 1], 0.0)
            lower[c, h] = part
            solve[c, h] = eye - jnp.where(gap_bits == 1, part, 0.0)
        size = 2
        while size < BLOCK:
            shift = size.bit_length() - 1
            inside = lax.shift_right_logical(gap_bits, shift) == 1
            right = {p: mm(jnp.where(inside, lower[p], 0.0), solve[p]) for p in some}
            solve = {p: solve[p] - mm(solve[p], right[p]) for p in some}
            size *= 2
        first = {p: solve[p].astype(BF16) for p in some}
        rest = {p: eye - first[p].astype(F32) - mm_left2(lower[p], first[p]) for p in some}
        solve = {p: first[p].astype(F32) + mm(first[p], rest[p]) for p in some}
        tails = {}
        for c, h in some:
            tokens = slice(c * BLOCK, (c + 1) * BLOCK)
            at = c * heads + h
            g = h // group
            cum_row, cum_col = cum_rows[at : at + 1, :], cum_cols[:, at : at + 1]
            rate_row = rate_rows[at : at + 1, :]
            end = cum_row[:, BLOCK - 1 :]
            w = mm_left2(solve[c, h] * (rate_row * jnp.exp(cum_row) * unit_rows[c, g]), keys[c, g])
            u = mm_left2(solve[c, h] * rate_row, value_ref[tokens, h * DV : (h + 1) * DV])
            wu = jnp.concatenate([w, u], axis=1)
            wu_ref[h, c] = wu.astype(BF16)
            tails[c, h] = mm_right2(keys_t[c, g], wu * (jnp.exp(end - cum_col) * unit_cols[c, g]))
        for c, h in some:
            at = c * heads + h
            kept = jnp.exp(cum_rows[at : at + 1, BLOCK - 1 :])
            tail = tails[c, h]
            if c == 0:
                start = jnp.concatenate([eye, jnp.zeros((DK, DV), F32)], axis=1)
                prefix_ref[h, c] = start.astype(BF16)
                carried[h] = jnp.concatenate([kept * eye - tail[:, :DK], tail[:, DK:]], axis=1)
            else:
                bias = jnp.concatenate([jnp.zeros((DK, DK), F32), tail[:, DK:]], axis=1)
                prefix_ref[h, c] = carried[h].astype(BF16)
                carried[h] = kept * carried[h] + bias - mm_both2(tail[:, :DK], carried[h])
    for h in range(heads):
        total_ref[h] = carried[h].astype(BF16)


def readout_kernel(query_ref, key_ref, decay_ref, ids_ref, weight_ref, wu_ref, prefix_ref,
                   lin_ref, own_ref, routes_ref):
    expert = lax.broadcasted_iota(jnp.int32, (LANES, ids_ref.shape[1]), 0)
    routes = jnp.zeros(expert.shape, F32)
    for k in range(ids_ref.shape[0]):
        routes += jnp.where(
            ids_ref[k : k + 1, :] == expert, weight_ref[k : k + 1, :].astype(F32), 0.0
        )
    routes_ref[...] = routes.T.astype(BF16)
    heads = decay_ref.shape[0]
    key_heads = key_ref.shape[1] // DK
    group = heads // key_heads
    blocks = key_ref.shape[0] // BLOCK
    row, col = grids()
    causal = row >= col
    diagonal = row == col
    cum_rows, cum_cols = decays(decay_ref, blocks, row, col)
    for c in range(blocks):
        tokens = slice(c * BLOCK, (c + 1) * BLOCK)
        for g in range(key_heads):
            key = key_ref[tokens, g * DK : (g + 1) * DK]
            query = query_ref[tokens, g * DK : (g + 1) * DK]
            key_f, query_f = key.astype(F32), query.astype(F32)
            gram = jnp.where(diagonal, mm_nt(key, key), 0.0)
            unit_row = lax.rsqrt(jnp.sum(gram, axis=0, keepdims=True) + EPS)
            query_unit = query_f * (
                lax.rsqrt(jnp.sum(query_f * query_f, axis=1, keepdims=True) + EPS) * DK ** (-0.5)
            )
            query_scale = lax.rsqrt(
                jnp.sum(query_f * query_f, axis=1, keepdims=True) + EPS
            ) * DK ** (-0.5)
            plain = mm_nt(query, key) * unit_row * query_scale
            for h in range(g * group, (g + 1) * group):
                at = c * heads + h
                cum_row, cum_col = cum_rows[at : at + 1, :], cum_cols[:, at : at + 1]
                fade = jnp.exp(jnp.where(causal, cum_col - cum_row, 0.0))
                scores = jnp.where(causal, plain * fade, 0.0)
                mixed_wu = mm(scores, wu_ref[h, c])
                reach = query_unit * jnp.exp(cum_col) - mixed_wu[:, :DK]
                lanes = slice(h * DV, (h + 1) * DV)
                if c == 0:
                    lin_ref[tokens, lanes] = reach.astype(BF16)
                    own_ref[tokens, lanes] = mixed_wu[:, DK:]
                else:
                    spread = mm(reach, prefix_ref[h, c])
                    lin_ref[tokens, lanes] = spread[:, :DK].astype(BF16)
                    own_ref[tokens, lanes] = mixed_wu[:, DK:] + spread[:, DK:]


def mix_kernel(spot_ref, gain_ref, gate_ref, lin_ref, own_ref, *refs):
    *total_refs, keep_ref, send_ref, totals_ref = refs
    core, place, here = spot_ref[0], spot_ref[1], spot_ref[2]
    heads = total_refs[0].shape[0]
    places = keep_ref.shape[0]
    rows = keep_ref.shape[1]
    for d, total_ref in enumerate(total_refs):
        totals_ref[d] = total_ref[...]
    states = [jnp.zeros((DK, DV), F32) for _ in range(heads)]
    for source in range(len(total_refs)):
        at = jnp.maximum(jnp.bitwise_xor(here, source) - 1, 0)
        for h in range(heads):
            step = totals_ref[at, h]
            moved = mm(step[:, :DK], states[h]) + step[:, DK:].astype(F32)
            states[h] = jnp.where(source < here, moved, states[h])
    states = [state.astype(BF16) for state in states]
    for d in range(places):
        at = jnp.bitwise_xor(place, d)
        for out_ref, side in ((send_ref, 1 - core), (keep_ref, core)):
            tokens = pl.ds(pl.multiple_of((2 * at + side) * rows, rows), rows)
            for h in range(heads):
                lanes = slice(h * DV, (h + 1) * DV)
                readout = own_ref[tokens, lanes] + mm(lin_ref[tokens, lanes], states[h])
                scale = lax.rsqrt(jnp.mean(readout * readout, axis=1, keepdims=True) + EPS)
                gate = gate_ref[tokens, lanes].astype(F32)
                gated = gain_ref[...] * gate / (1.0 + jnp.exp(-gate))
                out_ref[d, :, lanes] = (readout * scale * gated).astype(BF16)


def project_kernel(keep_ref, got_ref, own_ref, sib_ref, *out_refs):
    places, rows, depth = keep_ref.shape
    part, width = out_refs[0].shape
    tile = 512
    for lead in range(0, width, tile):
        lanes = slice(lead, lead + tile)
        product = jnp.dot(
            keep_ref[...].reshape(-1, depth), own_ref[:, lanes], preferred_element_type=F32
        ) + jnp.dot(got_ref[...].reshape(-1, depth), sib_ref[:, lanes], preferred_element_type=F32)
        for number, out_ref in enumerate(out_refs):
            start = number % places * rows + number // places * part
            out_ref[:, lanes] = product[start : start + part].astype(BF16)


def project(keep, got, own, sib):
    places, rows, _ = keep.shape
    outs = resident(
        project_kernel,
        (shape((rows // CHUNKS, own.shape[1]), BF16),) * (places * CHUNKS),
        keep,
        got,
        own,
        sib,
    )
    return [outs[c * places : (c + 1) * places] for c in range(CHUNKS)]


def norm_kernel(chunk, hidden_ref, gain_ref, routes_ref, *refs):
    *part_refs, residual_ref, out_ref = refs
    rows = residual_ref.shape[0]
    tokens = slice(chunk * rows, (chunk + 1) * rows)
    residual = hidden_ref[tokens, :].astype(F32)
    for part_ref in part_refs:
        residual += part_ref[:, : residual.shape[1]].astype(F32)
    residual_ref[...] = residual
    scale = lax.rsqrt(jnp.mean(residual * residual, axis=1, keepdims=True) + EPS)
    width = residual.shape[1]
    out_ref[:, :width] = (residual * scale * gain_ref[...]).astype(BF16)
    out_ref[:, width:] = routes_ref[tokens, :]


def expert_kernel(places, spot_ref, *refs):
    slots = refs[:places]
    weights = refs[places : places + 6]
    out_refs = refs[places + 6 :]
    place, core = spot_ref[0], spot_ref[1]
    rows, width = out_refs[0].shape
    x = jnp.concatenate([slot[:, :width] for slot in slots], axis=0)
    routes = jnp.concatenate([slot[:, width:] for slot in slots], axis=0).astype(F32)
    lane = lax.broadcasted_iota(jnp.int32, routes.shape, 1)
    inners, shares = [], []
    for number in range(2):
        gate_ref, up_ref = weights[3 * number : 3 * number + 2]
        expert = 2 * place + (core if number == 0 else 1 - core)
        gate_act = jnp.dot(x, gate_ref[0], preferred_element_type=F32)
        up_act = jnp.dot(x, up_ref[0], preferred_element_type=F32)
        inners.append((gate_act / (1.0 + jnp.exp(-gate_act)) * up_act).astype(BF16))
        shares.append(jnp.sum(jnp.where(lane == expert, routes, 0.0), axis=1, keepdims=True))
    tile = 512
    for lead in range(0, width, tile):
        lanes = slice(lead, lead + tile)
        total = jnp.dot(inners[0], weights[2][0, :, lanes], preferred_element_type=F32) * shares[0]
        total += jnp.dot(inners[1], weights[5][0, :, lanes], preferred_element_type=F32) * shares[1]
        for d, out_ref in enumerate(out_refs):
            out_ref[:, lanes] = total[d * rows : (d + 1) * rows].astype(BF16)


def experts(spot, slots, weights):
    rows = slots[0].shape[0]
    width = weights[0].shape[1]
    return resident(
        functools.partial(expert_kernel, len(slots)),
        (shape((rows, width), BF16),) * len(slots),
        *slots,
        *weights,
        scalars=spot,
        flops=3 * 10**9,
    )


def between_places(places, d):
    return [(2 * i + c, 2 * (i ^ d) + c) for i in range(places) for c in range(2)]


def exchange(piece, d):
    return lax.ppermute(piece, "exp", between_places(lax.axis_size("exp") // 2, d))


def reduce_places(chunks, spare=0):
    places = len(chunks[0])
    crossed = [[exchange(pieces[e ^ 1], 1) for e in range(2, places, 2)] for pieces in chunks]
    joined = []
    done = None
    for pieces, cross in zip(chunks, crossed):
        joined.append([])
        for e, got in zip(range(2, places, 2), cross):
            if done is not None:
                got = after(got, done)
            done = (pieces[e].astype(F32) + got.astype(F32)).astype(BF16)
            if len(joined) > 1:
                done = jnp.pad(done, ((0, 0), (0, spare)))
            joined[-1].append(done)
    return [
        [after(pieces[0], done)]
        + [exchange(sent, 2 * i + 2) for i, sent in enumerate(mine)]
        + [exchange(after(pieces[1], mine[-1]), 1)]
        for pieces, mine in zip(chunks, joined)
    ], done


def per_device(
    hidden_in,
    query_proj,
    key_proj,
    value_proj,
    gate_proj,
    log_decay,
    write_rate,
    head_gain,
    out_weight,
    post_gain,
    expert_ids,
    route_weight,
    gate_weight,
    up_weight,
    down_weight,
):
    length = value_proj.shape[0]
    heads = value_proj.shape[1] // DV
    blocks = length // BLOCK
    tok, width = hidden_in.shape
    seqs, exps = lax.axis_size("seq"), lax.axis_size("exp")
    places = exps // 2
    me = lax.axis_index("exp")
    place, core = lax.div(me, 2), lax.rem(me, 2)
    here = lax.axis_index("seq")
    swap = [(i, i ^ 1) for i in range(exps)]

    out_sib = lax.ppermute(out_weight, "exp", swap)
    own = (gate_weight, up_weight, down_weight)
    sib = tuple(lax.ppermute(w, "exp", swap) for w in own)

    wide = shape((heads, blocks, DK, DK + DV), BF16)
    wu, prefixes, total = call(
        state_kernel,
        (wide, wide, shape((heads, DK, DK + DV), BF16)),
        key_proj,
        value_proj,
        log_decay,
        write_rate,
        flops=10**10,
    )
    total, out_sib = lax.optimization_barrier((total, out_sib))
    lin, own_read, routes = call(
        readout_kernel,
        (
            shape((length, heads * DV), BF16),
            shape((length, heads * DV), F32),
            shape((tok, LANES), BF16),
        ),
        query_proj,
        key_proj,
        log_decay,
        expert_ids.T,
        route_weight.T,
        wu,
        prefixes,
        flops=4 * 10**9,
        vmem=SMALL_VMEM,
        stay=True,
    )

    totals = [
        lax.ppermute(total, "seq", [(i, i ^ d) for i in range(seqs)]) for d in range(1, seqs)
    ]
    fetched = fetch(gate_proj, out_weight, out_sib)
    totals, fetched, sib = lax.optimization_barrier((totals, fetched, sib))
    gate_here, out_own, out_sib = fetched

    half = shape((places, tok, heads * DV), BF16)
    keep, send = resident(
        mix_kernel,
        (half, half),
        head_gain.reshape(1, DV),
        gate_here,
        lin,
        own_read,
        *totals,
        scalars=jnp.stack([core, place, here]),
        flops=10**9,
        scratch=[pltpu.VMEM((seqs - 1, *total.shape), BF16)],
    )
    got = lax.ppermute(send, "exp", swap)
    spot = jnp.stack([place, core])
    rows = tok // CHUNKS
    chunks, joined = reduce_places(project(keep, got, out_own, out_sib), SPARE)
    sib = fetch(*(after(w, joined) for w in sib))
    chunks[0][0] = after(chunks[0][0], *sib)
    residuals, slots = [], []
    for chunk, summands in enumerate(chunks):
        if slots:
            summands[0] = after(summands[0], slots[-1][1])
        kept, sent = resident(
            functools.partial(norm_kernel, chunk),
            (shape((rows, width), F32), shape((rows, width + LANES), BF16)),
            hidden_in,
            post_gain.reshape(1, width),
            routes,
            *summands,
        )
        residuals.append(kept)
        slot = [sent] + [None] * (places - 1)
        for e in range(2, places, 2):
            slot[e] = exchange(sent, e)
        slot[1] = exchange(sent, 1)
        slots.append(slot)
    for slot in slots:
        for e in range(2, places, 2):
            slot[e + 1] = exchange(after(slot[e], slots[-1][0]), 1)
    made = []
    for slot in slots:
        if made:
            slot[0] = after(slot[0], made[-1][0])
        made.append(experts(spot, slot, (*own, *sib)))
    chunks, _ = reduce_places(made)
    return jnp.concatenate(
        [
            sum((s.astype(F32) for s in summands), kept).astype(BF16)
            for kept, summands in zip(residuals, chunks)
        ],
        axis=0,
    )


def solution(mesh):
    in_specs = (
        P(("seq", "exp"), None),
        P("seq", "exp"),
        P("seq", "exp"),
        P("seq", "exp"),
        P("seq", "exp"),
        P("exp", "seq"),
        P("exp", "seq"),
        P(),
        P("exp", None),
        P(),
        P(("seq", "exp"), None),
        P(("seq", "exp"), None),
        P("exp", None, None),
        P("exp", None, None),
        P("exp", None, None),
    )
    out_specs = P(("seq", "exp"), None)
    return jax.shard_map(
        per_device, mesh=mesh, in_specs=in_specs, out_specs=out_specs, check_vma=False
    )
```

```python
import functools

import jax
import jax.numpy as jnp
from jax import lax
from jax.experimental import pallas as pl
from jax.experimental.pallas import tpu as pltpu
from jax.sharding import PartitionSpec as P

DK = 128
DV = 128
EPS = 1e-06
BLOCK = 128
LANES = 128
F32 = jnp.float32
BF16 = jnp.bfloat16
EXACT = lax.Precision.HIGHEST
LARGE_VMEM = 60 * 1024 * 1024
SMALL_VMEM = 24 * 1024 * 1024
FETCH_VMEM = 24 * 1024 * 1024
SIZES = (32, 32)
SPARE = 256
PAIRS_AT_ONCE = 16


def whole(memory_space=pltpu.VMEM):
    return pl.BlockSpec(memory_space=memory_space)


def blocks_of(*arrays):
    return [pl.BlockSpec(a.shape, lambda i, n=a.ndim: (0,) * n) for a in arrays]


def fetch_kernel(*refs):
    count = len(refs) // 2
    copies = [
        pltpu.make_async_copy(refs[i], refs[count + i], refs[-1].at[i]) for i in range(count)
    ]
    for copy in copies:
        copy.start()
    for copy in copies:
        copy.wait()


def fetch(*arrays):
    return pl.pallas_call(
        fetch_kernel,
        out_shape=tuple(shape(a.shape, a.dtype) for a in arrays),
        in_specs=[whole(pl.ANY)] * len(arrays),
        out_specs=(whole(),) * len(arrays),
        scratch_shapes=[pltpu.SemaphoreType.DMA((len(arrays),))],
        compiler_params=pltpu.CompilerParams(vmem_limit_bytes=FETCH_VMEM),
        cost_estimate=pl.CostEstimate(
            flops=0, bytes_accessed=2 * sum(a.size * a.dtype.itemsize for a in arrays), transcendentals=0
        ),
    )(*arrays)


def resident(kernel, outs, *arrays, scalars=None, flops=0, scratch=()):
    moved = sum(a.size * a.dtype.itemsize for a in (*arrays, *outs))
    return pl.pallas_call(
        kernel,
        out_shape=tuple(outs),
        in_specs=([] if scalars is None else [whole(pltpu.SMEM)]) + [whole()] * len(arrays),
        out_specs=(whole(),) * len(outs),
        scratch_shapes=list(scratch),
        compiler_params=pltpu.CompilerParams(vmem_limit_bytes=SMALL_VMEM),
        cost_estimate=pl.CostEstimate(flops=flops, bytes_accessed=moved, transcendentals=0),
    )(*(() if scalars is None else (scalars,)), *arrays)


def after(value, *others):
    return lax.optimization_barrier((value, *others))[0]


def call(kernel, outs, *arrays, scalars=None, flops=0, vmem=LARGE_VMEM, scratch=(), stay=False):
    params = pltpu.CompilerParams(vmem_limit_bytes=vmem)
    moved = sum(a.size * a.dtype.itemsize for a in (*arrays, *outs))
    return pl.pallas_call(
        kernel,
        grid=(1,),
        out_shape=tuple(outs),
        in_specs=([] if scalars is None else [whole(pltpu.SMEM)]) + blocks_of(*arrays),
        out_specs=(whole(),) * len(outs) if stay else tuple(blocks_of(*outs)),
        scratch_shapes=list(scratch),
        compiler_params=params,
        cost_estimate=pl.CostEstimate(flops=flops, bytes_accessed=moved, transcendentals=0),
    )(*(() if scalars is None else (scalars,)), *arrays)


def shape(dims, dtype):
    return jax.ShapeDtypeStruct(dims, dtype)


def mm(a, b):
    return jnp.dot(a.astype(BF16), b.astype(BF16), preferred_element_type=F32)


def mm_nt(a, b, precision=None):
    return lax.dot_general(
        a, b, (((1,), (1,)), ((), ())), preferred_element_type=F32, precision=precision
    )


def split(a):
    high = a.astype(BF16)
    return high, (a - high.astype(F32)).astype(BF16)


def mm_left2(a, b):
    high, low = split(a)
    return jnp.dot(
        jnp.concatenate([high, low], axis=1),
        jnp.concatenate([b, b], axis=0),
        preferred_element_type=F32,
    )


def mm_both2(a, b):
    a_high, a_low = split(a)
    b_high, b_low = split(b)
    return jnp.dot(
        jnp.concatenate([a_high, a_low, a_high], axis=1),
        jnp.concatenate([b_high, b_high, b_low], axis=0),
        preferred_element_type=F32,
    )


def grids():
    row = lax.broadcasted_iota(jnp.int32, (BLOCK, BLOCK), 0)
    col = lax.broadcasted_iota(jnp.int32, (BLOCK, BLOCK), 1)
    return row, col


def stacked(ref, blocks):
    return jnp.concatenate([ref[:, c * BLOCK : (c + 1) * BLOCK] for c in range(blocks)], axis=0)


def decays(decay_ref, blocks, row, col):
    by_row = stacked(decay_ref, blocks)
    upto = jnp.where(row >= col, 1.0, 0.0).astype(F32)
    cum_rows = mm_nt(by_row, upto, EXACT)
    cum_cols = mm_nt(upto, by_row, EXACT)
    return cum_rows, cum_cols


def state_kernel(key_ref, value_ref, decay_ref, rate_ref, wu_ref, prefix_ref, total_ref):
    heads = decay_ref.shape[0]
    key_heads = key_ref.shape[1] // DK
    group = heads // key_heads
    blocks = key_ref.shape[0] // BLOCK
    row, col = grids()
    gap_bits = jnp.bitwise_xor(row, col)
    strict = row > col
    diagonal = row == col
    eye = jnp.where(diagonal, 1.0, 0.0).astype(F32)
    cum_rows, cum_cols = decays(decay_ref, blocks, row, col)
    rate_rows = stacked(rate_ref, blocks)
    rate_cols = mm_nt(eye, rate_rows, EXACT)
    carried = [None] * heads
    pairs = [(c, h) for c in range(blocks) for h in range(heads)]
    unit_rows, unit_cols, keys, keys_t, grams = {}, {}, {}, {}, {}
    for c in range(blocks):
        tokens = slice(c * BLOCK, (c + 1) * BLOCK)
        for g in range(key_heads):
            key = key_ref[tokens, g * DK : (g + 1) * DK]
            gram = mm_nt(key, key)
            on_diagonal = jnp.where(diagonal, gram, 0.0)
            unit_rows[c, g] = lax.rsqrt(jnp.sum(on_diagonal, axis=0, keepdims=True) + EPS)
            unit_cols[c, g] = lax.rsqrt(jnp.sum(on_diagonal, axis=1, keepdims=True) + EPS)
            keys[c, g] = key
            keys_t[c, g] = key.astype(F32).T.astype(BF16)
            grams[c, g] = gram * unit_rows[c, g] * unit_cols[c, g]
    for lead in range(0, len(pairs), PAIRS_AT_ONCE):
        some = pairs[lead : lead + PAIRS_AT_ONCE]
        lower, solve = {}, {}
        for c, h in some:
            at = c * heads + h
            cum_row, cum_col = cum_rows[at : at + 1, :], cum_cols[:, at : at + 1]
            fade = jnp.exp(jnp.where(strict, cum_col - cum_row, 0.0))
            part = jnp.where(strict, grams[c, h // group] * fade * rate_cols[:, at : at + 1], 0.0)
            lower[c, h] = part
            solve[c, h] = eye - jnp.where(gap_bits == 1, part, 0.0)
        size = 2
        while size < BLOCK:
            shift = size.bit_length() - 1
            inside = lax.shift_right_logical(gap_bits, shift) == 1
            right = {p: mm(jnp.where(inside, lower[p], 0.0), solve[p]) for p in some}
            solve = {p: solve[p] - mm(solve[p], right[p]) for p in some}
            size *= 2
        first = {p: solve[p].astype(BF16) for p in some}
        rest = {p: eye - first[p].astype(F32) - mm_left2(lower[p], first[p]) for p in some}
        solve = {p: first[p].astype(F32) + mm(first[p], rest[p]) for p in some}
        tails = {}
        for c, h in some:
            tokens = slice(c * BLOCK, (c + 1) * BLOCK)
            at = c * heads + h
            g = h // group
            cum_row, cum_col = cum_rows[at : at + 1, :], cum_cols[:, at : at + 1]
            rate_row = rate_rows[at : at + 1, :]
            end = cum_row[:, BLOCK - 1 :]
            w = mm(solve[c, h] * (rate_row * jnp.exp(cum_row) * unit_rows[c, g]), keys[c, g])
            u = mm(solve[c, h] * rate_row, value_ref[tokens, h * DV : (h + 1) * DV])
            wu = jnp.concatenate([w, u], axis=1)
            wu_ref[h, c] = wu.astype(BF16)
            tails[c, h] = mm(keys_t[c, g], wu * (jnp.exp(end - cum_col) * unit_cols[c, g]))
        for c, h in some:
            at = c * heads + h
            kept = jnp.exp(cum_rows[at : at + 1, BLOCK - 1 :])
            tail = tails[c, h]
            if c == 0:
                start = jnp.concatenate([eye, jnp.zeros((DK, DV), F32)], axis=1)
                prefix_ref[h, c] = start.astype(BF16)
                carried[h] = jnp.concatenate([kept * eye - tail[:, :DK], tail[:, DK:]], axis=1)
            else:
                bias = jnp.concatenate([jnp.zeros((DK, DK), F32), tail[:, DK:]], axis=1)
                prefix_ref[h, c] = carried[h].astype(BF16)
                carried[h] = kept * carried[h] + bias - mm_both2(tail[:, :DK], carried[h])
    for h in range(heads):
        total_ref[h] = carried[h].astype(BF16)


def readout_kernel(query_ref, key_ref, decay_ref, ids_ref, weight_ref, wu_ref, prefix_ref,
                   lin_ref, own_ref, routes_ref):
    expert = lax.broadcasted_iota(jnp.int32, (LANES, ids_ref.shape[1]), 0)
    routes = jnp.zeros(expert.shape, F32)
    for k in range(ids_ref.shape[0]):
        routes += jnp.where(
            ids_ref[k : k + 1, :] == expert, weight_ref[k : k + 1, :].astype(F32), 0.0
        )
    routes_ref[...] = routes.T.astype(BF16)
    heads = decay_ref.shape[0]
    key_heads = key_ref.shape[1] // DK
    group = heads // key_heads
    blocks = key_ref.shape[0] // BLOCK
    row, col = grids()
    causal = row >= col
    diagonal = row == col
    cum_rows, cum_cols = decays(decay_ref, blocks, row, col)
    for c in range(blocks):
        tokens = slice(c * BLOCK, (c + 1) * BLOCK)
        for g in range(key_heads):
            key = key_ref[tokens, g * DK : (g + 1) * DK]
            query = query_ref[tokens, g * DK : (g + 1) * DK]
            key_f, query_f = key.astype(F32), query.astype(F32)
            gram = jnp.where(diagonal, mm_nt(key, key), 0.0)
            unit_row = lax.rsqrt(jnp.sum(gram, axis=0, keepdims=True) + EPS)
            query_unit = query_f * (
                lax.rsqrt(jnp.sum(query_f * query_f, axis=1, keepdims=True) + EPS) * DK ** (-0.5)
            )
            query_scale = lax.rsqrt(
                jnp.sum(query_f * query_f, axis=1, keepdims=True) + EPS
            ) * DK ** (-0.5)
            plain = mm_nt(query, key) * unit_row * query_scale
            for h in range(g * group, (g + 1) * group):
                at = c * heads + h
                cum_row, cum_col = cum_rows[at : at + 1, :], cum_cols[:, at : at + 1]
                fade = jnp.exp(jnp.where(causal, cum_col - cum_row, 0.0))
                scores = jnp.where(causal, plain * fade, 0.0)
                mixed_wu = mm(scores, wu_ref[h, c])
                reach = query_unit * jnp.exp(cum_col) - mixed_wu[:, :DK]
                lanes = slice(h * DV, (h + 1) * DV)
                if c == 0:
                    lin_ref[tokens, lanes] = reach.astype(BF16)
                    own_ref[tokens, lanes] = mixed_wu[:, DK:]
                else:
                    spread = mm(reach, prefix_ref[h, c])
                    lin_ref[tokens, lanes] = spread[:, :DK].astype(BF16)
                    own_ref[tokens, lanes] = mixed_wu[:, DK:] + spread[:, DK:]


def mix_kernel(spot_ref, gain_ref, gate_ref, lin_ref, own_ref, *refs):
    *total_refs, keep_ref, send_ref, totals_ref = refs
    core, place, here = spot_ref[0], spot_ref[1], spot_ref[2]
    heads = total_refs[0].shape[0]
    places = keep_ref.shape[0]
    rows = keep_ref.shape[1]
    for d, total_ref in enumerate(total_refs):
        totals_ref[d] = total_ref[...]
    states = [jnp.zeros((DK, DV), F32) for _ in range(heads)]
    for source in range(len(total_refs)):
        at = jnp.maximum(jnp.bitwise_xor(here, source) - 1, 0)
        for h in range(heads):
            step = totals_ref[at, h]
            moved = mm(step[:, :DK], states[h]) + step[:, DK:].astype(F32)
            states[h] = jnp.where(source < here, moved, states[h])
    states = [state.astype(BF16) for state in states]
    for d in range(places):
        at = jnp.bitwise_xor(place, d)
        for out_ref, side in ((send_ref, 1 - core), (keep_ref, core)):
            tokens = pl.ds(pl.multiple_of((2 * at + side) * rows, rows), rows)
            for h in range(heads):
                lanes = slice(h * DV, (h + 1) * DV)
                readout = own_ref[tokens, lanes] + mm(lin_ref[tokens, lanes], states[h])
                scale = lax.rsqrt(jnp.mean(readout * readout, axis=1, keepdims=True) + EPS)
                gate = gate_ref[tokens, lanes].astype(F32)
                gated = gain_ref[...] * gate / (1.0 + jnp.exp(-gate))
                out_ref[d, :, lanes] = (readout * scale * gated).astype(BF16)


def project_kernel(keep_ref, got_ref, own_ref, sib_ref, *out_refs):
    places, rows, depth = keep_ref.shape
    width = out_refs[0].shape[1]
    tile = 512
    for lead in range(0, width, tile):
        lanes = slice(lead, lead + tile)
        product = jnp.dot(
            keep_ref[...].reshape(-1, depth), own_ref[:, lanes], preferred_element_type=F32
        ) + jnp.dot(got_ref[...].reshape(-1, depth), sib_ref[:, lanes], preferred_element_type=F32)
        start = 0
        for lead_ref in range(0, len(out_refs), places):
            part = out_refs[lead_ref].shape[0]
            for d in range(places):
                at = d * rows + start
                out_refs[lead_ref + d][:, lanes] = product[at : at + part].astype(BF16)
            start += part


def project(keep, got, own, sib, sizes):
    places, rows, _ = keep.shape
    outs = resident(
        project_kernel,
        [shape((size, own.shape[1]), BF16) for size in sizes for _ in range(places)],
        keep,
        got,
        own,
        sib,
    )
    return [outs[c * places : (c + 1) * places] for c in range(len(sizes))]


def norm_kernel(start, hidden_ref, gain_ref, routes_ref, *refs):
    *part_refs, residual_ref, out_ref = refs
    rows = residual_ref.shape[0]
    tokens = slice(start, start + rows)
    residual = hidden_ref[tokens, :].astype(F32)
    for part_ref in part_refs:
        residual += part_ref[:, : residual.shape[1]].astype(F32)
    residual_ref[...] = residual
    scale = lax.rsqrt(jnp.mean(residual * residual, axis=1, keepdims=True) + EPS)
    width = residual.shape[1]
    out_ref[:, :width] = (residual * scale * gain_ref[...]).astype(BF16)
    out_ref[:, width:] = routes_ref[tokens, :]


def expert_kernel(places, spot_ref, *refs):
    slots = refs[:places]
    weights = refs[places : places + 6]
    out_refs = refs[places + 6 :]
    place, core = spot_ref[0], spot_ref[1]
    rows, width = out_refs[0].shape
    x = jnp.concatenate([slot[:, :width] for slot in slots], axis=0)
    routes = jnp.concatenate([slot[:, width:] for slot in slots], axis=0).astype(F32)
    lane = lax.broadcasted_iota(jnp.int32, routes.shape, 1)
    inners, shares = [], []
    for number in range(2):
        gate_ref, up_ref = weights[3 * number : 3 * number + 2]
        expert = 2 * place + (core if number == 0 else 1 - core)
        gate_act = jnp.dot(x, gate_ref[0], preferred_element_type=F32)
        up_act = jnp.dot(x, up_ref[0], preferred_element_type=F32)
        inners.append((gate_act / (1.0 + jnp.exp(-gate_act)) * up_act).astype(BF16))
        shares.append(jnp.sum(jnp.where(lane == expert, routes, 0.0), axis=1, keepdims=True))
    tile = 512
    for lead in range(0, width, tile):
        lanes = slice(lead, lead + tile)
        total = jnp.dot(inners[0], weights[2][0, :, lanes], preferred_element_type=F32) * shares[0]
        total += jnp.dot(inners[1], weights[5][0, :, lanes], preferred_element_type=F32) * shares[1]
        for d, out_ref in enumerate(out_refs):
            out_ref[:, lanes] = total[d * rows : (d + 1) * rows].astype(BF16)


def experts(spot, slots, weights):
    rows = slots[0].shape[0]
    width = weights[0].shape[1]
    return resident(
        functools.partial(expert_kernel, len(slots)),
        (shape((rows, width), BF16),) * len(slots),
        *slots,
        *weights,
        scalars=spot,
        flops=3 * 10**9,
    )


def between_places(places, d):
    return [(2 * i + c, 2 * (i ^ d) + c) for i in range(places) for c in range(2)]


def exchange(piece, d):
    return lax.ppermute(piece, "exp", between_places(lax.axis_size("exp") // 2, d))


def reduce_places(chunks, spare=0):
    places = len(chunks[0])
    crossed = [[exchange(pieces[e ^ 1], 1) for e in range(2, places, 2)] for pieces in chunks]
    joined = []
    done = None
    for pieces, cross in zip(chunks, crossed):
        joined.append([])
        for e, got in zip(range(2, places, 2), cross):
            if done is not None:
                got = after(got, done)
            done = (pieces[e].astype(F32) + got.astype(F32)).astype(BF16)
            if len(joined) > 1:
                done = jnp.pad(done, ((0, 0), (0, spare)))
            joined[-1].append(done)
    return [
        [after(pieces[0], done)]
        + [exchange(sent, 2 * i + 2) for i, sent in enumerate(mine)]
        + [exchange(after(pieces[1], mine[-1]), 1)]
        for pieces, mine in zip(chunks, joined)
    ], done


def per_device(
    hidden_in,
    query_proj,
    key_proj,
    value_proj,
    gate_proj,
    log_decay,
    write_rate,
    head_gain,
    out_weight,
    post_gain,
    expert_ids,
    route_weight,
    gate_weight,
    up_weight,
    down_weight,
):
    length = value_proj.shape[0]
    heads = value_proj.shape[1] // DV
    blocks = length // BLOCK
    tok, width = hidden_in.shape
    seqs, exps = lax.axis_size("seq"), lax.axis_size("exp")
    places = exps // 2
    me = lax.axis_index("exp")
    place, core = lax.div(me, 2), lax.rem(me, 2)
    here = lax.axis_index("seq")
    swap = [(i, i ^ 1) for i in range(exps)]

    out_sib = lax.ppermute(out_weight, "exp", swap)
    own = (gate_weight, up_weight, down_weight)
    sib = tuple(lax.ppermute(w, "exp", swap) for w in own)

    wide = shape((heads, blocks, DK, DK + DV), BF16)
    wu, prefixes, total = call(
        state_kernel,
        (wide, wide, shape((heads, DK, DK + DV), BF16)),
        key_proj,
        value_proj,
        log_decay,
        write_rate,
        flops=10**10,
    )
    total, out_sib = lax.optimization_barrier((total, out_sib))
    lin, own_read, routes = call(
        readout_kernel,
        (
            shape((length, heads * DV), BF16),
            shape((length, heads * DV), F32),
            shape((tok, LANES), BF16),
        ),
        query_proj,
        key_proj,
        log_decay,
        expert_ids.T,
        route_weight.T,
        wu,
        prefixes,
        flops=4 * 10**9,
        vmem=SMALL_VMEM,
        stay=True,
    )

    totals = [
        lax.ppermute(total, "seq", [(i, i ^ d) for i in range(seqs)]) for d in range(1, seqs)
    ]
    fetched = fetch(gate_proj, out_weight, out_sib)
    totals, fetched, sib = lax.optimization_barrier((totals, fetched, sib))
    gate_here, out_own, out_sib = fetched

    half = shape((places, tok, heads * DV), BF16)
    keep, send = resident(
        mix_kernel,
        (half, half),
        head_gain.reshape(1, DV),
        gate_here,
        lin,
        own_read,
        *totals,
        scalars=jnp.stack([core, place, here]),
        flops=10**9,
        scratch=[pltpu.VMEM((seqs - 1, *total.shape), BF16)],
    )
    got = lax.ppermute(send, "exp", swap)
    spot = jnp.stack([place, core])
    sizes = SIZES if sum(SIZES) == tok else (tok // 2, tok // 2)
    starts = [sum(sizes[:i]) for i in range(len(sizes))]
    chunks, joined = reduce_places(project(keep, got, out_own, out_sib, sizes), SPARE)
    sib = fetch(*(after(w, joined) for w in sib))
    chunks[0][0] = after(chunks[0][0], *sib)
    residuals, slots = [], []
    for chunk, summands in enumerate(chunks):
        if slots:
            summands[0] = after(summands[0], *slots[-1][1:3])
        kept, sent = resident(
            functools.partial(norm_kernel, starts[chunk]),
            (shape((sizes[chunk], width), F32), shape((sizes[chunk], width + LANES), BF16)),
            hidden_in,
            post_gain.reshape(1, width),
            routes,
            *summands,
        )
        residuals.append(kept)
        slot = [sent] + [None] * (places - 1)
        for e in range(2, places, 2):
            slot[e] = exchange(sent, e)
        slot[1] = exchange(sent, 1)
        slots.append(slot)
    for slot in slots:
        for e in range(2, places, 2):
            slot[e + 1] = exchange(after(slot[e], slots[-1][0]), 1)
    made = []
    for slot in slots:
        if made:
            slot[0] = after(slot[0], made[-1][0])
        made.append(experts(spot, slot, (*own, *sib)))
    chunks, _ = reduce_places(made)
    return jnp.concatenate(
        [
            sum((s.astype(F32) for s in summands), kept).astype(BF16)
            for kept, summands in zip(residuals, chunks)
        ],
        axis=0,
    )


def solution(mesh):
    in_specs = (
        P(("seq", "exp"), None),
        P("seq", "exp"),
        P("seq", "exp"),
        P("seq", "exp"),
        P("seq", "exp"),
        P("exp", "seq"),
        P("exp", "seq"),
        P(),
        P("exp", None),
        P(),
        P(("seq", "exp"), None),
        P(("seq", "exp"), None),
        P("exp", None, None),
        P("exp", None, None),
        P("exp", None, None),
    )
    out_specs = P(("seq", "exp"), None)
    return jax.shard_map(
        per_device, mesh=mesh, in_specs=in_specs, out_specs=out_specs, check_vma=False
    )
```

```python
import functools

import jax
import jax.numpy as jnp
from jax import lax
from jax.experimental import pallas as pl
from jax.experimental.pallas import tpu as pltpu
from jax.sharding import PartitionSpec as P

DK = 128
DV = 128
EPS = 1e-06
BLOCK = 128
LANES = 128
F32 = jnp.float32
BF16 = jnp.bfloat16
EXACT = lax.Precision.HIGHEST
LARGE_VMEM = 60 * 1024 * 1024
SMALL_VMEM = 24 * 1024 * 1024
FETCH_VMEM = 24 * 1024 * 1024
SIZES = (32, 32)
SPARE = 256
PAIRS_AT_ONCE = 16


def whole(memory_space=pltpu.VMEM):
    return pl.BlockSpec(memory_space=memory_space)


def blocks_of(*arrays):
    return [pl.BlockSpec(a.shape, lambda i, n=a.ndim: (0,) * n) for a in arrays]


def fetch_kernel(*refs):
    count = len(refs) // 2
    copies = [
        pltpu.make_async_copy(refs[i], refs[count + i], refs[-1].at[i]) for i in range(count)
    ]
    for copy in copies:
        copy.start()
    for copy in copies:
        copy.wait()


def fetch(*arrays):
    return pl.pallas_call(
        fetch_kernel,
        out_shape=tuple(shape(a.shape, a.dtype) for a in arrays),
        in_specs=[whole(pl.ANY)] * len(arrays),
        out_specs=(whole(),) * len(arrays),
        scratch_shapes=[pltpu.SemaphoreType.DMA((len(arrays),))],
        compiler_params=pltpu.CompilerParams(vmem_limit_bytes=FETCH_VMEM),
        cost_estimate=pl.CostEstimate(
            flops=0, bytes_accessed=2 * sum(a.size * a.dtype.itemsize for a in arrays), transcendentals=0
        ),
    )(*arrays)


def resident(kernel, outs, *arrays, scalars=None, flops=0, scratch=()):
    moved = sum(a.size * a.dtype.itemsize for a in (*arrays, *outs))
    return pl.pallas_call(
        kernel,
        out_shape=tuple(outs),
        in_specs=([] if scalars is None else [whole(pltpu.SMEM)]) + [whole()] * len(arrays),
        out_specs=(whole(),) * len(outs),
        scratch_shapes=list(scratch),
        compiler_params=pltpu.CompilerParams(vmem_limit_bytes=SMALL_VMEM),
        cost_estimate=pl.CostEstimate(flops=flops, bytes_accessed=moved, transcendentals=0),
    )(*(() if scalars is None else (scalars,)), *arrays)


def after(value, *others):
    return lax.optimization_barrier((value, *others))[0]


def call(kernel, outs, *arrays, scalars=None, flops=0, vmem=LARGE_VMEM, scratch=(), stay=False):
    params = pltpu.CompilerParams(vmem_limit_bytes=vmem)
    moved = sum(a.size * a.dtype.itemsize for a in (*arrays, *outs))
    return pl.pallas_call(
        kernel,
        grid=(1,),
        out_shape=tuple(outs),
        in_specs=([] if scalars is None else [whole(pltpu.SMEM)]) + blocks_of(*arrays),
        out_specs=(whole(),) * len(outs) if stay else tuple(blocks_of(*outs)),
        scratch_shapes=list(scratch),
        compiler_params=params,
        cost_estimate=pl.CostEstimate(flops=flops, bytes_accessed=moved, transcendentals=0),
    )(*(() if scalars is None else (scalars,)), *arrays)


def shape(dims, dtype):
    return jax.ShapeDtypeStruct(dims, dtype)


def mm(a, b):
    return jnp.dot(a.astype(BF16), b.astype(BF16), preferred_element_type=F32)


def mm_nt(a, b, precision=None):
    return lax.dot_general(
        a, b, (((1,), (1,)), ((), ())), preferred_element_type=F32, precision=precision
    )


def split(a):
    high = a.astype(BF16)
    return high, (a - high.astype(F32)).astype(BF16)


def mm_left2(a, b):
    high, low = split(a)
    return jnp.dot(
        jnp.concatenate([high, low], axis=1),
        jnp.concatenate([b, b], axis=0),
        preferred_element_type=F32,
    )


def mm_both2(a, b):
    a_high, a_low = split(a)
    b_high, b_low = split(b)
    return jnp.dot(
        jnp.concatenate([a_high, a_low, a_high], axis=1),
        jnp.concatenate([b_high, b_high, b_low], axis=0),
        preferred_element_type=F32,
    )


def grids():
    row = lax.broadcasted_iota(jnp.int32, (BLOCK, BLOCK), 0)
    col = lax.broadcasted_iota(jnp.int32, (BLOCK, BLOCK), 1)
    return row, col


def stacked(ref, blocks):
    return jnp.concatenate([ref[:, c * BLOCK : (c + 1) * BLOCK] for c in range(blocks)], axis=0)


def decays(decay_ref, blocks, row, col):
    by_row = stacked(decay_ref, blocks)
    upto = jnp.where(row >= col, 1.0, 0.0).astype(F32)
    cum_rows = mm_nt(by_row, upto, EXACT)
    cum_cols = mm_nt(upto, by_row, EXACT)
    return cum_rows, cum_cols


def state_kernel(key_ref, value_ref, decay_ref, rate_ref, wu_ref, prefix_ref, total_ref):
    heads = decay_ref.shape[0]
    key_heads = key_ref.shape[1] // DK
    group = heads // key_heads
    blocks = key_ref.shape[0] // BLOCK
    row, col = grids()
    gap_bits = jnp.bitwise_xor(row, col)
    strict = row > col
    diagonal = row == col
    eye = jnp.where(diagonal, 1.0, 0.0).astype(F32)
    cum_rows, cum_cols = decays(decay_ref, blocks, row, col)
    rate_rows = stacked(rate_ref, blocks)
    rate_cols = mm_nt(eye, rate_rows, EXACT)
    carried = [None] * heads
    pairs = [(c, h) for c in range(blocks) for h in range(heads)]
    unit_rows, unit_cols, keys, keys_t, grams = {}, {}, {}, {}, {}
    for c in range(blocks):
        tokens = slice(c * BLOCK, (c + 1) * BLOCK)
        for g in range(key_heads):
            key = key_ref[tokens, g * DK : (g + 1) * DK]
            gram = mm_nt(key, key)
            on_diagonal = jnp.where(diagonal, gram, 0.0)
            unit_rows[c, g] = lax.rsqrt(jnp.sum(on_diagonal, axis=0, keepdims=True) + EPS)
            unit_cols[c, g] = lax.rsqrt(jnp.sum(on_diagonal, axis=1, keepdims=True) + EPS)
            keys[c, g] = key
            keys_t[c, g] = key.astype(F32).T.astype(BF16)
            grams[c, g] = gram * unit_rows[c, g] * unit_cols[c, g]
    for lead in range(0, len(pairs), PAIRS_AT_ONCE):
        some = pairs[lead : lead + PAIRS_AT_ONCE]
        lower, solve = {}, {}
        for c, h in some:
            at = c * heads + h
            cum_row, cum_col = cum_rows[at : at + 1, :], cum_cols[:, at : at + 1]
            fade = jnp.exp(jnp.where(strict, cum_col - cum_row, 0.0))
            part = jnp.where(strict, grams[c, h // group] * fade * rate_cols[:, at : at + 1], 0.0)
            lower[c, h] = part
            solve[c, h] = eye - jnp.where(gap_bits == 1, part, 0.0)
        size = 2
        while size < BLOCK:
            shift = size.bit_length() - 1
            inside = lax.shift_right_logical(gap_bits, shift) == 1
            right = {p: mm(jnp.where(inside, lower[p], 0.0), solve[p]) for p in some}
            solve = {p: solve[p] - mm(solve[p], right[p]) for p in some}
            size *= 2
        first = {p: solve[p].astype(BF16) for p in some}
        rest = {p: eye - first[p].astype(F32) - mm_left2(lower[p], first[p]) for p in some}
        solve = {p: first[p].astype(F32) + mm(first[p], rest[p]) for p in some}
        tails = {}
        for c, h in some:
            tokens = slice(c * BLOCK, (c + 1) * BLOCK)
            at = c * heads + h
            g = h // group
            cum_row, cum_col = cum_rows[at : at + 1, :], cum_cols[:, at : at + 1]
            rate_row = rate_rows[at : at + 1, :]
            end = cum_row[:, BLOCK - 1 :]
            w = mm(solve[c, h] * (rate_row * jnp.exp(cum_row) * unit_rows[c, g]), keys[c, g])
            u = mm(solve[c, h] * rate_row, value_ref[tokens, h * DV : (h + 1) * DV])
            wu = jnp.concatenate([w, u], axis=1)
            wu_ref[h, c] = wu.astype(BF16)
            tails[c, h] = mm(keys_t[c, g], wu * (jnp.exp(end - cum_col) * unit_cols[c, g]))
        for c, h in some:
            at = c * heads + h
            kept = jnp.exp(cum_rows[at : at + 1, BLOCK - 1 :])
            tail = tails[c, h]
            if c == 0:
                start = jnp.concatenate([eye, jnp.zeros((DK, DV), F32)], axis=1)
                prefix_ref[h, c] = start.astype(BF16)
                carried[h] = jnp.concatenate([kept * eye - tail[:, :DK], tail[:, DK:]], axis=1)
            else:
                bias = jnp.concatenate([jnp.zeros((DK, DK), F32), tail[:, DK:]], axis=1)
                prefix_ref[h, c] = carried[h].astype(BF16)
                carried[h] = kept * carried[h] + bias - mm_both2(tail[:, :DK], carried[h])
    for h in range(heads):
        total_ref[h] = carried[h].astype(BF16)


def readout_kernel(query_ref, key_ref, decay_ref, ids_ref, weight_ref, wu_ref, prefix_ref,
                   lin_ref, own_ref, routes_ref):
    expert = lax.broadcasted_iota(jnp.int32, (LANES, ids_ref.shape[1]), 0)
    routes = jnp.zeros(expert.shape, F32)
    for k in range(ids_ref.shape[0]):
        routes += jnp.where(
            ids_ref[k : k + 1, :] == expert, weight_ref[k : k + 1, :].astype(F32), 0.0
        )
    routes_ref[...] = routes.T.astype(BF16)
    heads = decay_ref.shape[0]
    key_heads = key_ref.shape[1] // DK
    group = heads // key_heads
    blocks = key_ref.shape[0] // BLOCK
    row, col = grids()
    causal = row >= col
    diagonal = row == col
    cum_rows, cum_cols = decays(decay_ref, blocks, row, col)
    for c in range(blocks):
        tokens = slice(c * BLOCK, (c + 1) * BLOCK)
        for g in range(key_heads):
            key = key_ref[tokens, g * DK : (g + 1) * DK]
            query = query_ref[tokens, g * DK : (g + 1) * DK]
            key_f, query_f = key.astype(F32), query.astype(F32)
            gram = jnp.where(diagonal, mm_nt(key, key), 0.0)
            unit_row = lax.rsqrt(jnp.sum(gram, axis=0, keepdims=True) + EPS)
            query_unit = query_f * (
                lax.rsqrt(jnp.sum(query_f * query_f, axis=1, keepdims=True) + EPS) * DK ** (-0.5)
            )
            query_scale = lax.rsqrt(
                jnp.sum(query_f * query_f, axis=1, keepdims=True) + EPS
            ) * DK ** (-0.5)
            plain = mm_nt(query, key) * unit_row * query_scale
            for h in range(g * group, (g + 1) * group):
                at = c * heads + h
                cum_row, cum_col = cum_rows[at : at + 1, :], cum_cols[:, at : at + 1]
                fade = jnp.exp(jnp.where(causal, cum_col - cum_row, 0.0))
                scores = jnp.where(causal, plain * fade, 0.0)
                mixed_wu = mm(scores, wu_ref[h, c])
                reach = query_unit * jnp.exp(cum_col) - mixed_wu[:, :DK]
                lanes = slice(h * DV, (h + 1) * DV)
                if c == 0:
                    lin_ref[tokens, lanes] = reach.astype(BF16)
                    own_ref[tokens, lanes] = mixed_wu[:, DK:]
                else:
                    spread = mm(reach, prefix_ref[h, c])
                    lin_ref[tokens, lanes] = spread[:, :DK].astype(BF16)
                    own_ref[tokens, lanes] = mixed_wu[:, DK:] + spread[:, DK:]


def with_map(bias):
    return jnp.concatenate([jnp.zeros((DK, DK), F32), bias.astype(F32)], axis=1)


def scan_kernel(last, later_ref, own_ref, got_ref, before_ref, total_ref, prefix_ref):
    later = later_ref[0] == 1
    for h in range(own_ref.shape[0]):
        own, got, before = own_ref[h], got_ref[h], before_ref[h]
        first = jnp.where(later, got, own)
        second = jnp.where(later, own, got)
        if last:
            total = mm(second[:, :DK], first[:, DK:]) + second[:, DK:].astype(F32)
        else:
            total = mm(second[:, :DK], first) + with_map(second[:, DK:])
        total_ref[h] = total.astype(BF16)
        joined = mm(before[:, :DK], got) + with_map(before[:, DK:])
        prefix_ref[h] = jnp.where(later, joined.astype(BF16), before)


def mix_kernel(spot_ref, gain_ref, gate_ref, lin_ref, own_ref, prefix_ref, got_ref, keep_ref, send_ref):
    core, place, later = spot_ref[0], spot_ref[1], spot_ref[2] == 1
    heads = prefix_ref.shape[0]
    places, rows, _ = keep_ref.shape
    states = []
    for h in range(heads):
        prefix = prefix_ref[h]
        bias = prefix[:, DK:].astype(F32)
        joined = mm(prefix[:, :DK], got_ref[h]) + bias
        states.append(jnp.where(later, joined, bias).astype(BF16))
    for d in range(places):
        at = jnp.bitwise_xor(place, d)
        for out_ref, side in ((send_ref, 1 - core), (keep_ref, core)):
            tokens = pl.ds(pl.multiple_of((2 * at + side) * rows, rows), rows)
            for h in range(heads):
                lanes = slice(h * DV, (h + 1) * DV)
                readout = own_ref[tokens, lanes] + mm(lin_ref[tokens, lanes], states[h])
                scale = lax.rsqrt(jnp.mean(readout * readout, axis=1, keepdims=True) + EPS)
                gate = gate_ref[tokens, lanes].astype(F32)
                gated = gain_ref[...] * gate / (1.0 + jnp.exp(-gate))
                out_ref[d, :, lanes] = (readout * scale * gated).astype(BF16)


def project_kernel(keep_ref, got_ref, own_ref, sib_ref, *out_refs):
    places, rows, depth = keep_ref.shape
    width = out_refs[0].shape[1]
    tile = 512
    for lead in range(0, width, tile):
        lanes = slice(lead, lead + tile)
        product = jnp.dot(
            keep_ref[...].reshape(-1, depth), own_ref[:, lanes], preferred_element_type=F32
        ) + jnp.dot(got_ref[...].reshape(-1, depth), sib_ref[:, lanes], preferred_element_type=F32)
        start = 0
        for lead_ref in range(0, len(out_refs), places):
            part = out_refs[lead_ref].shape[0]
            for d in range(places):
                at = d * rows + start
                out_refs[lead_ref + d][:, lanes] = product[at : at + part].astype(BF16)
            start += part


def project(keep, got, own, sib, sizes):
    places, rows, _ = keep.shape
    outs = resident(
        project_kernel,
        [shape((size, own.shape[1]), BF16) for size in sizes for _ in range(places)],
        keep,
        got,
        own,
        sib,
    )
    return [outs[c * places : (c + 1) * places] for c in range(len(sizes))]


def norm_kernel(start, hidden_ref, gain_ref, routes_ref, *refs):
    *part_refs, residual_ref, out_ref = refs
    rows = residual_ref.shape[0]
    tokens = slice(start, start + rows)
    residual = hidden_ref[tokens, :].astype(F32)
    for part_ref in part_refs:
        residual += part_ref[:, : residual.shape[1]].astype(F32)
    residual_ref[...] = residual
    scale = lax.rsqrt(jnp.mean(residual * residual, axis=1, keepdims=True) + EPS)
    width = residual.shape[1]
    out_ref[:, :width] = (residual * scale * gain_ref[...]).astype(BF16)
    out_ref[:, width:] = routes_ref[tokens, :]


def expert_kernel(places, spot_ref, *refs):
    slots = refs[:places]
    weights = refs[places : places + 6]
    out_refs = refs[places + 6 :]
    place, core = spot_ref[0], spot_ref[1]
    rows, width = out_refs[0].shape
    x = jnp.concatenate([slot[:, :width] for slot in slots], axis=0)
    routes = jnp.concatenate([slot[:, width:] for slot in slots], axis=0).astype(F32)
    lane = lax.broadcasted_iota(jnp.int32, routes.shape, 1)
    inners, shares = [], []
    for number in range(2):
        gate_ref, up_ref = weights[3 * number : 3 * number + 2]
        expert = 2 * place + (core if number == 0 else 1 - core)
        gate_act = jnp.dot(x, gate_ref[0], preferred_element_type=F32)
        up_act = jnp.dot(x, up_ref[0], preferred_element_type=F32)
        inners.append((gate_act / (1.0 + jnp.exp(-gate_act)) * up_act).astype(BF16))
        shares.append(jnp.sum(jnp.where(lane == expert, routes, 0.0), axis=1, keepdims=True))
    tile = 512
    for lead in range(0, width, tile):
        lanes = slice(lead, lead + tile)
        total = jnp.dot(inners[0], weights[2][0, :, lanes], preferred_element_type=F32) * shares[0]
        total += jnp.dot(inners[1], weights[5][0, :, lanes], preferred_element_type=F32) * shares[1]
        for d, out_ref in enumerate(out_refs):
            out_ref[:, lanes] = total[d * rows : (d + 1) * rows].astype(BF16)


def experts(spot, slots, weights):
    rows = slots[0].shape[0]
    width = weights[0].shape[1]
    return resident(
        functools.partial(expert_kernel, len(slots)),
        (shape((rows, width), BF16),) * len(slots),
        *slots,
        *weights,
        scalars=spot,
        flops=3 * 10**9,
    )


def between_places(places, d):
    return [(2 * i + c, 2 * (i ^ d) + c) for i in range(places) for c in range(2)]


def exchange(piece, d):
    return lax.ppermute(piece, "exp", between_places(lax.axis_size("exp") // 2, d))


def reduce_places(chunks, spare=0):
    places = len(chunks[0])
    crossed = [[exchange(pieces[e ^ 1], 1) for e in range(2, places, 2)] for pieces in chunks]
    joined = []
    done = None
    for pieces, cross in zip(chunks, crossed):
        joined.append([])
        for e, got in zip(range(2, places, 2), cross):
            if done is not None:
                got = after(got, done)
            done = (pieces[e].astype(F32) + got.astype(F32)).astype(BF16)
            if len(joined) > 1:
                done = jnp.pad(done, ((0, 0), (0, spare)))
            joined[-1].append(done)
    return [
        [after(pieces[0], done)]
        + [exchange(sent, 2 * i + 2) for i, sent in enumerate(mine)]
        + [exchange(after(pieces[1], mine[-1]), 1)]
        for pieces, mine in zip(chunks, joined)
    ], done


def per_device(
    hidden_in,
    query_proj,
    key_proj,
    value_proj,
    gate_proj,
    log_decay,
    write_rate,
    head_gain,
    out_weight,
    post_gain,
    expert_ids,
    route_weight,
    gate_weight,
    up_weight,
    down_weight,
):
    length = value_proj.shape[0]
    heads = value_proj.shape[1] // DV
    blocks = length // BLOCK
    tok, width = hidden_in.shape
    seqs, exps = lax.axis_size("seq"), lax.axis_size("exp")
    places = exps // 2
    me = lax.axis_index("exp")
    place, core = lax.div(me, 2), lax.rem(me, 2)
    here = lax.axis_index("seq")
    swap = [(i, i ^ 1) for i in range(exps)]

    out_sib = lax.ppermute(out_weight, "exp", swap)
    own = (gate_weight, up_weight, down_weight)
    sib = tuple(lax.ppermute(w, "exp", swap) for w in own)

    wide = shape((heads, blocks, DK, DK + DV), BF16)
    wu, prefixes, total = call(
        state_kernel,
        (wide, wide, shape((heads, DK, DK + DV), BF16)),
        key_proj,
        value_proj,
        log_decay,
        write_rate,
        flops=10**10,
    )
    total, out_sib = lax.optimization_barrier((total, out_sib))
    lin, own_read, routes = call(
        readout_kernel,
        (
            shape((length, heads * DV), BF16),
            shape((length, heads * DV), F32),
            shape((tok, LANES), BF16),
        ),
        query_proj,
        key_proj,
        log_decay,
        expert_ids.T,
        route_weight.T,
        wu,
        prefixes,
        flops=4 * 10**9,
        vmem=SMALL_VMEM,
        stay=True,
    )

    start = jnp.concatenate([jnp.eye(DK, dtype=BF16), jnp.zeros((DK, DV), BF16)], axis=1)
    before = jnp.broadcast_to(start, total.shape)
    summed, step = total, 1
    while True:
        later = lax.rem(lax.div(here, step), 2)
        got = lax.ppermute(summed, "seq", [(i, i ^ step) for i in range(seqs)])
        if 2 * step >= seqs:
            break
        last = 4 * step >= seqs
        summed, before = resident(
            functools.partial(scan_kernel, last),
            (shape((heads, DK, DV if last else DK + DV), BF16), shape(total.shape, BF16)),
            summed,
            after(got, lin) if step == 1 else got,
            before,
            scalars=later.reshape(1),
        )
        step *= 2
    fetched = fetch(gate_proj, out_weight, out_sib)
    got, before, fetched, sib = lax.optimization_barrier((got, before, fetched, sib))
    gate_here, out_own, out_sib = fetched

    half = shape((places, tok, heads * DV), BF16)
    keep, send = resident(
        mix_kernel,
        (half, half),
        head_gain.reshape(1, DV),
        gate_here,
        lin,
        own_read,
        before,
        got,
        scalars=jnp.stack([core, place, later]),
        flops=10**9,
    )
    got = lax.ppermute(send, "exp", swap)
    spot = jnp.stack([place, core])
    sizes = SIZES if sum(SIZES) == tok else (tok // 2, tok // 2)
    starts = [sum(sizes[:i]) for i in range(len(sizes))]
    chunks, joined = reduce_places(project(keep, got, out_own, out_sib, sizes), SPARE)
    sib = fetch(*(after(w, joined) for w in sib))
    chunks[0][0] = after(chunks[0][0], *sib)
    residuals, slots = [], []
    for chunk, summands in enumerate(chunks):
        if slots:
            summands[0] = after(summands[0], *slots[-1][1:3])
        kept, sent = resident(
            functools.partial(norm_kernel, starts[chunk]),
            (shape((sizes[chunk], width), F32), shape((sizes[chunk], width + LANES), BF16)),
            hidden_in,
            post_gain.reshape(1, width),
            routes,
            *summands,
        )
        residuals.append(kept)
        slot = [sent] + [None] * (places - 1)
        for e in range(2, places, 2):
            slot[e] = exchange(sent, e)
        slot[1] = exchange(sent, 1)
        slots.append(slot)
    for slot in slots:
        for e in range(2, places, 2):
            slot[e + 1] = exchange(after(slot[e], slots[-1][0]), 1)
    made = []
    for slot in slots:
        if made:
            slot[0] = after(slot[0], made[-1][0])
        made.append(experts(spot, slot, (*own, *sib)))
    chunks, _ = reduce_places(made)
    return jnp.concatenate(
        [
            sum((s.astype(F32) for s in summands), kept).astype(BF16)
            for kept, summands in zip(residuals, chunks)
        ],
        axis=0,
    )


def solution(mesh):
    in_specs = (
        P(("seq", "exp"), None),
        P("seq", "exp"),
        P("seq", "exp"),
        P("seq", "exp"),
        P("seq", "exp"),
        P("exp", "seq"),
        P("exp", "seq"),
        P(),
        P("exp", None),
        P(),
        P(("seq", "exp"), None),
        P(("seq", "exp"), None),
        P("exp", None, None),
        P("exp", None, None),
        P("exp", None, None),
    )
    out_specs = P(("seq", "exp"), None)
    return jax.shard_map(
        per_device, mesh=mesh, in_specs=in_specs, out_specs=out_specs, check_vma=False
    )
```

```python
import functools

import jax
import jax.numpy as jnp
from jax import lax
from jax.experimental import pallas as pl
from jax.experimental.pallas import tpu as pltpu
from jax.sharding import PartitionSpec as P

DK = 128
DV = 128
EPS = 1e-06
BLOCK = 128
LANES = 128
F32 = jnp.float32
BF16 = jnp.bfloat16
LARGE_VMEM = 60 * 1024 * 1024
SMALL_VMEM = 24 * 1024 * 1024
FETCH_VMEM = 24 * 1024 * 1024
SIZES = (32, 32)
SPARE = 256
PAIRS_AT_ONCE = 16


def whole(memory_space=pltpu.VMEM):
    return pl.BlockSpec(memory_space=memory_space)


def blocks_of(*arrays):
    return [pl.BlockSpec(a.shape, lambda i, n=a.ndim: (0,) * n) for a in arrays]


def fetch_kernel(*refs):
    count = len(refs) // 2
    copies = [
        pltpu.make_async_copy(refs[i], refs[count + i], refs[-1].at[i]) for i in range(count)
    ]
    for copy in copies:
        copy.start()
    for copy in copies:
        copy.wait()


def fetch(*arrays):
    return pl.pallas_call(
        fetch_kernel,
        out_shape=tuple(shape(a.shape, a.dtype) for a in arrays),
        in_specs=[whole(pl.ANY)] * len(arrays),
        out_specs=(whole(),) * len(arrays),
        scratch_shapes=[pltpu.SemaphoreType.DMA((len(arrays),))],
        compiler_params=pltpu.CompilerParams(vmem_limit_bytes=FETCH_VMEM),
        cost_estimate=pl.CostEstimate(
            flops=0, bytes_accessed=2 * sum(a.size * a.dtype.itemsize for a in arrays), transcendentals=0
        ),
    )(*arrays)


def resident(kernel, outs, *arrays, scalars=None, flops=0, scratch=()):
    moved = sum(a.size * a.dtype.itemsize for a in (*arrays, *outs))
    return pl.pallas_call(
        kernel,
        out_shape=tuple(outs),
        in_specs=([] if scalars is None else [whole(pltpu.SMEM)]) + [whole()] * len(arrays),
        out_specs=(whole(),) * len(outs),
        scratch_shapes=list(scratch),
        compiler_params=pltpu.CompilerParams(vmem_limit_bytes=SMALL_VMEM),
        cost_estimate=pl.CostEstimate(flops=flops, bytes_accessed=moved, transcendentals=0),
    )(*(() if scalars is None else (scalars,)), *arrays)


def after(value, *others):
    return lax.optimization_barrier((value, *others))[0]


def call(kernel, outs, *arrays, scalars=None, flops=0, vmem=LARGE_VMEM, scratch=(), stay=False):
    params = pltpu.CompilerParams(vmem_limit_bytes=vmem)
    moved = sum(a.size * a.dtype.itemsize for a in (*arrays, *outs))
    return pl.pallas_call(
        kernel,
        grid=(1,),
        out_shape=tuple(outs),
        in_specs=([] if scalars is None else [whole(pltpu.SMEM)]) + blocks_of(*arrays),
        out_specs=(whole(),) * len(outs) if stay else tuple(blocks_of(*outs)),
        scratch_shapes=list(scratch),
        compiler_params=params,
        cost_estimate=pl.CostEstimate(flops=flops, bytes_accessed=moved, transcendentals=0),
    )(*(() if scalars is None else (scalars,)), *arrays)


def shape(dims, dtype):
    return jax.ShapeDtypeStruct(dims, dtype)


def mm(a, b):
    return jnp.dot(a.astype(BF16), b.astype(BF16), preferred_element_type=F32)


def mm_nt(a, b):
    return lax.dot_general(
        a, b, (((1,), (1,)), ((), ())), preferred_element_type=F32
    )


def split(a):
    high = a.astype(BF16)
    return high, (a - high.astype(F32)).astype(BF16)


def mm_left2(a, b):
    high, low = split(a)
    return jnp.dot(
        jnp.concatenate([high, low], axis=1),
        jnp.concatenate([b, b], axis=0),
        preferred_element_type=F32,
    )


def mm_both2(a, b):
    a_high, a_low = split(a)
    b_high, b_low = split(b)
    return jnp.dot(
        jnp.concatenate([a_high, a_low, a_high], axis=1),
        jnp.concatenate([b_high, b_high, b_low], axis=0),
        preferred_element_type=F32,
    )


def grids():
    row = lax.broadcasted_iota(jnp.int32, (BLOCK, BLOCK), 0)
    col = lax.broadcasted_iota(jnp.int32, (BLOCK, BLOCK), 1)
    return row, col


def stacked(ref, blocks):
    return jnp.concatenate([ref[:, c * BLOCK : (c + 1) * BLOCK] for c in range(blocks)], axis=0)


def thirds(matrix):
    parts = []
    for _ in range(3):
        parts.append(matrix.astype(BF16))
        matrix = matrix - parts[-1].astype(F32)
    return jnp.concatenate(parts, axis=0)


def turned(mask, matrix):
    rows = matrix.shape[0]
    product = mm_nt(mask, thirds(matrix))
    return product[:, :rows] + product[:, rows : 2 * rows] + product[:, 2 * rows :]


def decays(decay_ref, blocks, row, col):
    by_row = stacked(decay_ref, blocks)
    upto = jnp.where(row >= col, 1.0, 0.0).astype(BF16)
    rows = by_row.shape[0]
    product = mm_nt(thirds(by_row), upto)
    cum_rows = product[:rows] + product[rows : 2 * rows] + product[2 * rows :]
    return cum_rows, turned(upto, by_row)


def state_kernel(key_ref, value_ref, decay_ref, rate_ref, wu_ref, prefix_ref, total_ref):
    heads = decay_ref.shape[0]
    key_heads = key_ref.shape[1] // DK
    group = heads // key_heads
    blocks = key_ref.shape[0] // BLOCK
    row, col = grids()
    gap_bits = jnp.bitwise_xor(row, col)
    strict = row > col
    diagonal = row == col
    eye = jnp.where(diagonal, 1.0, 0.0).astype(F32)
    cum_rows, cum_cols = decays(decay_ref, blocks, row, col)
    rate_rows = stacked(rate_ref, blocks)
    rate_cols = turned(eye.astype(BF16), rate_rows)
    carried = [None] * heads
    pairs = [(c, h) for c in range(blocks) for h in range(heads)]
    unit_rows, unit_cols, keys, keys_t, grams = {}, {}, {}, {}, {}
    for c in range(blocks):
        tokens = slice(c * BLOCK, (c + 1) * BLOCK)
        for g in range(key_heads):
            key = key_ref[tokens, g * DK : (g + 1) * DK]
            gram = mm_nt(key, key)
            on_diagonal = jnp.where(diagonal, gram, 0.0)
            unit_rows[c, g] = lax.rsqrt(jnp.sum(on_diagonal, axis=0, keepdims=True) + EPS)
            unit_cols[c, g] = lax.rsqrt(jnp.sum(on_diagonal, axis=1, keepdims=True) + EPS)
            keys[c, g] = key
            keys_t[c, g] = key.astype(F32).T.astype(BF16)
            grams[c, g] = gram * unit_rows[c, g] * unit_cols[c, g]
    for lead in range(0, len(pairs), PAIRS_AT_ONCE):
        some = pairs[lead : lead + PAIRS_AT_ONCE]
        lower, solve = {}, {}
        for c, h in some:
            at = c * heads + h
            cum_row, cum_col = cum_rows[at : at + 1, :], cum_cols[:, at : at + 1]
            fade = jnp.exp(jnp.where(strict, cum_col - cum_row, 0.0))
            part = jnp.where(strict, grams[c, h // group] * fade * rate_cols[:, at : at + 1], 0.0)
            lower[c, h] = part
            solve[c, h] = eye - jnp.where(gap_bits == 1, part, 0.0)
        size = 2
        while size < BLOCK:
            shift = size.bit_length() - 1
            inside = lax.shift_right_logical(gap_bits, shift) == 1
            right = {p: mm(jnp.where(inside, lower[p], 0.0), solve[p]) for p in some}
            solve = {p: solve[p] - mm(solve[p], right[p]) for p in some}
            size *= 2
        first = {p: solve[p].astype(BF16) for p in some}
        rest = {p: eye - first[p].astype(F32) - mm_left2(lower[p], first[p]) for p in some}
        solve = {p: first[p].astype(F32) + mm(first[p], rest[p]) for p in some}
        tails = {}
        for c, h in some:
            tokens = slice(c * BLOCK, (c + 1) * BLOCK)
            at = c * heads + h
            g = h // group
            cum_row, cum_col = cum_rows[at : at + 1, :], cum_cols[:, at : at + 1]
            rate_row = rate_rows[at : at + 1, :]
            end = cum_row[:, BLOCK - 1 :]
            w = mm(solve[c, h] * (rate_row * jnp.exp(cum_row) * unit_rows[c, g]), keys[c, g])
            u = mm(solve[c, h] * rate_row, value_ref[tokens, h * DV : (h + 1) * DV])
            wu = jnp.concatenate([w, u], axis=1)
            wu_ref[h, c] = wu.astype(BF16)
            tails[c, h] = mm(keys_t[c, g], wu * (jnp.exp(end - cum_col) * unit_cols[c, g]))
        for c, h in some:
            at = c * heads + h
            kept = jnp.exp(cum_rows[at : at + 1, BLOCK - 1 :])
            tail = tails[c, h]
            if c == 0:
                start = jnp.concatenate([eye, jnp.zeros((DK, DV), F32)], axis=1)
                prefix_ref[h, c] = start.astype(BF16)
                carried[h] = jnp.concatenate([kept * eye - tail[:, :DK], tail[:, DK:]], axis=1)
            else:
                bias = jnp.concatenate([jnp.zeros((DK, DK), F32), tail[:, DK:]], axis=1)
                prefix_ref[h, c] = carried[h].astype(BF16)
                carried[h] = kept * carried[h] + bias - mm_both2(tail[:, :DK], carried[h])
    for h in range(heads):
        total_ref[h] = carried[h].astype(BF16)


def readout_kernel(query_ref, key_ref, decay_ref, ids_ref, weight_ref, wu_ref, prefix_ref,
                   lin_ref, own_ref, routes_ref):
    expert = lax.broadcasted_iota(jnp.int32, (LANES, ids_ref.shape[1]), 0)
    routes = jnp.zeros(expert.shape, F32)
    for k in range(ids_ref.shape[0]):
        routes += jnp.where(
            ids_ref[k : k + 1, :] == expert, weight_ref[k : k + 1, :].astype(F32), 0.0
        )
    routes_ref[...] = routes.T.astype(BF16)
    heads = decay_ref.shape[0]
    key_heads = key_ref.shape[1] // DK
    group = heads // key_heads
    blocks = key_ref.shape[0] // BLOCK
    row, col = grids()
    causal = row >= col
    diagonal = row == col
    cum_rows, cum_cols = decays(decay_ref, blocks, row, col)
    for c in range(blocks):
        tokens = slice(c * BLOCK, (c + 1) * BLOCK)
        for g in range(key_heads):
            key = key_ref[tokens, g * DK : (g + 1) * DK]
            query = query_ref[tokens, g * DK : (g + 1) * DK]
            key_f, query_f = key.astype(F32), query.astype(F32)
            gram = jnp.where(diagonal, mm_nt(key, key), 0.0)
            unit_row = lax.rsqrt(jnp.sum(gram, axis=0, keepdims=True) + EPS)
            query_unit = query_f * (
                lax.rsqrt(jnp.sum(query_f * query_f, axis=1, keepdims=True) + EPS) * DK ** (-0.5)
            )
            query_scale = lax.rsqrt(
                jnp.sum(query_f * query_f, axis=1, keepdims=True) + EPS
            ) * DK ** (-0.5)
            plain = mm_nt(query, key) * unit_row * query_scale
            for h in range(g * group, (g + 1) * group):
                at = c * heads + h
                cum_row, cum_col = cum_rows[at : at + 1, :], cum_cols[:, at : at + 1]
                fade = jnp.exp(jnp.where(causal, cum_col - cum_row, 0.0))
                scores = jnp.where(causal, plain * fade, 0.0)
                mixed_wu = mm(scores, wu_ref[h, c])
                reach = query_unit * jnp.exp(cum_col) - mixed_wu[:, :DK]
                lanes = slice(h * DV, (h + 1) * DV)
                if c == 0:
                    lin_ref[tokens, lanes] = reach.astype(BF16)
                    own_ref[tokens, lanes] = mixed_wu[:, DK:]
                else:
                    spread = mm(reach, prefix_ref[h, c])
                    lin_ref[tokens, lanes] = spread[:, :DK].astype(BF16)
                    own_ref[tokens, lanes] = mixed_wu[:, DK:] + spread[:, DK:]


def with_map(bias):
    return jnp.concatenate([jnp.zeros((DK, DK), F32), bias.astype(F32)], axis=1)


def scan_kernel(last, later_ref, own_ref, got_ref, before_ref, total_ref, prefix_ref):
    later = later_ref[0] == 1
    for h in range(own_ref.shape[0]):
        own, got, before = own_ref[h], got_ref[h], before_ref[h]
        first = jnp.where(later, got, own)
        second = jnp.where(later, own, got)
        if last:
            total = mm(second[:, :DK], first[:, DK:]) + second[:, DK:].astype(F32)
        else:
            total = mm(second[:, :DK], first) + with_map(second[:, DK:])
        total_ref[h] = total.astype(BF16)
        joined = mm(before[:, :DK], got) + with_map(before[:, DK:])
        prefix_ref[h] = jnp.where(later, joined.astype(BF16), before)


def mixed_rows(tokens, states, gain_ref, gate_ref, lin_ref, own_ref):
    parts = []
    for h, state in enumerate(states):
        lanes = slice(h * DV, (h + 1) * DV)
        readout = own_ref[tokens, lanes] + mm(lin_ref[tokens, lanes], state)
        scale = lax.rsqrt(jnp.mean(readout * readout, axis=1, keepdims=True) + EPS)
        gate = gate_ref[tokens, lanes].astype(F32)
        gated = gain_ref[...] * gate / (1.0 + jnp.exp(-gate))
        parts.append((readout * scale * gated).astype(BF16))
    return jnp.concatenate(parts, axis=1)


def rows_of(place, side, d, rows):
    at = 2 * jnp.bitwise_xor(place, d) + side
    return pl.ds(pl.multiple_of(at * rows, rows), rows)


def send_kernel(spot_ref, gain_ref, gate_ref, lin_ref, own_ref, prefix_ref, got_ref, state_ref, send_ref):
    core, place, later = spot_ref[0], spot_ref[1], spot_ref[2] == 1
    places, rows, _ = send_ref.shape
    states = []
    for h in range(prefix_ref.shape[0]):
        prefix = prefix_ref[h]
        bias = prefix[:, DK:].astype(F32)
        joined = mm(prefix[:, :DK], got_ref[h]) + bias
        states.append(jnp.where(later, joined, bias).astype(BF16))
        state_ref[h] = states[h]
    for d in range(places):
        tokens = rows_of(place, 1 - core, d, rows)
        send_ref[d] = mixed_rows(tokens, states, gain_ref, gate_ref, lin_ref, own_ref)


def keep_kernel(spot_ref, gain_ref, gate_ref, lin_ref, own_ref, state_ref, keep_ref):
    core, place = spot_ref[0], spot_ref[1]
    states = [state_ref[h] for h in range(state_ref.shape[0])]
    places, rows, _ = keep_ref.shape
    for d in range(places):
        tokens = rows_of(place, core, d, rows)
        keep_ref[d] = mixed_rows(tokens, states, gain_ref, gate_ref, lin_ref, own_ref)


def project_kernel(start, keep_ref, got_ref, own_ref, sib_ref, *out_refs):
    places, rows, depth = keep_ref.shape
    part, width = out_refs[0].shape
    keep, got = (
        jnp.concatenate([ref[d, start : start + part] for d in range(places)], axis=0)
        for ref in (keep_ref, got_ref)
    )
    tile = 512
    for lead in range(0, width, tile):
        lanes = slice(lead, lead + tile)
        product = jnp.dot(keep, own_ref[:, lanes], preferred_element_type=F32) + jnp.dot(
            got, sib_ref[:, lanes], preferred_element_type=F32
        )
        for d, out_ref in enumerate(out_refs):
            out_ref[:, lanes] = product[d * part : (d + 1) * part].astype(BF16)


def project(keep, got, own, sib, sizes):
    places = keep.shape[0]
    chunks = []
    for number, size in enumerate(sizes):
        chunks.append(
            resident(
                functools.partial(project_kernel, sum(sizes[:number])),
                (shape((size, own.shape[1]), BF16),) * places,
                keep,
                after(got, chunks[-1][0]) if chunks else got,
                own,
                sib,
                flops=5 * 10**8,
            )
        )
    return chunks


def norm_kernel(start, hidden_ref, gain_ref, routes_ref, *refs):
    *part_refs, residual_ref, out_ref = refs
    rows = residual_ref.shape[0]
    tokens = slice(start, start + rows)
    residual = hidden_ref[tokens, :].astype(F32)
    for part_ref in part_refs:
        residual += part_ref[:, : residual.shape[1]].astype(F32)
    residual_ref[...] = residual
    scale = lax.rsqrt(jnp.mean(residual * residual, axis=1, keepdims=True) + EPS)
    width = residual.shape[1]
    out_ref[:, :width] = (residual * scale * gain_ref[...]).astype(BF16)
    out_ref[:, width:] = routes_ref[tokens, :]


def expert_kernel(places, spot_ref, *refs):
    slots = refs[:places]
    weights = refs[places : places + 6]
    out_refs = refs[places + 6 :]
    place, core = spot_ref[0], spot_ref[1]
    rows, width = out_refs[0].shape
    x = jnp.concatenate([slot[:, :width] for slot in slots], axis=0)
    routes = jnp.concatenate([slot[:, width:] for slot in slots], axis=0).astype(F32)
    lane = lax.broadcasted_iota(jnp.int32, routes.shape, 1)
    inners, shares = [], []
    for number in range(2):
        gate_ref, up_ref = weights[3 * number : 3 * number + 2]
        expert = 2 * place + (core if number == 0 else 1 - core)
        gate_act = jnp.dot(x, gate_ref[0], preferred_element_type=F32)
        up_act = jnp.dot(x, up_ref[0], preferred_element_type=F32)
        inners.append((gate_act / (1.0 + jnp.exp(-gate_act)) * up_act).astype(BF16))
        shares.append(jnp.sum(jnp.where(lane == expert, routes, 0.0), axis=1, keepdims=True))
    tile = 512
    for lead in range(0, width, tile):
        lanes = slice(lead, lead + tile)
        total = jnp.dot(inners[0], weights[2][0, :, lanes], preferred_element_type=F32) * shares[0]
        total += jnp.dot(inners[1], weights[5][0, :, lanes], preferred_element_type=F32) * shares[1]
        for d, out_ref in enumerate(out_refs):
            out_ref[:, lanes] = total[d * rows : (d + 1) * rows].astype(BF16)


def experts(spot, slots, weights):
    rows = slots[0].shape[0]
    width = weights[0].shape[1]
    return resident(
        functools.partial(expert_kernel, len(slots)),
        (shape((rows, width), BF16),) * len(slots),
        *slots,
        *weights,
        scalars=spot,
        flops=3 * 10**9,
    )


def between_places(places, d):
    return [(2 * i + c, 2 * (i ^ d) + c) for i in range(places) for c in range(2)]


def exchange(piece, d):
    return lax.ppermute(piece, "exp", between_places(lax.axis_size("exp") // 2, d))


def reduce_places(chunks, spare=0):
    places = len(chunks[0])
    crossed = [[exchange(pieces[e ^ 1], 1) for e in range(2, places, 2)] for pieces in chunks]
    joined = []
    done = None
    for pieces, cross in zip(chunks, crossed):
        joined.append([])
        for e, got in zip(range(2, places, 2), cross):
            if done is not None:
                got = after(got, done)
            done = (pieces[e].astype(F32) + got.astype(F32)).astype(BF16)
            if len(joined) > 1:
                done = jnp.pad(done, ((0, 0), (0, spare)))
            joined[-1].append(done)
    return [
        [after(pieces[0], done)]
        + [exchange(sent, 2 * i + 2) for i, sent in enumerate(mine)]
        + [exchange(after(pieces[1], mine[-1]), 1)]
        for pieces, mine in zip(chunks, joined)
    ], done


def per_device(
    hidden_in,
    query_proj,
    key_proj,
    value_proj,
    gate_proj,
    log_decay,
    write_rate,
    head_gain,
    out_weight,
    post_gain,
    expert_ids,
    route_weight,
    gate_weight,
    up_weight,
    down_weight,
):
    length = value_proj.shape[0]
    heads = value_proj.shape[1] // DV
    blocks = length // BLOCK
    tok, width = hidden_in.shape
    seqs, exps = lax.axis_size("seq"), lax.axis_size("exp")
    places = exps // 2
    me = lax.axis_index("exp")
    place, core = lax.div(me, 2), lax.rem(me, 2)
    here = lax.axis_index("seq")
    swap = [(i, i ^ 1) for i in range(exps)]

    out_sib = lax.ppermute(out_weight, "exp", swap)
    own = (gate_weight, up_weight, down_weight)
    sib = tuple(lax.ppermute(w, "exp", swap) for w in own)

    wide = shape((heads, blocks, DK, DK + DV), BF16)
    wu, prefixes, total = call(
        state_kernel,
        (wide, wide, shape((heads, DK, DK + DV), BF16)),
        key_proj,
        value_proj,
        log_decay,
        write_rate,
        flops=10**10,
    )
    total, out_sib = lax.optimization_barrier((total, out_sib))
    lin, own_read, routes = call(
        readout_kernel,
        (
            shape((length, heads * DV), BF16),
            shape((length, heads * DV), F32),
            shape((tok, LANES), BF16),
        ),
        query_proj,
        key_proj,
        log_decay,
        expert_ids.T,
        route_weight.T,
        wu,
        prefixes,
        flops=4 * 10**9,
        vmem=SMALL_VMEM,
        stay=True,
    )

    start = jnp.concatenate([jnp.eye(DK, dtype=BF16), jnp.zeros((DK, DV), BF16)], axis=1)
    before = jnp.broadcast_to(start, total.shape)
    summed, step = total, 1
    while True:
        later = lax.rem(lax.div(here, step), 2)
        got = lax.ppermute(summed, "seq", [(i, i ^ step) for i in range(seqs)])
        if 2 * step >= seqs:
            break
        last = 4 * step >= seqs
        summed, before = resident(
            functools.partial(scan_kernel, last),
            (shape((heads, DK, DV if last else DK + DV), BF16), shape(total.shape, BF16)),
            summed,
            after(got, lin) if step == 1 else got,
            before,
            scalars=later.reshape(1),
        )
        step *= 2
    fetched = fetch(gate_proj, out_weight, out_sib)
    got, before, fetched, sib = lax.optimization_barrier((got, before, fetched, sib))
    gate_here, out_own, out_sib = fetched

    half = shape((places, tok, heads * DV), BF16)
    where = jnp.stack([core, place, later])
    readout_parts = (head_gain.reshape(1, DV), gate_here, lin, own_read)
    state, send = resident(
        send_kernel,
        (shape((heads, DK, DV), BF16), half),
        *readout_parts,
        before,
        got,
        scalars=where,
        flops=10**9,
    )
    got = lax.ppermute(send, "exp", swap)
    (keep,) = resident(
        keep_kernel,
        (half,),
        *readout_parts,
        state,
        scalars=where,
        flops=10**9,
    )
    spot = jnp.stack([place, core])
    sizes = SIZES if sum(SIZES) == tok else (tok // 2, tok // 2)
    starts = [sum(sizes[:i]) for i in range(len(sizes))]
    chunks, joined = reduce_places(project(keep, got, out_own, out_sib, sizes), SPARE)
    sib = fetch(*(after(w, joined) for w in sib))
    chunks[0][0] = after(chunks[0][0], *sib)
    residuals, slots = [], []
    for chunk, summands in enumerate(chunks):
        if slots:
            summands[0] = after(summands[0], *slots[-1][1:3])
        kept, sent = resident(
            functools.partial(norm_kernel, starts[chunk]),
            (shape((sizes[chunk], width), F32), shape((sizes[chunk], width + LANES), BF16)),
            hidden_in,
            post_gain.reshape(1, width),
            routes,
            *summands,
        )
        residuals.append(kept)
        slot = [sent] + [None] * (places - 1)
        for e in range(2, places, 2):
            slot[e] = exchange(sent, e)
        slot[1] = exchange(sent, 1)
        slots.append(slot)
    for slot in slots:
        for e in range(2, places, 2):
            slot[e + 1] = exchange(after(slot[e], slots[-1][0]), 1)
    made = []
    for slot in slots:
        if made:
            slot[0] = after(slot[0], made[-1][0])
        made.append(experts(spot, slot, (*own, *sib)))
    chunks, _ = reduce_places(made)
    return jnp.concatenate(
        [
            sum((s.astype(F32) for s in summands), kept).astype(BF16)
            for kept, summands in zip(residuals, chunks)
        ],
        axis=0,
    )


def solution(mesh):
    in_specs = (
        P(("seq", "exp"), None),
        P("seq", "exp"),
        P("seq", "exp"),
        P("seq", "exp"),
        P("seq", "exp"),
        P("exp", "seq"),
        P("exp", "seq"),
        P(),
        P("exp", None),
        P(),
        P(("seq", "exp"), None),
        P(("seq", "exp"), None),
        P("exp", None, None),
        P("exp", None, None),
        P("exp", None, None),
    )
    out_specs = P(("seq", "exp"), None)
    return jax.shard_map(
        per_device, mesh=mesh, in_specs=in_specs, out_specs=out_specs, check_vma=False
    )
```

```python
import functools

import jax
import jax.numpy as jnp
from jax import lax
from jax.experimental import pallas as pl
from jax.experimental.pallas import tpu as pltpu
from jax.sharding import PartitionSpec as P

DK = 128
DV = 128
EPS = 1e-06
BLOCK = 128
LANES = 128
F32 = jnp.float32
BF16 = jnp.bfloat16
LARGE_VMEM = 60 * 1024 * 1024
SMALL_VMEM = 24 * 1024 * 1024
FETCH_VMEM = 24 * 1024 * 1024
SIZES = (32, 32)
SPARE = 256
PAIRS_AT_ONCE = 16


def whole(memory_space=pltpu.VMEM):
    return pl.BlockSpec(memory_space=memory_space)


def blocks_of(*arrays):
    return [pl.BlockSpec(a.shape, lambda i, n=a.ndim: (0,) * n) for a in arrays]


def fetch_kernel(*refs):
    count = len(refs) // 2
    copies = [
        pltpu.make_async_copy(refs[i], refs[count + i], refs[-1].at[i]) for i in range(count)
    ]
    for copy in copies:
        copy.start()
    for copy in copies:
        copy.wait()


def fetch(*arrays):
    return pl.pallas_call(
        fetch_kernel,
        out_shape=tuple(shape(a.shape, a.dtype) for a in arrays),
        in_specs=[whole(pl.ANY)] * len(arrays),
        out_specs=(whole(),) * len(arrays),
        scratch_shapes=[pltpu.SemaphoreType.DMA((len(arrays),))],
        compiler_params=pltpu.CompilerParams(vmem_limit_bytes=FETCH_VMEM),
        cost_estimate=pl.CostEstimate(
            flops=0, bytes_accessed=2 * sum(a.size * a.dtype.itemsize for a in arrays), transcendentals=0
        ),
    )(*arrays)


def resident(kernel, outs, *arrays, scalars=None, flops=0, scratch=()):
    moved = sum(a.size * a.dtype.itemsize for a in (*arrays, *outs))
    return pl.pallas_call(
        kernel,
        out_shape=tuple(outs),
        in_specs=([] if scalars is None else [whole(pltpu.SMEM)]) + [whole()] * len(arrays),
        out_specs=(whole(),) * len(outs),
        scratch_shapes=list(scratch),
        compiler_params=pltpu.CompilerParams(vmem_limit_bytes=SMALL_VMEM),
        cost_estimate=pl.CostEstimate(flops=flops, bytes_accessed=moved, transcendentals=0),
    )(*(() if scalars is None else (scalars,)), *arrays)


def after(value, *others):
    return lax.optimization_barrier((value, *others))[0]


def call(kernel, outs, *arrays, scalars=None, flops=0, vmem=LARGE_VMEM, scratch=(), stay=False):
    params = pltpu.CompilerParams(vmem_limit_bytes=vmem)
    moved = sum(a.size * a.dtype.itemsize for a in (*arrays, *outs))
    return pl.pallas_call(
        kernel,
        grid=(1,),
        out_shape=tuple(outs),
        in_specs=([] if scalars is None else [whole(pltpu.SMEM)]) + blocks_of(*arrays),
        out_specs=(whole(),) * len(outs) if stay else tuple(blocks_of(*outs)),
        scratch_shapes=list(scratch),
        compiler_params=params,
        cost_estimate=pl.CostEstimate(flops=flops, bytes_accessed=moved, transcendentals=0),
    )(*(() if scalars is None else (scalars,)), *arrays)


def shape(dims, dtype):
    return jax.ShapeDtypeStruct(dims, dtype)


def mm(a, b):
    return jnp.dot(a.astype(BF16), b.astype(BF16), preferred_element_type=F32)


def mm_nt(a, b):
    return lax.dot_general(
        a, b, (((1,), (1,)), ((), ())), preferred_element_type=F32
    )


def split(a):
    high = a.astype(BF16)
    return high, (a - high.astype(F32)).astype(BF16)


def mm_left2(a, b):
    high, low = split(a)
    return jnp.dot(
        jnp.concatenate([high, low], axis=1),
        jnp.concatenate([b, b], axis=0),
        preferred_element_type=F32,
    )


def mm_both2(a, b):
    a_high, a_low = split(a)
    b_high, b_low = split(b)
    return jnp.dot(
        jnp.concatenate([a_high, a_low, a_high], axis=1),
        jnp.concatenate([b_high, b_high, b_low], axis=0),
        preferred_element_type=F32,
    )


def grids():
    row = lax.broadcasted_iota(jnp.int32, (BLOCK, BLOCK), 0)
    col = lax.broadcasted_iota(jnp.int32, (BLOCK, BLOCK), 1)
    return row, col


def stacked(ref, blocks):
    return jnp.concatenate([ref[:, c * BLOCK : (c + 1) * BLOCK] for c in range(blocks)], axis=0)


def thirds(matrix):
    parts = []
    for _ in range(3):
        parts.append(matrix.astype(BF16))
        matrix = matrix - parts[-1].astype(F32)
    return jnp.concatenate(parts, axis=0)


def turned(mask, matrix):
    rows = matrix.shape[0]
    product = mm_nt(mask, thirds(matrix))
    return product[:, :rows] + product[:, rows : 2 * rows] + product[:, 2 * rows :]


def decays(decay_ref, blocks, row, col):
    by_row = stacked(decay_ref, blocks)
    upto = jnp.where(row >= col, 1.0, 0.0).astype(BF16)
    rows = by_row.shape[0]
    product = mm_nt(thirds(by_row), upto)
    cum_rows = product[:rows] + product[rows : 2 * rows] + product[2 * rows :]
    return cum_rows, turned(upto, by_row)


def state_kernel(key_ref, value_ref, decay_ref, rate_ref, wu_ref, prefix_ref, total_ref):
    heads = decay_ref.shape[0]
    key_heads = key_ref.shape[1] // DK
    group = heads // key_heads
    blocks = key_ref.shape[0] // BLOCK
    row, col = grids()
    gap_bits = jnp.bitwise_xor(row, col)
    strict = row > col
    diagonal = row == col
    eye = jnp.where(diagonal, 1.0, 0.0).astype(F32)
    cum_rows, cum_cols = decays(decay_ref, blocks, row, col)
    rate_rows = stacked(rate_ref, blocks)
    rate_cols = turned(eye.astype(BF16), rate_rows)
    carried = [None] * heads
    pairs = [(c, h) for c in range(blocks) for h in range(heads)]
    unit_rows, unit_cols, keys, keys_t, grams = {}, {}, {}, {}, {}
    for c in range(blocks):
        tokens = slice(c * BLOCK, (c + 1) * BLOCK)
        for g in range(key_heads):
            key = key_ref[tokens, g * DK : (g + 1) * DK]
            gram = mm_nt(key, key)
            on_diagonal = jnp.where(diagonal, gram, 0.0)
            unit_rows[c, g] = lax.rsqrt(jnp.sum(on_diagonal, axis=0, keepdims=True) + EPS)
            unit_cols[c, g] = lax.rsqrt(jnp.sum(on_diagonal, axis=1, keepdims=True) + EPS)
            keys[c, g] = key
            keys_t[c, g] = key.astype(F32).T.astype(BF16)
            grams[c, g] = gram * unit_rows[c, g] * unit_cols[c, g]
    for lead in range(0, len(pairs), PAIRS_AT_ONCE):
        some = pairs[lead : lead + PAIRS_AT_ONCE]
        lower, solve = {}, {}
        for c, h in some:
            at = c * heads + h
            cum_row, cum_col = cum_rows[at : at + 1, :], cum_cols[:, at : at + 1]
            fade = jnp.exp(jnp.where(strict, cum_col - cum_row, 0.0))
            part = jnp.where(strict, grams[c, h // group] * fade * rate_cols[:, at : at + 1], 0.0)
            lower[c, h] = part
            solve[c, h] = eye - jnp.where(gap_bits == 1, part, 0.0)
        size = 2
        while size < BLOCK:
            shift = size.bit_length() - 1
            inside = lax.shift_right_logical(gap_bits, shift) == 1
            right = {p: mm(jnp.where(inside, lower[p], 0.0), solve[p]) for p in some}
            solve = {p: solve[p] - mm(solve[p], right[p]) for p in some}
            size *= 2
        first = {p: solve[p].astype(BF16) for p in some}
        rest = {p: eye - first[p].astype(F32) - mm_left2(lower[p], first[p]) for p in some}
        solve = {p: first[p].astype(F32) + mm(first[p], rest[p]) for p in some}
        tails = {}
        for c, h in some:
            tokens = slice(c * BLOCK, (c + 1) * BLOCK)
            at = c * heads + h
            g = h // group
            cum_row, cum_col = cum_rows[at : at + 1, :], cum_cols[:, at : at + 1]
            rate_row = rate_rows[at : at + 1, :]
            end = cum_row[:, BLOCK - 1 :]
            w = mm(solve[c, h] * (rate_row * jnp.exp(cum_row) * unit_rows[c, g]), keys[c, g])
            u = mm(solve[c, h] * rate_row, value_ref[tokens, h * DV : (h + 1) * DV])
            wu = jnp.concatenate([w, u], axis=1)
            wu_ref[h, c] = wu.astype(BF16)
            tails[c, h] = mm(keys_t[c, g], wu * (jnp.exp(end - cum_col) * unit_cols[c, g]))
        for c, h in some:
            at = c * heads + h
            kept = jnp.exp(cum_rows[at : at + 1, BLOCK - 1 :])
            tail = tails[c, h]
            if c == 0:
                start = jnp.concatenate([eye, jnp.zeros((DK, DV), F32)], axis=1)
                prefix_ref[h, c] = start.astype(BF16)
                carried[h] = jnp.concatenate([kept * eye - tail[:, :DK], tail[:, DK:]], axis=1)
            else:
                bias = jnp.concatenate([jnp.zeros((DK, DK), F32), tail[:, DK:]], axis=1)
                prefix_ref[h, c] = carried[h].astype(BF16)
                carried[h] = kept * carried[h] + bias - mm_both2(tail[:, :DK], carried[h])
    for h in range(heads):
        total_ref[h] = carried[h].astype(BF16)


def readout_kernel(query_ref, key_ref, decay_ref, ids_ref, weight_ref, wu_ref, prefix_ref,
                   lin_ref, own_ref, routes_ref):
    expert = lax.broadcasted_iota(jnp.int32, (LANES, ids_ref.shape[1]), 0)
    routes = jnp.zeros(expert.shape, F32)
    for k in range(ids_ref.shape[0]):
        routes += jnp.where(
            ids_ref[k : k + 1, :] == expert, weight_ref[k : k + 1, :].astype(F32), 0.0
        )
    routes_ref[...] = routes.T.astype(BF16)
    heads = decay_ref.shape[0]
    key_heads = key_ref.shape[1] // DK
    group = heads // key_heads
    blocks = key_ref.shape[0] // BLOCK
    row, col = grids()
    causal = row >= col
    diagonal = row == col
    cum_rows, cum_cols = decays(decay_ref, blocks, row, col)
    for c in range(blocks):
        tokens = slice(c * BLOCK, (c + 1) * BLOCK)
        for g in range(key_heads):
            key = key_ref[tokens, g * DK : (g + 1) * DK]
            query = query_ref[tokens, g * DK : (g + 1) * DK]
            key_f, query_f = key.astype(F32), query.astype(F32)
            gram = jnp.where(diagonal, mm_nt(key, key), 0.0)
            unit_row = lax.rsqrt(jnp.sum(gram, axis=0, keepdims=True) + EPS)
            query_unit = query_f * (
                lax.rsqrt(jnp.sum(query_f * query_f, axis=1, keepdims=True) + EPS) * DK ** (-0.5)
            )
            query_scale = lax.rsqrt(
                jnp.sum(query_f * query_f, axis=1, keepdims=True) + EPS
            ) * DK ** (-0.5)
            plain = mm_nt(query, key) * unit_row * query_scale
            for h in range(g * group, (g + 1) * group):
                at = c * heads + h
                cum_row, cum_col = cum_rows[at : at + 1, :], cum_cols[:, at : at + 1]
                fade = jnp.exp(jnp.where(causal, cum_col - cum_row, 0.0))
                scores = jnp.where(causal, plain * fade, 0.0)
                mixed_wu = mm(scores, wu_ref[h, c])
                reach = query_unit * jnp.exp(cum_col) - mixed_wu[:, :DK]
                lanes = slice(h * DV, (h + 1) * DV)
                if c == 0:
                    lin_ref[tokens, lanes] = reach.astype(BF16)
                    own_ref[tokens, lanes] = mixed_wu[:, DK:]
                else:
                    spread = mm(reach, prefix_ref[h, c])
                    lin_ref[tokens, lanes] = spread[:, :DK].astype(BF16)
                    own_ref[tokens, lanes] = mixed_wu[:, DK:] + spread[:, DK:]


def with_map(bias):
    return jnp.concatenate([jnp.zeros((DK, DK), F32), bias.astype(F32)], axis=1)


def scan_kernel(last, later_ref, own_ref, got_ref, before_ref, total_ref, prefix_ref):
    later = later_ref[0] == 1
    for h in range(own_ref.shape[0]):
        own, got, before = own_ref[h], got_ref[h], before_ref[h]
        first = jnp.where(later, got, own)
        second = jnp.where(later, own, got)
        if last:
            total = mm(second[:, :DK], first[:, DK:]) + second[:, DK:].astype(F32)
        else:
            total = mm(second[:, :DK], first) + with_map(second[:, DK:])
        total_ref[h] = total.astype(BF16)
        joined = mm(before[:, :DK], got) + with_map(before[:, DK:])
        prefix_ref[h] = jnp.where(later, joined.astype(BF16), before)


def mixed_rows(tokens, states, gain_ref, gate_ref, lin_ref, own_ref):
    parts = []
    for h, state in enumerate(states):
        lanes = slice(h * DV, (h + 1) * DV)
        readout = own_ref[tokens, lanes] + mm(lin_ref[tokens, lanes], state)
        scale = lax.rsqrt(jnp.mean(readout * readout, axis=1, keepdims=True) + EPS)
        gate = gate_ref[tokens, lanes].astype(F32)
        gated = gain_ref[...] * gate / (1.0 + jnp.exp(-gate))
        parts.append((readout * scale * gated).astype(BF16))
    return jnp.concatenate(parts, axis=1)


def rows_of(place, side, d, rows):
    at = 2 * jnp.bitwise_xor(place, d) + side
    return pl.ds(pl.multiple_of(at * rows, rows), rows)


def send_kernel(spot_ref, gain_ref, gate_ref, lin_ref, own_ref, prefix_ref, got_ref, state_ref, send_ref):
    core, place, later = spot_ref[0], spot_ref[1], spot_ref[2] == 1
    places, rows, _ = send_ref.shape
    states = []
    for h in range(prefix_ref.shape[0]):
        prefix = prefix_ref[h]
        bias = prefix[:, DK:].astype(F32)
        joined = mm(prefix[:, :DK], got_ref[h]) + bias
        states.append(jnp.where(later, joined, bias).astype(BF16))
        state_ref[h] = states[h]
    for d in range(places):
        tokens = rows_of(place, 1 - core, d, rows)
        send_ref[d] = mixed_rows(tokens, states, gain_ref, gate_ref, lin_ref, own_ref)


def keep_kernel(spot_ref, gain_ref, gate_ref, lin_ref, own_ref, state_ref, keep_ref):
    core, place = spot_ref[0], spot_ref[1]
    states = [state_ref[h] for h in range(state_ref.shape[0])]
    places, rows, _ = keep_ref.shape
    for d in range(places):
        tokens = rows_of(place, core, d, rows)
        keep_ref[d] = mixed_rows(tokens, states, gain_ref, gate_ref, lin_ref, own_ref)


def project_kernel(start, keep_ref, got_ref, own_ref, sib_ref, *out_refs):
    places, rows, depth = keep_ref.shape
    part, width = out_refs[0].shape
    keep, got = (
        jnp.concatenate([ref[d, start : start + part] for d in range(places)], axis=0)
        for ref in (keep_ref, got_ref)
    )
    tile = 512
    for lead in range(0, width, tile):
        lanes = slice(lead, lead + tile)
        product = jnp.dot(keep, own_ref[:, lanes], preferred_element_type=F32) + jnp.dot(
            got, sib_ref[:, lanes], preferred_element_type=F32
        )
        for d, out_ref in enumerate(out_refs):
            out_ref[:, lanes] = product[d * part : (d + 1) * part].astype(BF16)


def project(keep, got, own, sib, sizes):
    places = keep.shape[0]
    chunks = []
    for number, size in enumerate(sizes):
        chunks.append(
            resident(
                functools.partial(project_kernel, sum(sizes[:number])),
                (shape((size, own.shape[1]), BF16),) * places,
                keep,
                after(got, chunks[-1][0]) if chunks else got,
                own,
                sib,
                flops=5 * 10**8,
            )
        )
    return chunks


def norm_kernel(start, hidden_ref, gain_ref, routes_ref, *refs):
    *part_refs, residual_ref, out_ref = refs
    rows = residual_ref.shape[0]
    tokens = slice(start, start + rows)
    residual = hidden_ref[tokens, :].astype(F32)
    for part_ref in part_refs:
        residual += part_ref[:, : residual.shape[1]].astype(F32)
    residual_ref[...] = residual
    scale = lax.rsqrt(jnp.mean(residual * residual, axis=1, keepdims=True) + EPS)
    width = residual.shape[1]
    out_ref[:, :width] = (residual * scale * gain_ref[...]).astype(BF16)
    out_ref[:, width:] = routes_ref[tokens, :]


def finish_kernel(*refs):
    *in_refs, out_ref = refs
    chunks = sum(ref.dtype == F32 for ref in in_refs)
    each = len(in_refs) // chunks - 1
    start = 0
    for number, kept_ref in enumerate(in_refs[:chunks]):
        total = kept_ref[...]
        for ref in in_refs[chunks + number * each : chunks + (number + 1) * each]:
            total += ref[...].astype(F32)
        out_ref[start : start + total.shape[0], :] = total.astype(BF16)
        start += total.shape[0]


def expert_kernel(places, spot_ref, *refs):
    slots = refs[:places]
    weights = refs[places : places + 6]
    out_refs = refs[places + 6 :]
    place, core = spot_ref[0], spot_ref[1]
    rows, width = out_refs[0].shape
    x = jnp.concatenate([slot[:, :width] for slot in slots], axis=0)
    routes = jnp.concatenate([slot[:, width:] for slot in slots], axis=0).astype(F32)
    lane = lax.broadcasted_iota(jnp.int32, routes.shape, 1)
    inners, shares = [], []
    for number in range(2):
        gate_ref, up_ref = weights[3 * number : 3 * number + 2]
        expert = 2 * place + (core if number == 0 else 1 - core)
        gate_act = jnp.dot(x, gate_ref[0], preferred_element_type=F32)
        up_act = jnp.dot(x, up_ref[0], preferred_element_type=F32)
        inners.append((gate_act / (1.0 + jnp.exp(-gate_act)) * up_act).astype(BF16))
        shares.append(jnp.sum(jnp.where(lane == expert, routes, 0.0), axis=1, keepdims=True))
    tile = 512
    for lead in range(0, width, tile):
        lanes = slice(lead, lead + tile)
        total = jnp.dot(inners[0], weights[2][0, :, lanes], preferred_element_type=F32) * shares[0]
        total += jnp.dot(inners[1], weights[5][0, :, lanes], preferred_element_type=F32) * shares[1]
        for d, out_ref in enumerate(out_refs):
            out_ref[:, lanes] = total[d * rows : (d + 1) * rows].astype(BF16)


def experts(spot, slots, weights):
    rows = slots[0].shape[0]
    width = weights[0].shape[1]
    return resident(
        functools.partial(expert_kernel, len(slots)),
        (shape((rows, width), BF16),) * len(slots),
        *slots,
        *weights,
        scalars=spot,
        flops=3 * 10**9,
    )


def between_places(places, d):
    return [(2 * i + c, 2 * (i ^ d) + c) for i in range(places) for c in range(2)]


def exchange(piece, d):
    return lax.ppermute(piece, "exp", between_places(lax.axis_size("exp") // 2, d))


def reduce_places(chunks, spare=0):
    places = len(chunks[0])
    crossed = [[exchange(pieces[e ^ 1], 1) for e in range(2, places, 2)] for pieces in chunks]
    joined = []
    done = None
    for pieces, cross in zip(chunks, crossed):
        joined.append([])
        for e, got in zip(range(2, places, 2), cross):
            if done is not None:
                got = after(got, done)
            done = (pieces[e].astype(F32) + got.astype(F32)).astype(BF16)
            if len(joined) > 1:
                done = jnp.pad(done, ((0, 0), (0, spare)))
            joined[-1].append(done)
    return [
        [after(pieces[0], done)]
        + [exchange(sent, 2 * i + 2) for i, sent in enumerate(mine)]
        + [exchange(after(pieces[1], joined[0][-1] if spare else mine[-1]), 1)]
        for pieces, mine in zip(chunks, joined)
    ], done


def per_device(
    hidden_in,
    query_proj,
    key_proj,
    value_proj,
    gate_proj,
    log_decay,
    write_rate,
    head_gain,
    out_weight,
    post_gain,
    expert_ids,
    route_weight,
    gate_weight,
    up_weight,
    down_weight,
):
    length = value_proj.shape[0]
    heads = value_proj.shape[1] // DV
    blocks = length // BLOCK
    tok, width = hidden_in.shape
    seqs, exps = lax.axis_size("seq"), lax.axis_size("exp")
    places = exps // 2
    me = lax.axis_index("exp")
    place, core = lax.div(me, 2), lax.rem(me, 2)
    here = lax.axis_index("seq")
    swap = [(i, i ^ 1) for i in range(exps)]

    out_sib = lax.ppermute(out_weight, "exp", swap)
    own = (gate_weight, up_weight, down_weight)
    sib = tuple(lax.ppermute(w, "exp", swap) for w in own)

    wide = shape((heads, blocks, DK, DK + DV), BF16)
    wu, prefixes, total = call(
        state_kernel,
        (wide, wide, shape((heads, DK, DK + DV), BF16)),
        key_proj,
        value_proj,
        log_decay,
        write_rate,
        flops=10**10,
    )
    total, out_sib = lax.optimization_barrier((total, out_sib))
    lin, own_read, routes = call(
        readout_kernel,
        (
            shape((length, heads * DV), BF16),
            shape((length, heads * DV), F32),
            shape((tok, LANES), BF16),
        ),
        query_proj,
        key_proj,
        log_decay,
        expert_ids.T,
        route_weight.T,
        wu,
        prefixes,
        flops=4 * 10**9,
        vmem=SMALL_VMEM,
        stay=True,
    )

    start = jnp.concatenate([jnp.eye(DK, dtype=BF16), jnp.zeros((DK, DV), BF16)], axis=1)
    before = jnp.broadcast_to(start, total.shape)
    summed, step = total, 1
    while True:
        later = lax.rem(lax.div(here, step), 2)
        got = lax.ppermute(summed, "seq", [(i, i ^ step) for i in range(seqs)])
        if 2 * step >= seqs:
            break
        last = 4 * step >= seqs
        summed, before = resident(
            functools.partial(scan_kernel, last),
            (shape((heads, DK, DV if last else DK + DV), BF16), shape(total.shape, BF16)),
            summed,
            after(got, lin) if step == 1 else got,
            before,
            scalars=later.reshape(1),
        )
        step *= 2
    fetched = fetch(gate_proj, out_weight, out_sib)
    got, before, fetched, sib = lax.optimization_barrier((got, before, fetched, sib))
    gate_here, out_own, out_sib = fetched

    half = shape((places, tok, heads * DV), BF16)
    where = jnp.stack([core, place, later])
    readout_parts = (head_gain.reshape(1, DV), gate_here, lin, own_read)
    state, send = resident(
        send_kernel,
        (shape((heads, DK, DV), BF16), half),
        *readout_parts,
        before,
        got,
        scalars=where,
        flops=10**9,
    )
    got = lax.ppermute(send, "exp", swap)
    (keep,) = resident(
        keep_kernel,
        (half,),
        *readout_parts,
        state,
        scalars=where,
        flops=10**9,
    )
    spot = jnp.stack([place, core])
    sizes = SIZES if sum(SIZES) == tok else (tok // 2, tok // 2)
    starts = [sum(sizes[:i]) for i in range(len(sizes))]
    chunks, joined = reduce_places(project(keep, got, out_own, out_sib, sizes), SPARE)
    sib = fetch(*(after(w, joined) for w in sib))
    chunks[0][0] = after(chunks[0][0], *sib)
    residuals, slots = [], []
    for chunk, summands in enumerate(chunks):
        if slots:
            summands[0] = after(summands[0], *slots[-1][1:3])
        kept, sent = resident(
            functools.partial(norm_kernel, starts[chunk]),
            (shape((sizes[chunk], width), F32), shape((sizes[chunk], width + LANES), BF16)),
            hidden_in,
            post_gain.reshape(1, width),
            routes,
            *summands,
        )
        residuals.append(kept)
        slot = [sent] + [None] * (places - 1)
        for e in range(2, places, 2):
            slot[e] = exchange(sent, e)
        slot[1] = exchange(sent, 1)
        slots.append(slot)
    for slot in slots:
        for e in range(2, places, 2):
            slot[e + 1] = exchange(after(slot[e], slots[-1][0]), 1)
    made = []
    for slot in slots:
        if made:
            slot[0] = after(slot[0], made[-1][0])
        made.append(experts(spot, slot, (*own, *sib)))
    chunks, _ = reduce_places(made)
    return call(
        finish_kernel,
        (shape((tok, width), BF16),),
        *residuals,
        *(summand for summands in chunks for summand in summands),
        vmem=SMALL_VMEM,
    )[0]


def solution(mesh):
    in_specs = (
        P(("seq", "exp"), None),
        P("seq", "exp"),
        P("seq", "exp"),
        P("seq", "exp"),
        P("seq", "exp"),
        P("exp", "seq"),
        P("exp", "seq"),
        P(),
        P("exp", None),
        P(),
        P(("seq", "exp"), None),
        P(("seq", "exp"), None),
        P("exp", None, None),
        P("exp", None, None),
        P("exp", None, None),
    )
    out_specs = P(("seq", "exp"), None)
    return jax.shard_map(
        per_device, mesh=mesh, in_specs=in_specs, out_specs=out_specs, check_vma=False
    )
```
